256 devices in a mesh: member: 8 (over y, x_lo), lon: 32 (over x_hi, z, core).
Axes of the slice: x: 4 (x_hi: 2, x_lo: 2; x = x_hi * 2 + x_lo), y: 4, z: 8, core: 2. Of those that a mesh axis runs over, the one named last changes fastest.
Arguments:
- fields: bfloat16 [8, 641, 20, 1440], P('member', None, None, 'lon'), may hold values from -6 to 6
- weight: bfloat16 [5, 5, 73, 641], replicated, may hold values from -0.046875 to 0.046875
- out_bias: float32 [73], replicated, may hold values from -3 to 3
- observed: float32 [73, 16, 1440], P(None, None, 'lon'), may hold values from -6 to 6
- widths: float32 [73], replicated, may hold values from 0.5 to 2
- owner_start: int32 [32, 9], P('lon'), may hold values from 0 to 16, as said below
Outputs:
- out_grad: bfloat16 [8, 73, 16, 1440], P('member', None, None, 'lon')
- owned_score: float32 [32, 8, 270], P('lon', 'member')
- weight_grad: float32 [5, 5, 73, 641], replicated
- bias_grad: float32 [73], replicated
The draws below stay inside these ranges and needn't reach their ends.
Inputs may be any that keep to these rules, and one draw needn't show every extreme that they name: Each row owner_start[l] starts at 0, never falls and ends at 16; owner r of longitude group l holds blocks owner_start[l, r] to owner_start[l, r + 1] - 1, at most 6 of them, and in every group some owner holds exactly 6.
All inputs are finite; a program needn't handle non-finite values.
Results may differ from the reference program's by a relative error of at most 0.0063.
Values may be sent and summed in bfloat16 or wider, within the bound.
A program may use at most 128 MiB of HBM per device.

```python
import math
import jax
import jax.numpy as jnp
from jax import lax

CIN = 641
COUT = 73
LAT = 16
LON_DEV = 45
BLOCK = 45
MEMBERS = 8
LON = 1440
PB = 16
CAP = 6
N_MEMBER = 8
N_LON = 32


def draw_owner_start(key, part):

    def one_group(group_key):
        first_key = jax.random.fold_in(group_key, 11)
        second_key = jax.random.fold_in(group_key, 23)
        busiest = jax.random.randint(first_key, (), 0, N_MEMBER)
        counts = jnp.where(jnp.arange(N_MEMBER) == busiest, CAP, 0).astype(jnp.int32)

        def place_block(index, current):
            ranks = jax.random.randint(jax.random.fold_in(second_key, index), (N_MEMBER,), 0, 1 << 20)
            ranks = ranks * N_MEMBER + jnp.arange(N_MEMBER, dtype=jnp.int32)
            ranks = jnp.where(current < CAP, ranks, -1)
            winner = jnp.argmax(ranks)
            return current + (jnp.arange(N_MEMBER) == winner).astype(jnp.int32)
        counts = lax.fori_loop(0, PB - CAP, place_block, counts)
        return jnp.concatenate([jnp.zeros((1,), jnp.int32), jnp.cumsum(counts).astype(jnp.int32)])
    group_keys = jax.random.split(jax.random.fold_in(key, 7), N_LON)
    return jax.vmap(one_group)(group_keys).astype(jnp.int32)


def steps_of(own_key, extent, shards, low, high):
    def one(position, shards_of):
        heights = jax.random.uniform(jax.random.fold_in(jax.random.fold_in(own_key, 6), position), (shards_of,), jnp.float32, low / len(shards), high / len(shards))
        return jnp.repeat(jnp.exp(heights), extent[position] // shards_of).reshape((-1,) + (1,) * (len(extent) - position - 1))

    factor_of = one(*shards[0])
    for cut in shards[1:]:
        factor_of = factor_of * one(*cut)
    return factor_of


def gaussian(key, extent, deviation, most, cuts=(), kind=jnp.bfloat16):
    array = jax.random.normal(key, extent, jnp.float32) * deviation
    if len(cuts) > 0:
        array = steps_of(key, extent, cuts, -0.22, 0.18) * array
    return jnp.clip(array, min=-most, max=most).astype(kind)


def setup_inputs(seed: int = 0) -> dict:
    arg_keys = jax.random.split(jax.random.key(seed), 7)
    fields = gaussian(arg_keys[0], (MEMBERS, CIN, LAT + 4, LON), 1.0, 6.0, ((0, 8), (3, 32)))
    weight = gaussian(arg_keys[1], (5, 5, COUT, CIN), (25 * CIN) ** -0.5, 0.046875)
    out_bias = gaussian(arg_keys[2], (COUT,), 0.5, 3.0, (), jnp.float32)
    observed = gaussian(arg_keys[3], (COUT, LAT, LON), 1.0, 6.0, ((2, 32),), jnp.float32)
    widths = jnp.clip(jnp.exp(jax.random.uniform(arg_keys[4], (COUT,), jnp.float32, math.log(0.5), math.log(2.0))), 0.5, 2.0)
    owner_start = draw_owner_start(jax.random.fold_in(arg_keys[6], 71), 0)
    return {"fields": fields, "weight": weight, "out_bias": out_bias, "observed": observed, "widths": widths, "owner_start": owner_start}


def kernel_terms(values, target, widths):
    members = values.astype(jnp.float32)
    ensemble = members.shape[0]
    inverse = (1.0 / (widths * widths))[:, None]
    spread = members[:, None] - members[None, :]
    kernel_pair = jnp.exp(-0.5 * spread * spread * inverse)
    misfit = members - target[None]
    kernel_obs = jnp.exp(-0.5 * misfit * misfit * inverse)
    per_channel = lax.optimization_barrier(jnp.sum(kernel_pair, axis=(0, 1))) / (2.0 * ensemble * ensemble) - lax.optimization_barrier(jnp.sum(kernel_obs, axis=0)) / ensemble
    scores = lax.optimization_barrier(jnp.mean(per_channel, axis=0))
    gradient = inverse * (misfit * kernel_obs - lax.optimization_barrier(jnp.sum(kernel_pair * spread, axis=1)) / ensemble)
    return (scores, gradient.astype(jnp.bfloat16))

def wrap_lon(member_field):
    return jnp.concatenate([member_field[..., -2:], member_field, member_field[..., :2]], axis=-1)

def tap_stack(gradients, rows_in, padded_width):
    leading = gradients.ndim - 2
    padded = jnp.pad(gradients, [(0, 0)] * leading + [(4, 4), (4, 4)])
    pieces = [padded[..., 4 - row_tap:4 - row_tap + rows_in, 4 - col_tap:4 - col_tap + padded_width] for row_tap in range(5) for col_tap in range(5)]
    return jnp.stack(pieces, axis=-4)

def reference(fields, weight, out_bias, observed, widths, owner_start):
    flat_weight = weight.reshape(25 * COUT, CIN)
    rows_in = LAT + 4
    padded_width = LON + 4

    def forward(member_field):
        padded = wrap_lon(member_field).reshape(CIN, rows_in * padded_width)
        tap_sums = jnp.dot(flat_weight, padded, preferred_element_type=jnp.float32).reshape(5, 5, COUT, rows_in, padded_width)
        convolved = jnp.broadcast_to(out_bias[:, None, None], (COUT, LAT, LON))
        for row_tap in range(5):
            for col_tap in range(5):
                convolved = convolved + tap_sums[row_tap, col_tap, :, row_tap:row_tap + LAT, col_tap:col_tap + LON]
        return convolved.astype(jnp.bfloat16)
    outputs = lax.map(forward, fields)
    by_channel = jnp.transpose(outputs.reshape(MEMBERS, COUT, LAT * LON), (1, 0, 2))
    truth_flat = observed.reshape(COUT, LAT * LON)

    def channel_terms(packed):
        values, target, spread_width = packed
        return kernel_terms(values[:, None, :], target[None, :], spread_width[None])
    scores, gradients = lax.map(channel_terms, (by_channel, truth_flat, widths))
    point_score = lax.optimization_barrier(jnp.mean(scores, axis=0))
    out_grad = jnp.transpose(gradients[:, :, 0, :], (1, 0, 2)).reshape(MEMBERS, COUT, LAT, LON)
    blocked = jnp.transpose(point_score.reshape(LAT, N_LON, LON_DEV), (1, 0, 2)).reshape(N_LON, PB, BLOCK)
    slot_index = jnp.arange(CAP, dtype=jnp.int32)
    starts = owner_start[:, :-1]
    owned_blocks = owner_start[:, 1:] - starts
    filled = slot_index[None, None, :] < owned_blocks[:, :, None]
    chosen = jnp.where(filled, starts[:, :, None] + slot_index[None, None, :], 0).reshape(N_LON, N_MEMBER * CAP).astype(jnp.int32)
    picked = jnp.take_along_axis(blocked, chosen[:, :, None], axis=1).reshape(N_LON, N_MEMBER, CAP, BLOCK)
    owned_score = jnp.where(filled[..., None], picked, 0.0).reshape(N_LON, N_MEMBER, CAP * BLOCK)

    def accumulate(running, packed):
        member_field, member_grad = packed
        padded = wrap_lon(member_field).reshape(CIN, rows_in * padded_width)
        stacked = tap_stack(member_grad, rows_in, padded_width).reshape(25 * COUT, rows_in * padded_width)
        weight_part = lax.dot_general(stacked, padded, (((1,), (1,)), ((), ())), preferred_element_type=jnp.float32)
        bias_part = lax.optimization_barrier(jnp.sum(member_grad.astype(jnp.float32), axis=(1, 2)))
        return ((running[0] + weight_part, running[1] + bias_part), None)
    start_sums = (jnp.zeros((25 * COUT, CIN), jnp.float32), jnp.zeros((COUT,), jnp.float32))
    (weight_sum, bias_sum), _ = lax.scan(accumulate, start_sums, (fields, out_grad))
    factor = 1.0 / math.sqrt(MEMBERS * LAT * LON)
    return (out_grad, owned_score, (weight_sum * factor).reshape(5, 5, COUT, CIN), bias_sum * factor)
```

```python
import math

import jax
import jax.numpy as jnp
from jax import lax
from jax.experimental import pallas as pl
from jax.sharding import PartitionSpec as P
from jax.experimental.pallas import tpu as pltpu

MESH = pl.DeviceIdType.MESH
ROWS = 2048
LANES = 128
PARTS = 3
COLS = 2 * PARTS * LANES
ORDERS = (("x", "y", "z"), ("y", "x", "z"), ("z", "x", "y"))


def position():
    member = lax.axis_index("member")
    lon = lax.axis_index("lon")
    return {
        "x": (lon // 16) * 2 + member % 2,
        "y": member // 2,
        "z": (lon // 2) % 8,
        "core": lon % 2,
    }


EXTENT = {"x": 4, "y": 4, "z": 8, "core": 2}


def device(at):
    return (at["y"] * 2 + at["x"] % 2, (at["x"] // 2) * 16 + at["z"] * 2 + at["core"])


def moved(at, axis, delta):
    there = dict(at)
    there[axis] = lax.rem(at[axis] + delta, EXTENT[axis])
    return there


def send(src, dst, send_sem, recv_sem, at):
    copy = pltpu.make_async_remote_copy(
        src_ref=src, dst_ref=dst, send_sem=send_sem, recv_sem=recv_sem,
        device_id=device(at), device_id_type=MESH,
    )
    copy.start()


def finish(ref, send_sem, recv_sem, at):
    copy = pltpu.make_async_remote_copy(
        src_ref=ref, dst_ref=ref, send_sem=send_sem, recv_sem=recv_sem,
        device_id=device(at), device_id_type=MESH,
    )
    return copy


def greet(at, axes):
    barrier = pltpu.get_barrier_semaphore()
    count = 0
    for axis in axes:
        for delta in range(1, EXTENT[axis]):
            pl.semaphore_signal(
                barrier, inc=1, device_id=device(moved(at, axis, delta)), device_id_type=MESH
            )
            count += 1
    pl.semaphore_wait(barrier, count)


def stage_rows(order):
    rows, sizes = ROWS, []
    for axis in order:
        rows //= EXTENT[axis]
        sizes.append(rows)
    return sizes


def all_reduce(at, dw, out, core_rx, cur, rxs, send_sems, recv_sems):
    core = at["core"]
    partner = moved(at, "core", 1)
    for k in range(PARTS):
        send(dw.at[1 - core, k], core_rx.at[k], send_sems.at[k, 0], recv_sems.at[k, 0], partner)
    row = [0] * PARTS
    sizes = [stage_rows(order) for order in ORDERS]

    def launch(k, s):
        axis, rows = ORDERS[k][s], sizes[k][s]
        for delta in range(1, EXTENT[axis]):
            there = moved(at, axis, delta)
            source = cur[k][s].at[pl.ds(pl.multiple_of(there[axis] * rows, 16), rows)]
            send(source, rxs[k][s].at[delta - 1], send_sems.at[k, s + 1], recv_sems.at[k, s + 1], there)

    for k in range(PARTS):
        finish(core_rx.at[k], send_sems.at[k, 0], recv_sems.at[k, 0], partner).wait_recv()
        step = 256

        def add(i, _, k=k):
            here = pl.ds(pl.multiple_of(i * step, step), step)
            total = dw[core, k, here, :].astype(jnp.float32) + core_rx[k, here, :].astype(jnp.float32)
            cur[k][0][here, :] = total.astype(jnp.bfloat16)
            return 0

        lax.fori_loop(0, ROWS // step, add, 0)
        launch(k, 0)
    for s in range(3):
        for k in range(PARTS):
            axis, rows = ORDERS[k][s], sizes[k][s]
            finish(rxs[k][s], send_sems.at[k, s + 1], recv_sems.at[k, s + 1], partner).wait_recv()
            row[k] = row[k] + at[axis] * rows
            base = pl.multiple_of(at[axis] * rows, 16)
            step = min(rows, 128)
            lane = pl.ds(pl.multiple_of(core * (PARTS * LANES) + k * LANES, LANES), LANES)

            def add(i, _, k=k, s=s, axis=axis, base=base, step=step, lane=lane):
                total = cur[k][s][pl.ds(pl.multiple_of(base + i * step, 16), step), :].astype(jnp.float32)
                here = pl.ds(pl.multiple_of(i * step, 16), step)
                for slot in range(EXTENT[axis] - 1):
                    total = total + rxs[k][s][slot, here, :].astype(jnp.float32)
                if s < 2:
                    cur[k][s + 1][here, :] = total.astype(jnp.bfloat16)
                else:
                    out[pl.ds(pl.multiple_of(row[k], 16), step), lane] = total.astype(jnp.bfloat16)
                return 0

            if rows == step:
                add(0, 0)
            else:
                lax.fori_loop(0, rows // step, add, 0)
            if s < 2:
                launch(k, s + 1)
            else:
                gather(at, out, k, 2, row, sizes, send_sems, recv_sems)
    for s in (2, 1, 0):
        for k in range(PARTS):
            axis, rows = ORDERS[k][s], sizes[k][s]
            whole = rxs[k][s]
            finish(whole, send_sems.at[k, 4 + s], recv_sems.at[k, 4 + s], partner).wait_recv()
            row[k] = row[k] - at[axis] * rows
            if s > 0:
                gather(at, out, k, s - 1, row, sizes, send_sems, recv_sems)
            else:
                lane = pl.ds(pl.multiple_of(core * (PARTS * LANES) + k * LANES, LANES), LANES)
                send(out.at[:, lane], out.at[:, lane], send_sems.at[k, 7], recv_sems.at[k, 7], partner)
    for k in range(PARTS):
        finish(core_rx.at[k], send_sems.at[k, 7], recv_sems.at[k, 7], partner).wait_recv()
    for k in range(PARTS):
        finish(core_rx.at[k], send_sems.at[k, 0], recv_sems.at[k, 0], partner).wait_send()
        finish(core_rx.at[k], send_sems.at[k, 7], recv_sems.at[k, 7], partner).wait_send()
        for s in range(3):
            finish(rxs[k][s], send_sems.at[k, s + 1], recv_sems.at[k, s + 1], partner).wait_send()
            finish(rxs[k][s], send_sems.at[k, s + 4], recv_sems.at[k, s + 4], partner).wait_send()


def gather(at, out, k, s, row, sizes, send_sems, recv_sems):
    axis, rows = ORDERS[k][s], sizes[k][s]
    lane = pl.ds(pl.multiple_of(at["core"] * (PARTS * LANES) + k * LANES, LANES), LANES)
    block = out.at[pl.ds(pl.multiple_of(row[k], 16), rows), lane]
    for delta in range(1, EXTENT[axis]):
        send(block, block, send_sems.at[k, 4 + s], recv_sems.at[k, 4 + s], moved(at, axis, delta))


def reduce_scratch():
    shapes = [pltpu.VMEM((PARTS, ROWS, LANES), jnp.bfloat16)]
    for order in ORDERS:
        rows = ROWS
        for size in stage_rows(order):
            shapes.append(pltpu.VMEM((rows, LANES), jnp.bfloat16))
            rows = size
    for order in ORDERS:
        for axis, size in zip(order, stage_rows(order)):
            shapes.append(pltpu.VMEM((EXTENT[axis] - 1, size, LANES), jnp.bfloat16))
    shapes += [pltpu.SemaphoreType.DMA((PARTS, 8)), pltpu.SemaphoreType.DMA((PARTS, 8))]
    return shapes


def reduce_kernel(dw, out, *scratch):
    core_rx, rest = scratch[0], scratch[1:]
    cur = [rest[3 * k : 3 * k + 3] for k in range(PARTS)]
    rxs = [rest[9 + 3 * k : 12 + 3 * k] for k in range(PARTS)]
    send_sems, recv_sems = rest[18], rest[19]
    at = position()
    greet(at, ("core", "x", "y", "z"))
    all_reduce(at, dw, out, core_rx, cur, rxs, send_sems, recv_sems)


def reduced(dw):
    return pl.pallas_call(
        reduce_kernel,
        out_shape=jax.ShapeDtypeStruct((ROWS, COLS), jnp.bfloat16),
        in_specs=[pl.BlockSpec(memory_space=pltpu.VMEM)],
        out_specs=pl.BlockSpec(memory_space=pltpu.VMEM),
        scratch_shapes=reduce_scratch(),
        compiler_params=pltpu.CompilerParams(
            collective_id=1, has_side_effects=True, vmem_limit_bytes=48 * 1024 * 1024
        ),
        cost_estimate=pl.CostEstimate(flops=2048 * 768 * 4, bytes_accessed=8 << 20, transcendentals=0),
    )(dw)

BLOCK = 45


def extended(block, sides, width):
    for axis, dim in sides:
        count = lax.axis_size(axis)
        forward = [(i, i + 1) for i in range(count - 1)]
        forward.append((count - 1, 0))
        backward = [(target, source) for source, target in forward]
        low = lax.ppermute(
            lax.slice_in_dim(block, block.shape[dim] - width, None, axis=dim), axis, forward
        )
        high = lax.ppermute(lax.slice_in_dim(block, 0, width, axis=dim), axis, backward)
        block = jnp.concatenate([low, block, high], axis=dim)
    return block


def kernel_terms(values, target, widths):
    members = values.astype(jnp.float32)
    ensemble = members.shape[0]
    inverse = (1.0 / (widths * widths))[:, None]
    spread = members[:, None] - members[None, :]
    kernel_pair = jnp.exp(-0.5 * spread * spread * inverse)
    misfit = members - target[None]
    kernel_obs = jnp.exp(-0.5 * misfit * misfit * inverse)
    per_channel = (
        jnp.sum(kernel_pair, axis=(0, 1)) / (2.0 * ensemble * ensemble)
        - jnp.sum(kernel_obs, axis=0) / ensemble
    )
    scores = jnp.mean(per_channel, axis=0)
    gradient = inverse * (misfit * kernel_obs - jnp.sum(kernel_pair * spread, axis=1) / ensemble)
    return (scores, gradient.astype(jnp.bfloat16))


def tap_stack(gradients, rows_in, padded_width):
    leading = gradients.ndim - 2
    padded = jnp.pad(gradients, [(0, 0)] * leading + [(4, 4), (4, 4)])
    pieces = [
        padded[..., 4 - row_tap : 4 - row_tap + rows_in, 4 - col_tap : 4 - col_tap + padded_width]
        for row_tap in range(5)
        for col_tap in range(5)
    ]
    return jnp.stack(pieces, axis=-4)


def body(fields, weight, out_bias, observed, widths, owner_start):
    local_members, in_chan, rows_in, lon_dev = fields.shape
    out_chan = weight.shape[2]
    rows_out = rows_in - 4
    padded_width = lon_dev + 4
    padded = extended(fields, (("lon", 3),), 2)
    flat_field = padded.reshape(local_members, in_chan, rows_in * padded_width)
    flat_weight = weight.reshape(25 * out_chan, in_chan)
    tap_sums = jnp.einsum(
        "kc,mcp->mkp", flat_weight, flat_field, preferred_element_type=jnp.float32
    )
    tap_sums = tap_sums.reshape(local_members, 5, 5, out_chan, rows_in, padded_width)
    convolved = jnp.broadcast_to(
        out_bias[None, :, None, None], (local_members, out_chan, rows_out, lon_dev)
    )
    for row_tap in range(5):
        for col_tap in range(5):
            convolved = (
                convolved
                + tap_sums[
                    :,
                    row_tap,
                    col_tap,
                    :,
                    row_tap : row_tap + rows_out,
                    col_tap : col_tap + lon_dev,
                ]
            )
    outputs = convolved.astype(jnp.bfloat16)
    owners = lax.axis_size("member")
    own_rank = lax.axis_index("member")
    blocks = rows_out * lon_dev // BLOCK
    capacity = max(2, 3 * blocks // owners)
    starts = owner_start[0]
    slot_index = jnp.arange(capacity, dtype=jnp.int32)
    owned_blocks = starts[1:] - starts[:-1]
    filled = slot_index[None, :] < owned_blocks[:, None]
    global_block = starts[:-1, None] + slot_index[None, :]
    even_blocks = blocks // owners
    sending = outputs.reshape(local_members, out_chan, owners, even_blocks * BLOCK)
    arrived = lax.all_to_all(sending, "member", split_axis=2, concat_axis=0, tiled=True).reshape(
        -1, out_chan, even_blocks * BLOCK
    )
    target = lax.dynamic_slice_in_dim(observed, own_rank * even_blocks, even_blocks, 1)
    target = target.reshape(out_chan, even_blocks * BLOCK)
    scores, gradients = kernel_terms(arrived, target, widths)
    local_grad = lax.all_to_all(
        gradients.reshape(-1, out_chan, 1, even_blocks * BLOCK),
        "member",
        split_axis=0,
        concat_axis=2,
        tiled=True,
    )
    from_self = filled & (global_block // even_blocks == own_rank)
    local_index = jnp.clip(global_block - own_rank * even_blocks, 0, even_blocks - 1)
    parcel = jnp.take(scores.reshape(even_blocks, BLOCK), local_index.reshape(-1), axis=0)
    parcel = jnp.where(from_self[..., None], parcel.reshape(owners, capacity, BLOCK), 0.0)
    gathered = lax.all_to_all(
        parcel.reshape(owners, capacity * BLOCK), "member", split_axis=0, concat_axis=0, tiled=True
    )
    owned_score = jnp.sum(gathered, axis=0).reshape(1, 1, capacity * BLOCK)
    out_grad = local_grad.reshape(local_members, out_chan, rows_out, lon_dev)
    stacked = tap_stack(out_grad, rows_in, padded_width).reshape(
        local_members, 25 * out_chan, rows_in * padded_width
    )
    weight_part = lax.dot_general(
        stacked, flat_field, (((0, 2), (0, 2)), ((), ())), preferred_element_type=jnp.float32
    )
    bias_part = jnp.sum(out_grad.astype(jnp.float32), axis=(0, 2, 3))
    terms = jnp.pad(
        weight_part.reshape(25, out_chan, in_chan), ((0, 0), (0, 80 - out_chan), (0, COLS - in_chan))
    )
    bias_column = jnp.pad(bias_part, (0, 80 - out_chan))
    terms = terms.at[:, :, in_chan].set(bias_column[None])
    terms = jnp.pad(terms.reshape(2000, COLS), ((0, ROWS - 2000), (0, 0))).astype(jnp.bfloat16)
    terms = jnp.transpose(terms.reshape(ROWS, 2, PARTS, LANES), (1, 2, 0, 3))
    summed = reduced(terms)[:2000].reshape(25, 80, COLS)
    factor = 1.0 / math.sqrt(local_members * owners * rows_out * lon_dev * lax.axis_size("lon"))
    weight_sum = summed[:, :out_chan, :in_chan].astype(jnp.float32)
    bias_sum = summed[12, :out_chan, in_chan].astype(jnp.float32)
    weight_grad = (weight_sum * factor).reshape(5, 5, out_chan, in_chan)
    bias_grad = bias_sum * factor
    return (out_grad, owned_score, weight_grad, bias_grad)


def solution(mesh):
    in_specs = (P("member", None, None, "lon"), P(), P(), P(None, None, "lon"), P(), P("lon", None))
    out_specs = (P("member", None, None, "lon"), P("lon", "member", None), P(), P())
    return jax.shard_map(body, mesh=mesh, in_specs=in_specs, out_specs=out_specs, check_vma=False)
```

```python
import math

import jax
import jax.numpy as jnp
import numpy as np
from jax import lax
from jax.experimental import pallas as pl
from jax.experimental.pallas import tpu as pltpu
from jax.sharding import PartitionSpec as P

MESH = pl.DeviceIdType.MESH
MEMBERS = 8
GROUPS = 32
TAPS = 5
CIN = 641
COUT = 73
CHAN = 80
LAT = 16
LON_DEV = 45
PITCH = 48
POINTS = LAT * PITCH
CHUNK = 2 * PITCH
CAP = 6
TAP_ROWS = TAPS * CHAN
NT = (((1,), (1,)), ((), ()))
ROWS = 2048
LANES = 128
PARTS = 3
COLS = 2 * PARTS * LANES
ORDERS = (("x", "y", "z"), ("y", "x", "z"), ("z", "x", "y"))


def position():
    member = lax.axis_index("member")
    lon = lax.axis_index("lon")
    return {
        "x": (lon // 16) * 2 + member % 2,
        "y": member // 2,
        "z": (lon // 2) % 8,
        "core": lon % 2,
    }


EXTENT = {"x": 4, "y": 4, "z": 8, "core": 2}


def device(at):
    return (at["y"] * 2 + at["x"] % 2, (at["x"] // 2) * 16 + at["z"] * 2 + at["core"])


def moved(at, axis, delta):
    there = dict(at)
    there[axis] = lax.rem(at[axis] + delta, EXTENT[axis])
    return there


def send(src, dst, send_sem, recv_sem, at):
    copy = pltpu.make_async_remote_copy(
        src_ref=src, dst_ref=dst, send_sem=send_sem, recv_sem=recv_sem,
        device_id=device(at), device_id_type=MESH,
    )
    copy.start()


def send_to(src, dst, send_sem, recv_sem, there):
    copy = pltpu.make_async_remote_copy(
        src_ref=src, dst_ref=dst, send_sem=send_sem, recv_sem=recv_sem,
        device_id=there, device_id_type=MESH,
    )
    copy.start()


def finish(ref, send_sem, recv_sem, at):
    copy = pltpu.make_async_remote_copy(
        src_ref=ref, dst_ref=ref, send_sem=send_sem, recv_sem=recv_sem,
        device_id=device(at), device_id_type=MESH,
    )
    return copy


def greet(at):
    barrier = pltpu.get_barrier_semaphore()
    count = 0
    for axis in ("core", "x", "y", "z"):
        for delta in range(1, EXTENT[axis]):
            pl.semaphore_signal(
                barrier, inc=1, device_id=device(moved(at, axis, delta)), device_id_type=MESH
            )
            count += 1
    member, lon = lax.axis_index("member"), lax.axis_index("lon")
    for delta in range(1, MEMBERS):
        there = (lax.rem(member + delta, MEMBERS), lon)
        pl.semaphore_signal(barrier, inc=1, device_id=there, device_id_type=MESH)
        count += 1
    for delta in (1, GROUPS - 1):
        there = (member, lax.rem(lon + delta, GROUPS))
        pl.semaphore_signal(barrier, inc=1, device_id=there, device_id_type=MESH)
        count += 1
    return barrier, count


def stage_rows(order):
    rows, sizes = ROWS, []
    for axis in order:
        rows //= EXTENT[axis]
        sizes.append(rows)
    return sizes


def send_halves(at, theirs, core_rx, send_sems, recv_sems):
    partner = moved(at, "core", 1)
    for k in range(PARTS):
        send(theirs.at[k], core_rx.at[k], send_sems.at[k, 0], recv_sems.at[k, 0], partner)


def all_reduce(at, mine, out, core_rx, cur, rxs, send_sems, recv_sems):
    core = at["core"]
    partner = moved(at, "core", 1)
    row = [0] * PARTS
    sizes = [stage_rows(order) for order in ORDERS]

    def launch(k, s):
        axis, rows = ORDERS[k][s], sizes[k][s]
        for delta in range(1, EXTENT[axis]):
            there = moved(at, axis, delta)
            source = cur[k][s].at[pl.ds(pl.multiple_of(there[axis] * rows, 16), rows)]
            send(source, rxs[k][s].at[delta - 1], send_sems.at[k, s + 1], recv_sems.at[k, s + 1], there)

    for k in range(PARTS):
        finish(core_rx.at[k], send_sems.at[k, 0], recv_sems.at[k, 0], partner).wait_recv()
        step = 256

        def add(i, _, k=k):
            here = pl.ds(pl.multiple_of(i * step, step), step)
            total = mine[k, here, :] + core_rx[k, here, :].astype(jnp.float32)
            cur[k][0][here, :] = total.astype(jnp.bfloat16)
            return 0

        lax.fori_loop(0, ROWS // step, add, 0)
        launch(k, 0)
    for s in range(3):
        for k in range(PARTS):
            axis, rows = ORDERS[k][s], sizes[k][s]
            finish(rxs[k][s], send_sems.at[k, s + 1], recv_sems.at[k, s + 1], partner).wait_recv()
            row[k] = row[k] + at[axis] * rows
            base = pl.multiple_of(at[axis] * rows, 16)
            step = min(rows, 128)
            lane = pl.ds(pl.multiple_of(core * (PARTS * LANES) + k * LANES, LANES), LANES)

            def add(i, _, k=k, s=s, axis=axis, base=base, step=step, lane=lane):
                total = cur[k][s][pl.ds(pl.multiple_of(base + i * step, 16), step), :].astype(jnp.float32)
                here = pl.ds(pl.multiple_of(i * step, 16), step)
                for slot in range(EXTENT[axis] - 1):
                    total = total + rxs[k][s][slot, here, :].astype(jnp.float32)
                if s < 2:
                    cur[k][s + 1][here, :] = total.astype(jnp.bfloat16)
                else:
                    out[pl.ds(pl.multiple_of(row[k], 16), step), lane] = total.astype(jnp.bfloat16)
                return 0

            if rows == step:
                add(0, 0)
            else:
                lax.fori_loop(0, rows // step, add, 0)
            if s < 2:
                launch(k, s + 1)
            else:
                gather(at, out, k, 2, row, sizes, send_sems, recv_sems)
    for s in (2, 1, 0):
        for k in range(PARTS):
            axis, rows = ORDERS[k][s], sizes[k][s]
            whole = rxs[k][s]
            finish(whole, send_sems.at[k, 4 + s], recv_sems.at[k, 4 + s], partner).wait_recv()
            row[k] = row[k] - at[axis] * rows
            if s > 0:
                gather(at, out, k, s - 1, row, sizes, send_sems, recv_sems)
            else:
                lane = pl.ds(pl.multiple_of(core * (PARTS * LANES) + k * LANES, LANES), LANES)
                send(out.at[:, lane], out.at[:, lane], send_sems.at[k, 7], recv_sems.at[k, 7], partner)
    for k in range(PARTS):
        finish(core_rx.at[k], send_sems.at[k, 7], recv_sems.at[k, 7], partner).wait_recv()
    for k in range(PARTS):
        finish(core_rx.at[k], send_sems.at[k, 0], recv_sems.at[k, 0], partner).wait_send()
        finish(core_rx.at[k], send_sems.at[k, 7], recv_sems.at[k, 7], partner).wait_send()
        for s in range(3):
            finish(rxs[k][s], send_sems.at[k, s + 1], recv_sems.at[k, s + 1], partner).wait_send()
            finish(rxs[k][s], send_sems.at[k, s + 4], recv_sems.at[k, s + 4], partner).wait_send()


def gather(at, out, k, s, row, sizes, send_sems, recv_sems):
    axis, rows = ORDERS[k][s], sizes[k][s]
    lane = pl.ds(pl.multiple_of(at["core"] * (PARTS * LANES) + k * LANES, LANES), LANES)
    block = out.at[pl.ds(pl.multiple_of(row[k], 16), rows), lane]
    for delta in range(1, EXTENT[axis]):
        send(block, block, send_sems.at[k, 4 + s], recv_sems.at[k, 4 + s], moved(at, axis, delta))


def reduce_scratch():
    shapes = [pltpu.VMEM((PARTS, ROWS, LANES), jnp.bfloat16)]
    for order in ORDERS:
        rows = ROWS
        for size in stage_rows(order):
            shapes.append(pltpu.VMEM((rows, LANES), jnp.bfloat16))
            rows = size
    for order in ORDERS:
        for axis, size in zip(order, stage_rows(order)):
            shapes.append(pltpu.VMEM((EXTENT[axis] - 1, size, LANES), jnp.bfloat16))
    shapes += [pltpu.SemaphoreType.DMA((PARTS, 8)), pltpu.SemaphoreType.DMA((PARTS, 8))]
    return shapes


def edge_picks():
    picks = np.zeros((2, PITCH, (LAT + 4) * PITCH), np.float32)
    for side, first in ((0, LON_DEV - 2), (1, 0)):
        for i in range(LAT + 4):
            for h in range(2):
                picks[side, 2 * i + h, i * PITCH + first + h] = 1.0
    return picks.reshape(2 * PITCH, -1)


def margin_places():
    places = np.zeros((TAPS, 2, LAT, 2, LAT, PITCH), np.float32)
    for b in range(TAPS):
        for side, first in ((0, -2), (1, LON_DEV)):
            for h in range(2):
                j = first + h - b + 2
                if 0 <= j < LON_DEV:
                    for i in range(LAT):
                        places[b, side, i, h, i, j] = 1.0
    return places.reshape(TAPS, 4 * LAT, POINTS)


def stage_weight(w, staged):
    zeros = jnp.zeros((16, COLS), jnp.bfloat16)
    for a in range(TAPS):
        for b in range(TAPS):
            base = (a * TAPS + b) * CHAN
            staged[base + 64 : base + 80, :] = zeros
            staged[base : base + 64, 640:COLS] = jnp.zeros((64, COLS - 640), jnp.bfloat16)
            staged[base : base + COUT, 0:CIN] = w[a, b]


def forward_own(x, staged, taps):
    for n in range(3):
        lanes = slice(n * 256, n * 256 + 256)

        def one(a, total, n=n):
            rows = pl.ds(pl.multiple_of(a * PITCH + n * 256, 16), 256)
            left = staged[pl.ds(pl.multiple_of(a * TAP_ROWS, 16), TAP_ROWS), :]
            return total + lax.dot_general(left, x[rows, :], NT, preferred_element_type=jnp.float32)

        taps[:, lanes] = lax.fori_loop(0, TAPS, one, jnp.zeros((TAP_ROWS, 256), jnp.float32))


def stage_margin(halo, margin):
    left = halo[0].astype(jnp.float32)
    right = halo[1].astype(jnp.float32)
    for a in range(TAPS):
        margin[a, 0:32, :] = left[2 * a : 2 * a + 32, :].astype(jnp.bfloat16)
        margin[a, 32:64, :] = right[2 * a : 2 * a + 32, :].astype(jnp.bfloat16)


def forward_margin(margin, staged, edge_taps):
    def one(a, total):
        left = staged[pl.ds(pl.multiple_of(a * TAP_ROWS, 16), TAP_ROWS), :]
        return total + lax.dot_general(left, margin[a], NT, preferred_element_type=jnp.float32)

    edge_taps[...] = lax.fori_loop(0, TAPS, one, jnp.zeros((TAP_ROWS, 64), jnp.float32))


def convolved(taps, edge_taps, places, bias):
    total = jnp.broadcast_to(bias, (CHAN, POINTS))
    for b in range(TAPS):
        rows = slice(b * CHAN, b * CHAN + CHAN)
        part = taps[rows, :]
        total = total + (part if b == 2 else pltpu.roll(part, (2 - b) % POINTS, 1))
        if b != 2:
            total = total + jnp.dot(
                edge_taps[rows, :], places[b].astype(jnp.float32),
                precision=lax.Precision.HIGHEST, preferred_element_type=jnp.float32,
            )
    return total


def kernel_terms(values, target, vectors, gradients, score):
    lane = lax.broadcasted_iota(jnp.int32, (16, LANES), 1)
    real = (lane < LON_DEV) | ((lane >= PITCH) & (lane < PITCH + LON_DEV))

    def block(t, score_sum):
        rows = pl.ds(pl.multiple_of(t * 16, 16), 16)
        members = [values[m, rows, :].astype(jnp.float32) for m in range(MEMBERS)]
        width = vectors[rows, :][:, 1:2]
        inverse = jnp.broadcast_to(1.0 / (width * width), (16, LANES))
        half = -0.5 * inverse
        goal = target[rows, :]
        pulls = [jnp.zeros((16, LANES), jnp.float32) for _ in range(MEMBERS)]
        pair_sum = jnp.zeros((16, LANES), jnp.float32)
        for m in range(MEMBERS):
            for n in range(m + 1, MEMBERS):
                spread = members[m] - members[n]
                kernel_pair = jnp.exp(spread * spread * half)
                pair_sum = pair_sum + kernel_pair
                pull = kernel_pair * spread
                pulls[m] = pulls[m] + pull
                pulls[n] = pulls[n] - pull
        obs_sum = jnp.zeros((16, LANES), jnp.float32)
        for m in range(MEMBERS):
            misfit = members[m] - goal
            kernel_obs = jnp.exp(misfit * misfit * half)
            obs_sum = obs_sum + kernel_obs
            gradient = inverse * (misfit * kernel_obs - pulls[m] * (1.0 / MEMBERS))
            gradients[m, rows, :] = jnp.where(real, gradient, 0.0).astype(jnp.bfloat16)
        per_channel = (MEMBERS + 2.0 * pair_sum) * (1.0 / (2 * MEMBERS * MEMBERS)) - obs_sum * (1.0 / MEMBERS)
        channel = t * 16 + lax.broadcasted_iota(jnp.int32, (16, LANES), 0)
        return score_sum + jnp.where(channel < COUT, per_channel, 0.0)

    total = lax.fori_loop(0, CHAN // 16, block, jnp.zeros((16, LANES), jnp.float32))
    score[...] = jnp.broadcast_to(jnp.sum(total, axis=0, keepdims=True) * (1.0 / COUT), (8, LANES))


def stack_gradient(gathered, grad_out, stacked, edge_stacked, places):
    grad = jnp.concatenate(
        [gathered[q].astype(jnp.float32)[:, :CHUNK] for q in range(MEMBERS)], axis=1
    )
    packed = grad.astype(jnp.bfloat16)
    grad_out[...] = packed
    for b in range(TAPS):
        rows = slice(b * CHAN, b * CHAN + CHAN)
        if b == 2:
            stacked[rows, :] = packed
            edge_stacked[rows, :] = jnp.zeros((CHAN, 64), jnp.bfloat16)
        else:
            stacked[rows, :] = pltpu.roll(grad, (b - 2) % POINTS, 1).astype(jnp.bfloat16)
            edge = lax.dot_general(packed, places[b], NT, preferred_element_type=jnp.float32)
            edge_stacked[rows, :] = edge.astype(jnp.bfloat16)


def weight_terms(half, x, margin, stacked, edge_stacked, into):
    lanes = pl.ds(pl.multiple_of(half * (PARTS * LANES), LANES), PARTS * LANES)

    def one(a, _):
        right = x[pl.ds(pl.multiple_of(a * PITCH, 16), POINTS), lanes]
        total = jnp.dot(stacked[...], right, preferred_element_type=jnp.float32)
        total = total + jnp.dot(
            edge_stacked[...], margin[a, :, lanes], preferred_element_type=jnp.float32
        )
        total = total.astype(into.dtype)
        for k in range(PARTS):
            into[k, pl.ds(pl.multiple_of(a * TAP_ROWS, 16), TAP_ROWS), :] = total[
                :, k * LANES : (k + 1) * LANES
            ]
        return 0

    lax.fori_loop(0, TAPS, one, 0)
    for k in range(PARTS):
        into[k, TAPS * TAP_ROWS : ROWS, :] = jnp.zeros((ROWS - TAPS * TAP_ROWS, LANES), into.dtype)


def own_scores(starts, score_rx, owned):
    lane = lax.broadcasted_iota(jnp.int32, (8, LANES), 1)
    row = lax.broadcasted_iota(jnp.int32, (8, LANES), 0)
    me = lax.axis_index("member")
    first, count = starts[me], starts[me + 1] - starts[me]
    wanted = jnp.where(row < count, first + row, -1)
    total = jnp.zeros((8, LANES), jnp.float32)
    for q in range(MEMBERS):
        pair = score_rx[q]
        low = jnp.where(lane < LON_DEV, pair, 0.0)
        high = jnp.where(lane < LON_DEV, pltpu.roll(pair, LANES - PITCH, 1), 0.0)
        total = total + jnp.where(wanted == 2 * q, low, 0.0) + jnp.where(wanted == 2 * q + 1, high, 0.0)
    owned[...] = total


def whole_kernel(x, w, vectors, target, places, picks, starts, out, grad_out, owned, *scratch):
    (
        staged, edges, halo, margin, taps, edge_taps, to_score, values, gradients, gathered, score, score_rx,
        stacked, edge_stacked, theirs, mine, near_send, near_recv,
    ) = scratch[:18]
    core_rx, rest = scratch[18], scratch[19:]
    cur = [rest[3 * k : 3 * k + 3] for k in range(PARTS)]
    rxs = [rest[9 + 3 * k : 12 + 3 * k] for k in range(PARTS)]
    send_sems, recv_sems = rest[18], rest[19]
    at = position()
    member, lon = lax.axis_index("member"), lax.axis_index("lon")
    ahead = (member, lax.rem(lon + 1, GROUPS))
    behind = (member, lax.rem(lon + GROUPS - 1, GROUPS))
    others = [lax.rem(member + delta, MEMBERS) for delta in range(1, MEMBERS)]

    barrier, count = greet(at)
    edge = jnp.dot(picks[...], x[...], preferred_element_type=jnp.float32).astype(jnp.bfloat16)
    edges[0] = edge[:PITCH]
    edges[1] = edge[PITCH:]
    pl.semaphore_wait(barrier, count)
    send_to(edges.at[0], halo.at[0], near_send.at[0], near_recv.at[0], ahead)
    send_to(edges.at[1], halo.at[1], near_send.at[1], near_recv.at[1], behind)
    stage_weight(w, staged)
    forward_own(x, staged, taps)
    finish(halo.at[0], near_send.at[0], near_recv.at[0], at).wait()
    finish(halo.at[1], near_send.at[1], near_recv.at[1], at).wait()
    stage_margin(halo, margin)
    forward_margin(margin, staged, edge_taps)
    outputs = convolved(taps, edge_taps, places, vectors[...][:, 0:1])
    for q in range(MEMBERS):
        to_score[q, :, 0:CHUNK] = outputs[:, q * CHUNK : (q + 1) * CHUNK].astype(jnp.bfloat16)
        to_score[q, :, CHUNK:LANES] = jnp.zeros((CHAN, LANES - CHUNK), jnp.bfloat16)
    for there in others:
        send_to(to_score.at[there], values.at[member], near_send.at[2], near_recv.at[2], (there, lon))
    values[member] = to_score[member]
    finish(values.at[0:7], near_send.at[2], near_recv.at[2], at).wait_recv()
    kernel_terms(values, target, vectors, gradients, score)
    for there in others:
        send_to(gradients.at[there], gathered.at[member], near_send.at[3], near_recv.at[3], (there, lon))
    for there in others:
        send_to(score, score_rx.at[member], near_send.at[4], near_recv.at[4], (there, lon))
    gathered[member] = gradients[member]
    score_rx[member] = score[...]
    finish(gathered.at[0:7], near_send.at[3], near_recv.at[3], at).wait_recv()
    stack_gradient(gathered, grad_out, stacked, edge_stacked, places)
    weight_terms(1 - at["core"], x, margin, stacked, edge_stacked, theirs)
    send_halves(at, theirs, core_rx, send_sems, recv_sems)
    weight_terms(at["core"], x, margin, stacked, edge_stacked, mine)
    finish(score_rx.at[0:7], near_send.at[4], near_recv.at[4], at).wait_recv()
    own_scores(starts, score_rx, owned)
    all_reduce(at, mine, out, core_rx, cur, rxs, send_sems, recv_sems)
    finish(values.at[0:7], near_send.at[2], near_recv.at[2], at).wait_send()
    finish(gathered.at[0:7], near_send.at[3], near_recv.at[3], at).wait_send()
    finish(score_rx.at[0:7], near_send.at[4], near_recv.at[4], at).wait_send()


def kernel_scratch():
    chunk = (MEMBERS, CHAN, LANES)
    return [
        pltpu.VMEM((TAPS * TAP_ROWS, COLS), jnp.bfloat16),
        pltpu.VMEM((2, PITCH, COLS), jnp.bfloat16),
        pltpu.VMEM((2, PITCH, COLS), jnp.bfloat16),
        pltpu.VMEM((TAPS, 64, COLS), jnp.bfloat16),
        pltpu.VMEM((TAP_ROWS, POINTS), jnp.float32),
        pltpu.VMEM((TAP_ROWS, 64), jnp.float32),
        pltpu.VMEM(chunk, jnp.bfloat16),
        pltpu.VMEM(chunk, jnp.bfloat16),
        pltpu.VMEM(chunk, jnp.bfloat16),
        pltpu.VMEM(chunk, jnp.bfloat16),
        pltpu.VMEM((8, LANES), jnp.float32),
        pltpu.VMEM((MEMBERS, 8, LANES), jnp.float32),
        pltpu.VMEM((TAP_ROWS, POINTS), jnp.bfloat16),
        pltpu.VMEM((TAP_ROWS, 64), jnp.bfloat16),
        pltpu.VMEM((PARTS, ROWS, LANES), jnp.bfloat16),
        pltpu.VMEM((PARTS, ROWS, LANES), jnp.float32),
        pltpu.SemaphoreType.DMA((5,)),
        pltpu.SemaphoreType.DMA((5,)),
    ] + reduce_scratch()


def padded_field(fields):
    field = jnp.transpose(fields[0], (1, 2, 0))
    field = jnp.pad(field, ((0, 0), (0, PITCH - LON_DEV), (0, COLS - CIN)))
    longitude = lax.broadcasted_iota(jnp.int32, field.shape, 1)
    channel = lax.broadcasted_iota(jnp.int32, field.shape, 2)
    field = jnp.where((channel == CIN) & (longitude < LON_DEV), jnp.bfloat16(1), field)
    return field.reshape((LAT + 4) * PITCH, COLS)


def body(fields, weight, out_bias, observed, widths, owner_start):
    x = padded_field(fields)
    extra = CHAN - COUT
    vectors = jnp.stack([jnp.pad(out_bias, (0, extra)), jnp.pad(widths, (0, extra), constant_values=1.0)], axis=1)
    vectors = jnp.pad(vectors, ((0, 0), (0, LANES - 2)))
    target = lax.dynamic_slice_in_dim(observed, 2 * lax.axis_index("member"), 2, 1)
    target = jnp.pad(target, ((0, extra), (0, 0), (0, PITCH - LON_DEV))).reshape(CHAN, CHUNK)
    target = jnp.pad(target, ((0, 0), (0, LANES - CHUNK)))
    vmem = pl.BlockSpec(memory_space=pltpu.VMEM)
    summed, grad, owned = pl.pallas_call(
        whole_kernel,
        out_shape=[
            jax.ShapeDtypeStruct((ROWS, COLS), jnp.bfloat16),
            jax.ShapeDtypeStruct((CHAN, POINTS), jnp.bfloat16),
            jax.ShapeDtypeStruct((8, LANES), jnp.float32),
        ],
        in_specs=[vmem] * 6 + [pl.BlockSpec(memory_space=pltpu.SMEM)],
        out_specs=[vmem] * 3,
        scratch_shapes=kernel_scratch(),
        compiler_params=pltpu.CompilerParams(
            collective_id=1, has_side_effects=True, vmem_limit_bytes=56 * 1024 * 1024
        ),
        cost_estimate=pl.CostEstimate(flops=6 << 30, bytes_accessed=16 << 20, transcendentals=1 << 20),
    )(
        x, weight, vectors, target, jnp.asarray(margin_places(), jnp.bfloat16),
        jnp.asarray(edge_picks(), jnp.bfloat16), owner_start[0],
    )
    factor = 1.0 / math.sqrt(MEMBERS * LAT * LON_DEV * GROUPS)
    summed = summed[: TAPS * TAP_ROWS].reshape(TAPS, TAPS, CHAN, COLS)
    weight_grad = summed[:, :, :COUT, :CIN].astype(jnp.float32) * factor
    bias_grad = summed[2, 2, :COUT, CIN].astype(jnp.float32) * factor
    out_grad = grad.reshape(CHAN, LAT, PITCH)[None, :COUT, :, :LON_DEV]
    owned_score = owned[:CAP, :LON_DEV].reshape(1, 1, CAP * LON_DEV)
    return (out_grad, owned_score, weight_grad, bias_grad)


def solution(mesh):
    in_specs = (P("member", None, None, "lon"), P(), P(), P(None, None, "lon"), P(), P("lon", None))
    out_specs = (P("member", None, None, "lon"), P("lon", "member", None), P(), P())
    return jax.shard_map(body, mesh=mesh, in_specs=in_specs, out_specs=out_specs, check_vma=False)
```

```python
import math

import jax
import jax.numpy as jnp
import numpy as np
from jax import lax
from jax.experimental import pallas as pl
from jax.experimental.pallas import tpu as pltpu
from jax.sharding import PartitionSpec as P

MESH = pl.DeviceIdType.MESH
MEMBERS = 8
GROUPS = 32
TAPS = 5
CIN = 641
COUT = 73
CHAN = 80
LAT = 16
LON_DEV = 45
PITCH = 48
POINTS = LAT * PITCH
CHUNK = 2 * PITCH
CAP = 6
TAP_ROWS = TAPS * CHAN
NT = (((1,), (1,)), ((), ()))
ROWS = 2048
LANES = 128
PARTS = 3
COLS = 2 * PARTS * LANES
ORDERS = (("x", "y", "z"), ("y", "x", "z"), ("z", "x", "y"))


def position():
    member = lax.axis_index("member")
    lon = lax.axis_index("lon")
    return {
        "x": (lon // 16) * 2 + member % 2,
        "y": member // 2,
        "z": (lon // 2) % 8,
        "core": lon % 2,
    }


EXTENT = {"x": 4, "y": 4, "z": 8, "core": 2}


def device(at):
    return (at["y"] * 2 + at["x"] % 2, (at["x"] // 2) * 16 + at["z"] * 2 + at["core"])


def moved(at, axis, delta):
    there = dict(at)
    there[axis] = lax.rem(at[axis] + delta, EXTENT[axis])
    return there


def send(src, dst, send_sem, recv_sem, at):
    copy = pltpu.make_async_remote_copy(
        src_ref=src, dst_ref=dst, send_sem=send_sem, recv_sem=recv_sem,
        device_id=device(at), device_id_type=MESH,
    )
    copy.start()


def send_to(src, dst, send_sem, recv_sem, there):
    copy = pltpu.make_async_remote_copy(
        src_ref=src, dst_ref=dst, send_sem=send_sem, recv_sem=recv_sem,
        device_id=there, device_id_type=MESH,
    )
    copy.start()


def finish(ref, send_sem, recv_sem, at):
    copy = pltpu.make_async_remote_copy(
        src_ref=ref, dst_ref=ref, send_sem=send_sem, recv_sem=recv_sem,
        device_id=device(at), device_id_type=MESH,
    )
    return copy


def greet(at):
    barrier = pltpu.get_barrier_semaphore()
    count = 0
    for axis in ("core", "x", "y", "z"):
        for delta in range(1, EXTENT[axis]):
            pl.semaphore_signal(
                barrier, inc=1, device_id=device(moved(at, axis, delta)), device_id_type=MESH
            )
            count += 1
    member, lon = lax.axis_index("member"), lax.axis_index("lon")
    for delta in range(1, MEMBERS):
        there = (lax.rem(member + delta, MEMBERS), lon)
        pl.semaphore_signal(barrier, inc=1, device_id=there, device_id_type=MESH)
        count += 1
    for delta in (1, GROUPS - 1):
        there = (member, lax.rem(lon + delta, GROUPS))
        pl.semaphore_signal(barrier, inc=1, device_id=there, device_id_type=MESH)
        count += 1
    return barrier, count


def stage_rows(order):
    rows, sizes = ROWS, []
    for axis in order:
        rows //= EXTENT[axis]
        sizes.append(rows)
    return sizes


def send_halves(at, theirs, core_rx, send_sems, recv_sems):
    partner = moved(at, "core", 1)
    for k in range(PARTS):
        send(theirs.at[k], core_rx.at[k], send_sems.at[k, 0], recv_sems.at[k, 0], partner)


def all_reduce(at, mine, out, core_rx, cur, rxs, send_sems, recv_sems, meanwhile):
    core = at["core"]
    partner = moved(at, "core", 1)
    row = [0] * PARTS
    sizes = [stage_rows(order) for order in ORDERS]

    def launch(k, s):
        axis, rows = ORDERS[k][s], sizes[k][s]
        for delta in range(1, EXTENT[axis]):
            there = moved(at, axis, delta)
            source = cur[k][s].at[pl.ds(pl.multiple_of(there[axis] * rows, 16), rows)]
            send(source, rxs[k][s].at[delta - 1], send_sems.at[k, s + 1], recv_sems.at[k, s + 1], there)

    for k in range(PARTS):
        finish(core_rx.at[k], send_sems.at[k, 0], recv_sems.at[k, 0], partner).wait_recv()
        step = 256

        def add(i, _, k=k):
            here = pl.ds(pl.multiple_of(i * step, step), step)
            total = mine[k, here, :] + core_rx[k, here, :].astype(jnp.float32)
            cur[k][0][here, :] = total.astype(jnp.bfloat16)
            return 0

        lax.fori_loop(0, ROWS // step, add, 0)
        launch(k, 0)
    meanwhile()
    for s in range(3):
        for k in range(PARTS):
            axis, rows = ORDERS[k][s], sizes[k][s]
            finish(rxs[k][s], send_sems.at[k, s + 1], recv_sems.at[k, s + 1], partner).wait_recv()
            row[k] = row[k] + at[axis] * rows
            base = pl.multiple_of(at[axis] * rows, 16)
            step = min(rows, 128)
            lane = pl.ds(pl.multiple_of(core * (PARTS * LANES) + k * LANES, LANES), LANES)

            def add(i, _, k=k, s=s, axis=axis, base=base, step=step, lane=lane):
                total = cur[k][s][pl.ds(pl.multiple_of(base + i * step, 16), step), :].astype(jnp.float32)
                here = pl.ds(pl.multiple_of(i * step, 16), step)
                for slot in range(EXTENT[axis] - 1):
                    total = total + rxs[k][s][slot, here, :].astype(jnp.float32)
                if s < 2:
                    cur[k][s + 1][here, :] = total.astype(jnp.bfloat16)
                else:
                    out[pl.ds(pl.multiple_of(row[k], 16), step), lane] = total.astype(jnp.bfloat16)
                return 0

            if rows == step:
                add(0, 0)
            else:
                lax.fori_loop(0, rows // step, add, 0)
            if s < 2:
                launch(k, s + 1)
            else:
                gather(at, out, k, 2, row, sizes, send_sems, recv_sems)
    for s in (2, 1, 0):
        for k in range(PARTS):
            axis, rows = ORDERS[k][s], sizes[k][s]
            whole = rxs[k][s]
            finish(whole, send_sems.at[k, 4 + s], recv_sems.at[k, 4 + s], partner).wait_recv()
            row[k] = row[k] - at[axis] * rows
            if s > 0:
                gather(at, out, k, s - 1, row, sizes, send_sems, recv_sems)
            else:
                lane = pl.ds(pl.multiple_of(core * (PARTS * LANES) + k * LANES, LANES), LANES)
                send(out.at[0:ROWS, lane], out.at[0:ROWS, lane], send_sems.at[k, 7], recv_sems.at[k, 7], partner)
    for k in range(PARTS):
        finish(core_rx.at[k], send_sems.at[k, 7], recv_sems.at[k, 7], partner).wait_recv()
    for k in range(PARTS):
        finish(core_rx.at[k], send_sems.at[k, 0], recv_sems.at[k, 0], partner).wait_send()
        finish(core_rx.at[k], send_sems.at[k, 7], recv_sems.at[k, 7], partner).wait_send()
        for s in range(3):
            finish(rxs[k][s], send_sems.at[k, s + 1], recv_sems.at[k, s + 1], partner).wait_send()
            finish(rxs[k][s], send_sems.at[k, s + 4], recv_sems.at[k, s + 4], partner).wait_send()


def gather(at, out, k, s, row, sizes, send_sems, recv_sems):
    axis, rows = ORDERS[k][s], sizes[k][s]
    lane = pl.ds(pl.multiple_of(at["core"] * (PARTS * LANES) + k * LANES, LANES), LANES)
    block = out.at[pl.ds(pl.multiple_of(row[k], 16), rows), lane]
    for delta in range(1, EXTENT[axis]):
        send(block, block, send_sems.at[k, 4 + s], recv_sems.at[k, 4 + s], moved(at, axis, delta))


def reduce_scratch():
    shapes = [pltpu.VMEM((PARTS, ROWS, LANES), jnp.bfloat16)]
    for order in ORDERS:
        rows = ROWS
        for size in stage_rows(order):
            shapes.append(pltpu.VMEM((rows, LANES), jnp.bfloat16))
            rows = size
    for order in ORDERS:
        for axis, size in zip(order, stage_rows(order)):
            shapes.append(pltpu.VMEM((EXTENT[axis] - 1, size, LANES), jnp.bfloat16))
    shapes += [pltpu.SemaphoreType.DMA((PARTS, 8)), pltpu.SemaphoreType.DMA((PARTS, 8))]
    return shapes


def edge_picks():
    picks = np.zeros((2, PITCH, (LAT + 4) * PITCH), np.float32)
    for side, first in ((0, LON_DEV - 2), (1, 0)):
        for i in range(LAT + 4):
            for h in range(2):
                picks[side, 2 * i + h, i * PITCH + first + h] = 1.0
    return picks.reshape(2 * PITCH, -1)


def margin_places():
    places = np.zeros((TAPS, 2, LAT, 2, LAT, PITCH), np.float32)
    for b in range(TAPS):
        for side, first in ((0, -2), (1, LON_DEV)):
            for h in range(2):
                j = first + h - b + 2
                if 0 <= j < LON_DEV:
                    for i in range(LAT):
                        places[b, side, i, h, i, j] = 1.0
    return places.reshape(TAPS, 4 * LAT, POINTS)


def stage_field(raw, x):
    lane = lax.broadcasted_iota(jnp.int32, (PITCH, LANES), 1)
    row = lax.broadcasted_iota(jnp.int32, (PITCH, LANES), 0)
    tail = jnp.where((lane == CIN - 640) & (row < LON_DEV), 1.0, 0.0).astype(jnp.bfloat16)
    zeros = jnp.zeros((16, COLS), jnp.bfloat16)

    def one(i, _):
        base = pl.multiple_of(i * PITCH, 16)
        x[pl.ds(base + 32, 16), :] = zeros
        x[pl.ds(base, PITCH), 640:COLS] = tail
        x[pl.ds(base, LON_DEV), 0:CIN] = raw[i]
        return 0

    lax.fori_loop(0, LAT + 4, one, 0)


def stage_columns(bias, widths, tile, vectors):
    tile[...] = jnp.ones((8, LANES), jnp.float32)
    tile[0:1, 0:COUT] = bias[...]
    tile[1:2, 0:COUT] = widths[...]
    vectors[:, 0:8] = jnp.transpose(tile[...])[0:CHAN, :]


def stage_target(observed, wide, target):
    spots = LON_DEV * LAT
    point = lax.broadcasted_iota(jnp.int32, (LANES, spots), 0)
    spot = lax.broadcasted_iota(jnp.int32, (LANES, spots), 1)
    second = (point >= PITCH).astype(jnp.int32)
    wanted = (point - PITCH * second) * LAT + 2 * lax.axis_index("member") + second
    chosen = ((spot == wanted) & (point < CHUNK)).astype(jnp.float32)
    wide[...] = jnp.zeros((LANES, LANES), jnp.float32)
    wide[:, 0:COUT] = jnp.dot(
        chosen, observed[...].reshape(spots, COUT),
        precision=lax.Precision.HIGHEST, preferred_element_type=jnp.float32,
    )
    target[...] = jnp.transpose(wide[...])[0:CHAN, :]


def write_gradient(packed, grad_out):
    spots = LON_DEV * LAT
    spot = lax.broadcasted_iota(jnp.int32, (spots, POINTS), 0)
    point = lax.broadcasted_iota(jnp.int32, (spots, POINTS), 1)
    wanted = (spot & (LAT - 1)) * PITCH + (spot >> 4)
    moves = jnp.where(point == wanted, 1.0, 0.0).astype(jnp.bfloat16)
    moved_grad = lax.dot_general(moves, packed[...], NT, preferred_element_type=jnp.float32)
    grad_out[...] = moved_grad.astype(jnp.bfloat16).reshape(LON_DEV, LAT, CHAN)[:, :, :COUT]


def stage_weight(w, staged):
    zeros = jnp.zeros((16, COLS), jnp.bfloat16)
    tail = jnp.zeros((64, COLS - 640), jnp.bfloat16)

    def one(a, _):
        for b in range(TAPS):
            base = pl.multiple_of(a * TAP_ROWS + b * CHAN, 16)
            staged[pl.ds(base + 64, 16), :] = zeros
            staged[pl.ds(base, 64), 640:COLS] = tail
            staged[pl.ds(base, COUT), 0:CIN] = w[a, b]
        return 0

    lax.fori_loop(0, TAPS, one, 0)


def forward_own(x, staged, taps):
    for n in range(3):
        lanes = slice(n * 256, n * 256 + 256)

        def one(a, total, n=n):
            rows = pl.ds(pl.multiple_of(a * PITCH + n * 256, 16), 256)
            left = staged[pl.ds(pl.multiple_of(a * TAP_ROWS, 16), TAP_ROWS), :]
            return total + lax.dot_general(left, x[rows, :], NT, preferred_element_type=jnp.float32)

        taps[:, lanes] = lax.fori_loop(0, TAPS, one, jnp.zeros((TAP_ROWS, 256), jnp.float32))


def stage_margin(halo, margin):
    left = halo[0].astype(jnp.float32)
    right = halo[1].astype(jnp.float32)
    for a in range(TAPS):
        margin[a, 0:32, :] = left[2 * a : 2 * a + 32, :].astype(jnp.bfloat16)
        margin[a, 32:64, :] = right[2 * a : 2 * a + 32, :].astype(jnp.bfloat16)


def forward_margin(margin, staged, edge_taps):
    def one(a, total):
        left = staged[pl.ds(pl.multiple_of(a * TAP_ROWS, 16), TAP_ROWS), :]
        return total + lax.dot_general(left, margin[a], NT, preferred_element_type=jnp.float32)

    edge_taps[...] = lax.fori_loop(0, TAPS, one, jnp.zeros((TAP_ROWS, 64), jnp.float32))


def convolved(taps, edge_taps, places, bias):
    total = jnp.broadcast_to(bias, (CHAN, POINTS))
    for b in range(TAPS):
        rows = slice(b * CHAN, b * CHAN + CHAN)
        part = taps[rows, :]
        total = total + (part if b == 2 else pltpu.roll(part, (2 - b) % POINTS, 1))
        if b != 2:
            total = total + jnp.dot(
                edge_taps[rows, :], places[b].astype(jnp.float32),
                precision=lax.Precision.HIGHEST, preferred_element_type=jnp.float32,
            )
    return total


def kernel_terms(values, target, vectors, gradients, score):
    lane = lax.broadcasted_iota(jnp.int32, (16, LANES), 1)
    real = (lane < LON_DEV) | ((lane >= PITCH) & (lane < PITCH + LON_DEV))

    def block(t, score_sum):
        rows = pl.ds(pl.multiple_of(t * 16, 16), 16)
        members = [values[m, rows, :].astype(jnp.float32) for m in range(MEMBERS)]
        width = vectors[rows, :][:, 1:2]
        inverse = jnp.broadcast_to(1.0 / (width * width), (16, LANES))
        half = -0.5 * inverse
        goal = target[rows, :]
        pulls = [jnp.zeros((16, LANES), jnp.float32) for _ in range(MEMBERS)]
        pair_sum = jnp.zeros((16, LANES), jnp.float32)
        for m in range(MEMBERS):
            for n in range(m + 1, MEMBERS):
                spread = members[m] - members[n]
                kernel_pair = jnp.exp(spread * spread * half)
                pair_sum = pair_sum + kernel_pair
                pull = kernel_pair * spread
                pulls[m] = pulls[m] + pull
                pulls[n] = pulls[n] - pull
        obs_sum = jnp.zeros((16, LANES), jnp.float32)
        for m in range(MEMBERS):
            misfit = members[m] - goal
            kernel_obs = jnp.exp(misfit * misfit * half)
            obs_sum = obs_sum + kernel_obs
            gradient = inverse * (misfit * kernel_obs - pulls[m] * (1.0 / MEMBERS))
            gradients[m, rows, :] = jnp.where(real, gradient, 0.0).astype(jnp.bfloat16)
        per_channel = (MEMBERS + 2.0 * pair_sum) * (1.0 / (2 * MEMBERS * MEMBERS)) - obs_sum * (1.0 / MEMBERS)
        channel = t * 16 + lax.broadcasted_iota(jnp.int32, (16, LANES), 0)
        return score_sum + jnp.where(channel < COUT, per_channel, 0.0)

    total = lax.fori_loop(0, CHAN // 16, block, jnp.zeros((16, LANES), jnp.float32))
    score[...] = jnp.broadcast_to(jnp.sum(total, axis=0, keepdims=True) * (1.0 / COUT), (8, LANES))


def stack_gradient(gathered, packed_grad, stacked, edge_stacked, places):
    grad = jnp.concatenate(
        [gathered[q].astype(jnp.float32)[:, :CHUNK] for q in range(MEMBERS)], axis=1
    )
    packed = grad.astype(jnp.bfloat16)
    packed_grad[...] = packed
    for b in range(TAPS):
        rows = slice(b * CHAN, b * CHAN + CHAN)
        if b == 2:
            stacked[rows, :] = packed
            edge_stacked[rows, :] = jnp.zeros((CHAN, 64), jnp.bfloat16)
        else:
            stacked[rows, :] = pltpu.roll(grad, (b - 2) % POINTS, 1).astype(jnp.bfloat16)
            edge = lax.dot_general(packed, places[b], NT, preferred_element_type=jnp.float32)
            edge_stacked[rows, :] = edge.astype(jnp.bfloat16)


def weight_terms(half, x, margin, stacked, edge_stacked, into):
    lanes = pl.ds(pl.multiple_of(half * (PARTS * LANES), LANES), PARTS * LANES)

    def one(a, _):
        right = x[pl.ds(pl.multiple_of(a * PITCH, 16), POINTS), lanes]
        total = jnp.dot(stacked[...], right, preferred_element_type=jnp.float32)
        total = total + jnp.dot(
            edge_stacked[...], margin[a, :, lanes], preferred_element_type=jnp.float32
        )
        total = total.astype(into.dtype)
        for k in range(PARTS):
            into[k, pl.ds(pl.multiple_of(a * TAP_ROWS, 16), TAP_ROWS), :] = total[
                :, k * LANES : (k + 1) * LANES
            ]
        return 0

    lax.fori_loop(0, TAPS, one, 0)
    for k in range(PARTS):
        into[k, TAPS * TAP_ROWS : ROWS, :] = jnp.zeros((ROWS - TAPS * TAP_ROWS, LANES), into.dtype)


def own_scores(starts, score_rx, owned):
    lane = lax.broadcasted_iota(jnp.int32, (8, LANES), 1)
    row = lax.broadcasted_iota(jnp.int32, (8, LANES), 0)
    me = lax.axis_index("member")
    first, count = starts[me], starts[me + 1] - starts[me]
    wanted = jnp.where(row < count, first + row, -1)
    total = jnp.zeros((8, LANES), jnp.float32)
    for q in range(MEMBERS):
        pair = score_rx[q]
        low = jnp.where(lane < LON_DEV, pair, 0.0)
        high = jnp.where(lane < LON_DEV, pltpu.roll(pair, LANES - PITCH, 1), 0.0)
        total = total + jnp.where(wanted == 2 * q, low, 0.0) + jnp.where(wanted == 2 * q + 1, high, 0.0)
    owned[...] = total


def whole_kernel(
    raw_hbm, w_hbm, observed_hbm, places_hbm, picks_hbm, bias, widths, starts, out, grad_out, owned, *scratch
):
    raw, w, observed, places, picks, x, tile, wide, vectors, target, packed, local = scratch[:12]
    scratch = scratch[12:]
    (
        staged, edges, halo, margin, taps, edge_taps, to_score, values, gradients, gathered, score, score_rx,
        stacked, edge_stacked, theirs, mine, near_send, near_recv,
    ) = scratch[:18]
    core_rx, rest = scratch[18], scratch[19:]
    cur = [rest[3 * k : 3 * k + 3] for k in range(PARTS)]
    rxs = [rest[9 + 3 * k : 12 + 3 * k] for k in range(PARTS)]
    send_sems, recv_sems = rest[18], rest[19]
    at = position()
    member, lon = lax.axis_index("member"), lax.axis_index("lon")
    ahead = (member, lax.rem(lon + 1, GROUPS))
    behind = (member, lax.rem(lon + GROUPS - 1, GROUPS))
    others = [lax.rem(member + delta, MEMBERS) for delta in range(1, MEMBERS)]

    loads = [
        pltpu.make_async_copy(source, target_ref, local.at[n])
        for n, (source, target_ref) in enumerate(
            ((raw_hbm, raw), (picks_hbm, picks), (w_hbm, w), (places_hbm, places), (observed_hbm, observed))
        )
    ]
    for load in loads:
        load.start()
    barrier, count = greet(at)
    stage_columns(bias, widths, tile, vectors)
    loads[0].wait()
    stage_field(raw, x)
    loads[1].wait()
    edge = jnp.dot(picks[...], x[...], preferred_element_type=jnp.float32).astype(jnp.bfloat16)
    edges[0] = edge[:PITCH]
    edges[1] = edge[PITCH:]
    pl.semaphore_wait(barrier, count)
    send_to(edges.at[0], halo.at[0], near_send.at[0], near_recv.at[0], ahead)
    send_to(edges.at[1], halo.at[1], near_send.at[1], near_recv.at[1], behind)
    loads[2].wait()
    stage_weight(w, staged)
    forward_own(x, staged, taps)
    loads[3].wait()
    loads[4].wait()
    stage_target(observed, wide, target)
    finish(halo.at[0], near_send.at[0], near_recv.at[0], at).wait()
    finish(halo.at[1], near_send.at[1], near_recv.at[1], at).wait()
    stage_margin(halo, margin)
    forward_margin(margin, staged, edge_taps)
    outputs = convolved(taps, edge_taps, places, vectors[...][:, 0:1])
    for q in range(MEMBERS):
        to_score[q, :, 0:CHUNK] = outputs[:, q * CHUNK : (q + 1) * CHUNK].astype(jnp.bfloat16)
        to_score[q, :, CHUNK:LANES] = jnp.zeros((CHAN, LANES - CHUNK), jnp.bfloat16)
    for there in others:
        send_to(to_score.at[there], values.at[member], near_send.at[2], near_recv.at[2], (there, lon))
    values[member] = to_score[member]
    finish(values.at[0:7], near_send.at[2], near_recv.at[2], at).wait_recv()
    kernel_terms(values, target, vectors, gradients, score)
    for there in others:
        send_to(gradients.at[there], gathered.at[member], near_send.at[3], near_recv.at[3], (there, lon))
    for there in others:
        send_to(score, score_rx.at[member], near_send.at[4], near_recv.at[4], (there, lon))
    gathered[member] = gradients[member]
    score_rx[member] = score[...]
    finish(gathered.at[0:7], near_send.at[3], near_recv.at[3], at).wait_recv()
    stack_gradient(gathered, packed, stacked, edge_stacked, places)
    weight_terms(1 - at["core"], x, margin, stacked, edge_stacked, theirs)
    send_halves(at, theirs, core_rx, send_sems, recv_sems)
    weight_terms(at["core"], x, margin, stacked, edge_stacked, mine)

    def meanwhile():
        write_gradient(packed, grad_out)
        finish(score_rx.at[0:7], near_send.at[4], near_recv.at[4], at).wait_recv()
        own_scores(starts, score_rx, owned)

    all_reduce(at, mine, out, core_rx, cur, rxs, send_sems, recv_sems, meanwhile)
    finish(values.at[0:7], near_send.at[2], near_recv.at[2], at).wait_send()
    finish(gathered.at[0:7], near_send.at[3], near_recv.at[3], at).wait_send()
    finish(score_rx.at[0:7], near_send.at[4], near_recv.at[4], at).wait_send()


def kernel_scratch():
    chunk = (MEMBERS, CHAN, LANES)
    return [
        pltpu.VMEM((LAT + 4, LON_DEV, CIN), jnp.bfloat16),
        pltpu.VMEM((TAPS, TAPS, COUT, CIN), jnp.bfloat16),
        pltpu.VMEM((LON_DEV, LAT, COUT), jnp.float32),
        pltpu.VMEM((TAPS, 4 * LAT, POINTS), jnp.bfloat16),
        pltpu.VMEM((2 * PITCH, (LAT + 4) * PITCH), jnp.bfloat16),
        pltpu.VMEM(((LAT + 4) * PITCH, COLS), jnp.bfloat16),
        pltpu.VMEM((8, LANES), jnp.float32),
        pltpu.VMEM((LANES, LANES), jnp.float32),
        pltpu.VMEM((CHAN, LANES), jnp.float32),
        pltpu.VMEM((CHAN, LANES), jnp.float32),
        pltpu.VMEM((CHAN, POINTS), jnp.bfloat16),
        pltpu.SemaphoreType.DMA((5,)),
        pltpu.VMEM((TAPS * TAP_ROWS, COLS), jnp.bfloat16),
        pltpu.VMEM((2, PITCH, COLS), jnp.bfloat16),
        pltpu.VMEM((2, PITCH, COLS), jnp.bfloat16),
        pltpu.VMEM((TAPS, 64, COLS), jnp.bfloat16),
        pltpu.VMEM((TAP_ROWS, POINTS), jnp.float32),
        pltpu.VMEM((TAP_ROWS, 64), jnp.float32),
        pltpu.VMEM(chunk, jnp.bfloat16),
        pltpu.VMEM(chunk, jnp.bfloat16),
        pltpu.VMEM(chunk, jnp.bfloat16),
        pltpu.VMEM(chunk, jnp.bfloat16),
        pltpu.VMEM((8, LANES), jnp.float32),
        pltpu.VMEM((MEMBERS, 8, LANES), jnp.float32),
        pltpu.VMEM((TAP_ROWS, POINTS), jnp.bfloat16),
        pltpu.VMEM((TAP_ROWS, 64), jnp.bfloat16),
        pltpu.VMEM((PARTS, ROWS, LANES), jnp.bfloat16),
        pltpu.VMEM((PARTS, ROWS, LANES), jnp.float32),
        pltpu.SemaphoreType.DMA((5,)),
        pltpu.SemaphoreType.DMA((5,)),
    ] + reduce_scratch()


def body(fields, weight, out_bias, observed, widths, owner_start):
    vmem = pl.BlockSpec(memory_space=pltpu.VMEM)
    hbm = pl.BlockSpec(memory_space=pl.ANY)
    summed, grad, owned = pl.pallas_call(
        whole_kernel,
        out_shape=[
            jax.ShapeDtypeStruct((26 * CHAN, COLS), jnp.bfloat16),
            jax.ShapeDtypeStruct((LON_DEV, LAT, COUT), jnp.bfloat16),
            jax.ShapeDtypeStruct((8, LANES), jnp.float32),
        ],
        in_specs=[hbm] * 5 + [vmem] * 2 + [pl.BlockSpec(memory_space=pltpu.SMEM)],
        out_specs=[vmem] * 3,
        scratch_shapes=kernel_scratch(),
        compiler_params=pltpu.CompilerParams(
            collective_id=1, has_side_effects=True, vmem_limit_bytes=56 * 1024 * 1024
        ),
        cost_estimate=pl.CostEstimate(flops=6 << 30, bytes_accessed=16 << 20, transcendentals=1 << 20),
    )(
        jnp.transpose(fields[0], (1, 2, 0)), weight, jnp.transpose(observed, (2, 1, 0)),
        jnp.asarray(margin_places(), jnp.bfloat16), jnp.asarray(edge_picks(), jnp.bfloat16),
        out_bias.reshape(1, COUT), widths.reshape(1, COUT), owner_start[0],
    )
    factor = 1.0 / math.sqrt(MEMBERS * LAT * LON_DEV * GROUPS)
    summed = summed.reshape(26, CHAN, COLS)
    weight_grad = (summed[:25, :COUT, :CIN].astype(jnp.float32) * factor).reshape(TAPS, TAPS, COUT, CIN)
    bias_grad = summed[12, :COUT, CIN].astype(jnp.float32) * factor
    out_grad = jnp.transpose(grad, (2, 1, 0))[None]
    owned_score = owned[:CAP, :LON_DEV].reshape(1, 1, CAP * LON_DEV)
    return (out_grad, owned_score, weight_grad, bias_grad)


def solution(mesh):
    in_specs = (P("member", None, None, "lon"), P(), P(), P(None, None, "lon"), P(), P("lon", None))
    out_specs = (P("member", None, None, "lon"), P("lon", "member", None), P(), P())
    return jax.shard_map(body, mesh=mesh, in_specs=in_specs, out_specs=out_specs, check_vma=False)
```

```python
import math

import jax
import jax.numpy as jnp
import numpy as np
from jax import lax
from jax.experimental import pallas as pl
from jax.experimental.pallas import tpu as pltpu
from jax.sharding import PartitionSpec as P

MESH = pl.DeviceIdType.MESH
MEMBERS = 8
GROUPS = 32
TAPS = 5
CIN = 641
COUT = 73
CHAN = 80
LAT = 16
LON_DEV = 45
PITCH = 48
POINTS = LAT * PITCH
CHUNK = 2 * PITCH
CAP = 6
TAP_ROWS = TAPS * CHAN
NT = (((1,), (1,)), ((), ()))
ROWS = 2048
LANES = 128
PARTS = 3
COLS = 768
WIDE = 640
PART_ROWS = (2048, 2048, 1024)
ORDERS = (("x", "y", "z"), ("y", "x", "z"), ("z", "x", "y"))


def position():
    member = lax.axis_index("member")
    lon = lax.axis_index("lon")
    return {
        "x": (lon // 16) * 2 + member % 2,
        "y": member // 2,
        "z": (lon // 2) % 8,
        "core": lon % 2,
    }


EXTENT = {"x": 4, "y": 4, "z": 8, "core": 2}


def device(at):
    return (at["y"] * 2 + at["x"] % 2, (at["x"] // 2) * 16 + at["z"] * 2 + at["core"])


def moved(at, axis, delta):
    there = dict(at)
    there[axis] = lax.rem(at[axis] + delta, EXTENT[axis])
    return there


def send(src, dst, send_sem, recv_sem, at):
    copy = pltpu.make_async_remote_copy(
        src_ref=src, dst_ref=dst, send_sem=send_sem, recv_sem=recv_sem,
        device_id=device(at), device_id_type=MESH,
    )
    copy.start()


def send_to(src, dst, send_sem, recv_sem, there):
    copy = pltpu.make_async_remote_copy(
        src_ref=src, dst_ref=dst, send_sem=send_sem, recv_sem=recv_sem,
        device_id=there, device_id_type=MESH,
    )
    copy.start()


def finish(ref, send_sem, recv_sem, at):
    copy = pltpu.make_async_remote_copy(
        src_ref=ref, dst_ref=ref, send_sem=send_sem, recv_sem=recv_sem,
        device_id=device(at), device_id_type=MESH,
    )
    return copy


def greet(at):
    barrier = pltpu.get_barrier_semaphore()
    count = 0
    for axis in ("core", "x", "y", "z"):
        for delta in range(1, EXTENT[axis]):
            pl.semaphore_signal(
                barrier, inc=1, device_id=device(moved(at, axis, delta)), device_id_type=MESH
            )
            count += 1
    member, lon = lax.axis_index("member"), lax.axis_index("lon")
    for delta in range(1, MEMBERS):
        there = (lax.rem(member + delta, MEMBERS), lon)
        pl.semaphore_signal(barrier, inc=1, device_id=there, device_id_type=MESH)
        count += 1
    for delta in (1, GROUPS - 1):
        there = (member, lax.rem(lon + delta, GROUPS))
        pl.semaphore_signal(barrier, inc=1, device_id=there, device_id_type=MESH)
        count += 1
    return barrier, count


def stage_rows(k):
    rows, sizes = PART_ROWS[k], []
    for axis in ORDERS[k][: 2 if k == 2 else 3]:
        rows //= EXTENT[axis]
        sizes.append(rows)
    return sizes


SIZES = [stage_rows(k) for k in range(PARTS)]


def place(at, out, k, row, rows):
    if k == 2:
        return out.at[pl.ds(pl.multiple_of(at["core"] * 1024 + row, 16), rows), 512:640]
    lane = pl.multiple_of((2 * at["core"] + k) * LANES, LANES)
    return out.at[pl.ds(pl.multiple_of(row, 16), rows), pl.ds(lane, LANES)]


def launch(at, k, s, cur, rxs, send_sems, recv_sems):
    axis, rows = ORDERS[k][s], SIZES[k][s]
    for delta in range(1, EXTENT[axis]):
        there = moved(at, axis, delta)
        source = cur[k][s].at[pl.ds(pl.multiple_of(there[axis] * rows, 16), rows)]
        send(source, rxs[k][s].at[delta - 1], send_sems.at[k, s + 1], recv_sems.at[k, s + 1], there)


def add_core(at, k, mine, core_rx, cur, send_sems, recv_sems):
    finish(core_rx[k], send_sems.at[k, 0], recv_sems.at[k, 0], at).wait_recv()
    step = 256

    def add(i, _):
        here = pl.ds(pl.multiple_of(i * step, step), step)
        if k == 2:
            own = mine[pl.ds(pl.multiple_of(at["core"] * 1024 + i * step, step), step), :]
        else:
            own = mine[k, here, :]
        cur[k][0][here, :] = (own + core_rx[k][here, :].astype(jnp.float32)).astype(jnp.bfloat16)
        return 0

    lax.fori_loop(0, PART_ROWS[k] // step, add, 0)


def gather(at, out, k, s, row, send_sems, recv_sems):
    axis = ORDERS[k][s]
    block = place(at, out, k, row, SIZES[k][s])
    for delta in range(1, EXTENT[axis]):
        send(block, block, send_sems.at[k, 4 + s], recv_sems.at[k, 4 + s], moved(at, axis, delta))


def all_reduce(at, out, core_rx, cur, rxs, shared, send_sems, recv_sems):
    row = [0] * PARTS
    partner = moved(at, "core", 1)
    for s in range(3):
        for k in (2, 0, 1):
            if k == 2 and s == 2:
                finish(shared.at[0:3], send_sems.at[k, 3], recv_sems.at[k, 3], at).wait_recv()
                total = shared[0].astype(jnp.float32)
                for y in range(1, 4):
                    total = total + shared[y].astype(jnp.float32)
                place(at, out, k, row[k], 32)[...] = total.astype(jnp.bfloat16)
                gather(at, out, k, 1, row[k], send_sems, recv_sems)
                continue
            axis, rows = ORDERS[k][s], SIZES[k][s]
            finish(rxs[k][s], send_sems.at[k, s + 1], recv_sems.at[k, s + 1], at).wait_recv()
            row[k] = row[k] + at[axis] * rows
            base = pl.multiple_of(at[axis] * rows, 16)
            step = min(rows, 128)

            def add(i, _, k=k, s=s, axis=axis, base=base, step=step):
                total = cur[k][s][pl.ds(pl.multiple_of(base + i * step, 16), step), :].astype(jnp.float32)
                here = pl.ds(pl.multiple_of(i * step, 16), step)
                for slot in range(EXTENT[axis] - 1):
                    total = total + rxs[k][s][slot, here, :].astype(jnp.float32)
                total = total.astype(jnp.bfloat16)
                if k == 2 and s == 1:
                    shared[at["y"]] = total
                elif s == 2:
                    place(at, out, k, row[k], step)[...] = total
                else:
                    cur[k][s + 1][here, :] = total
                return 0

            if rows == step:
                add(0, 0)
            else:
                lax.fori_loop(0, rows // step, add, 0)
            if k == 2 and s == 1:
                for delta in range(1, 4):
                    own = shared.at[at["y"]]
                    send(own, own, send_sems.at[k, 3], recv_sems.at[k, 3], moved(at, "y", delta))
            elif s == 2:
                gather(at, out, k, 2, row[k], send_sems, recv_sems)
            else:
                launch(at, k, s + 1, cur, rxs, send_sems, recv_sems)
    for s in (2, 1, 0):
        for k in (2, 0, 1):
            if k == 2 and s == 2:
                continue
            axis, rows = ORDERS[k][s], SIZES[k][s]
            finish(rxs[k][s], send_sems.at[k, 4 + s], recv_sems.at[k, 4 + s], at).wait_recv()
            row[k] = row[k] - at[axis] * rows
            if s > 0:
                gather(at, out, k, s - 1, row[k], send_sems, recv_sems)
            else:
                block = place(at, out, k, 0, PART_ROWS[k])
                send(block, block, send_sems.at[k, 7], recv_sems.at[k, 7], partner)
    for k in (2, 0, 1):
        finish(core_rx[k], send_sems.at[k, 7], recv_sems.at[k, 7], partner).wait_recv()
    for k in range(PARTS):
        finish(core_rx[k], send_sems.at[k, 0], recv_sems.at[k, 0], partner).wait_send()
        finish(core_rx[k], send_sems.at[k, 7], recv_sems.at[k, 7], partner).wait_send()
        for s in range(len(SIZES[k])):
            finish(rxs[k][s], send_sems.at[k, s + 1], recv_sems.at[k, s + 1], partner).wait_send()
            finish(rxs[k][s], send_sems.at[k, s + 4], recv_sems.at[k, s + 4], partner).wait_send()
    finish(shared.at[0:3], send_sems.at[2, 3], recv_sems.at[2, 3], partner).wait_send()


def reduce_scratch():
    shapes = [pltpu.VMEM((PART_ROWS[k], LANES), jnp.bfloat16) for k in range(PARTS)]
    for k in range(PARTS):
        rows = PART_ROWS[k]
        for size in SIZES[k]:
            shapes.append(pltpu.VMEM((rows, LANES), jnp.bfloat16))
            rows = size
    for k in range(PARTS):
        for axis, size in zip(ORDERS[k], SIZES[k]):
            shapes.append(pltpu.VMEM((EXTENT[axis] - 1, size, LANES), jnp.bfloat16))
    shapes.append(pltpu.VMEM((4, 32, LANES), jnp.bfloat16))
    shapes += [pltpu.SemaphoreType.DMA((PARTS, 8)), pltpu.SemaphoreType.DMA((PARTS, 8))]
    return shapes


def edge_picks():
    picks = np.zeros((2, PITCH, (LAT + 4) * PITCH), np.float32)
    for side, first in ((0, LON_DEV - 2), (1, 0)):
        for i in range(LAT + 4):
            for h in range(2):
                picks[side, 2 * i + h, i * PITCH + first + h] = 1.0
    return picks.reshape(2 * PITCH, -1)


def margin_places():
    places = np.zeros((TAPS, 2, LAT, 2, LAT, PITCH), np.float32)
    for b in range(TAPS):
        for side, first in ((0, -2), (1, LON_DEV)):
            for h in range(2):
                j = first + h - b + 2
                if 0 <= j < LON_DEV:
                    for i in range(LAT):
                        places[b, side, i, h, i, j] = 1.0
    return places.reshape(TAPS, 4 * LAT, POINTS)


def stage_field(raw, x):
    lane = lax.broadcasted_iota(jnp.int32, (PITCH, LANES), 1)
    row = lax.broadcasted_iota(jnp.int32, (PITCH, LANES), 0)
    tail = jnp.where((lane == CIN - 640) & (row < LON_DEV), 1.0, 0.0).astype(jnp.bfloat16)
    zeros = jnp.zeros((16, COLS), jnp.bfloat16)

    def one(i, _):
        base = pl.multiple_of(i * PITCH, 16)
        x[pl.ds(base + 32, 16), :] = zeros
        x[pl.ds(base, PITCH), 640:COLS] = tail
        x[pl.ds(base, LON_DEV), 0:CIN] = raw[i]
        return 0

    lax.fori_loop(0, LAT + 4, one, 0)


def stage_columns(bias, widths, tile, vectors):
    tile[...] = jnp.ones((8, LANES), jnp.float32)
    tile[0:1, 0:COUT] = bias[...]
    tile[1:2, 0:COUT] = widths[...]
    vectors[:, 0:8] = jnp.transpose(tile[...])[0:CHAN, :]


def stage_target(observed, wide, target):
    spots = LON_DEV * LAT
    point = lax.broadcasted_iota(jnp.int32, (LANES, spots), 0)
    spot = lax.broadcasted_iota(jnp.int32, (LANES, spots), 1)
    second = (point >= PITCH).astype(jnp.int32)
    wanted = (point - PITCH * second) * LAT + 2 * lax.axis_index("member") + second
    chosen = ((spot == wanted) & (point < CHUNK)).astype(jnp.float32)
    wide[...] = jnp.zeros((LANES, LANES), jnp.float32)
    wide[:, 0:COUT] = jnp.dot(
        chosen, observed[...].reshape(spots, COUT),
        precision=lax.Precision.HIGHEST, preferred_element_type=jnp.float32,
    )
    target[...] = jnp.transpose(wide[...])[0:CHAN, :]


def write_gradient(packed, grad_out):
    spots = LON_DEV * LAT
    spot = lax.broadcasted_iota(jnp.int32, (spots, POINTS), 0)
    point = lax.broadcasted_iota(jnp.int32, (spots, POINTS), 1)
    wanted = (spot & (LAT - 1)) * PITCH + (spot >> 4)
    moves = jnp.where(point == wanted, 1.0, 0.0).astype(jnp.bfloat16)
    moved_grad = lax.dot_general(moves, packed[...], NT, preferred_element_type=jnp.float32)
    grad_out[...] = moved_grad.astype(jnp.bfloat16).reshape(LON_DEV, LAT, CHAN)[:, :, :COUT]


def stage_weight(w, staged):
    zeros = jnp.zeros((16, COLS), jnp.bfloat16)
    tail = jnp.zeros((64, COLS - 640), jnp.bfloat16)

    def one(a, _):
        for b in range(TAPS):
            base = pl.multiple_of(a * TAP_ROWS + b * CHAN, 16)
            staged[pl.ds(base + 64, 16), :] = zeros
            staged[pl.ds(base, 64), 640:COLS] = tail
            staged[pl.ds(base, COUT), 0:CIN] = w[a, b]
        return 0

    lax.fori_loop(0, TAPS, one, 0)


def forward_own(x, staged, taps):
    for n in range(3):
        lanes = slice(n * 256, n * 256 + 256)

        def one(a, total, n=n):
            rows = pl.ds(pl.multiple_of(a * PITCH + n * 256, 16), 256)
            left = staged[pl.ds(pl.multiple_of(a * TAP_ROWS, 16), TAP_ROWS), :]
            return total + lax.dot_general(left, x[rows, :], NT, preferred_element_type=jnp.float32)

        taps[:, lanes] = lax.fori_loop(0, TAPS, one, jnp.zeros((TAP_ROWS, 256), jnp.float32))


def stage_margin(halo, margin):
    left = halo[0].astype(jnp.float32)
    right = halo[1].astype(jnp.float32)
    for a in range(TAPS):
        margin[a, 0:32, :] = left[2 * a : 2 * a + 32, :].astype(jnp.bfloat16)
        margin[a, 32:64, :] = right[2 * a : 2 * a + 32, :].astype(jnp.bfloat16)


def forward_margin(margin, staged, edge_taps):
    def one(a, total):
        left = staged[pl.ds(pl.multiple_of(a * TAP_ROWS, 16), TAP_ROWS), :]
        return total + lax.dot_general(left, margin[a], NT, preferred_element_type=jnp.float32)

    edge_taps[...] = lax.fori_loop(0, TAPS, one, jnp.zeros((TAP_ROWS, 64), jnp.float32))


def convolved(taps, edge_taps, places, bias):
    total = jnp.broadcast_to(bias, (CHAN, POINTS))
    for b in range(TAPS):
        rows = slice(b * CHAN, b * CHAN + CHAN)
        part = taps[rows, :]
        total = total + (part if b == 2 else pltpu.roll(part, (2 - b) % POINTS, 1))
        if b != 2:
            total = total + jnp.dot(
                edge_taps[rows, :], places[b].astype(jnp.float32),
                precision=lax.Precision.HIGHEST, preferred_element_type=jnp.float32,
            )
    return total


def kernel_terms(values, target, vectors, gradients, score):
    lane = lax.broadcasted_iota(jnp.int32, (16, LANES), 1)
    real = (lane < LON_DEV) | ((lane >= PITCH) & (lane < PITCH + LON_DEV))

    def block(t, score_sum):
        rows = pl.ds(pl.multiple_of(t * 16, 16), 16)
        members = [values[m, rows, :].astype(jnp.float32) for m in range(MEMBERS)]
        width = vectors[rows, :][:, 1:2]
        inverse = jnp.broadcast_to(1.0 / (width * width), (16, LANES))
        half = -0.5 * inverse
        goal = target[rows, :]
        pulls = [jnp.zeros((16, LANES), jnp.float32) for _ in range(MEMBERS)]
        pair_sum = jnp.zeros((16, LANES), jnp.float32)
        for m in range(MEMBERS):
            for n in range(m + 1, MEMBERS):
                spread = members[m] - members[n]
                kernel_pair = jnp.exp(spread * spread * half)
                pair_sum = pair_sum + kernel_pair
                pull = kernel_pair * spread
                pulls[m] = pulls[m] + pull
                pulls[n] = pulls[n] - pull
        obs_sum = jnp.zeros((16, LANES), jnp.float32)
        for m in range(MEMBERS):
            misfit = members[m] - goal
            kernel_obs = jnp.exp(misfit * misfit * half)
            obs_sum = obs_sum + kernel_obs
            gradient = inverse * (misfit * kernel_obs - pulls[m] * (1.0 / MEMBERS))
            gradients[m, rows, :] = jnp.where(real, gradient, 0.0).astype(jnp.bfloat16)
        per_channel = (MEMBERS + 2.0 * pair_sum) * (1.0 / (2 * MEMBERS * MEMBERS)) - obs_sum * (1.0 / MEMBERS)
        channel = t * 16 + lax.broadcasted_iota(jnp.int32, (16, LANES), 0)
        return score_sum + jnp.where(channel < COUT, per_channel, 0.0)

    total = lax.fori_loop(0, CHAN // 16, block, jnp.zeros((16, LANES), jnp.float32))
    score[...] = jnp.broadcast_to(jnp.sum(total, axis=0, keepdims=True) * (1.0 / COUT), (8, LANES))


def stack_gradient(gathered, packed_grad, stacked, edge_stacked, places):
    grad = jnp.concatenate(
        [gathered[q].astype(jnp.float32)[:, :CHUNK] for q in range(MEMBERS)], axis=1
    )
    packed = grad.astype(jnp.bfloat16)
    packed_grad[...] = packed
    for b in range(TAPS):
        rows = slice(b * CHAN, b * CHAN + CHAN)
        if b == 2:
            stacked[rows, :] = packed
            edge_stacked[rows, :] = jnp.zeros((CHAN, 64), jnp.bfloat16)
        else:
            stacked[rows, :] = pltpu.roll(grad, (b - 2) % POINTS, 1).astype(jnp.bfloat16)
            edge = lax.dot_general(packed, places[b], NT, preferred_element_type=jnp.float32)
            edge_stacked[rows, :] = edge.astype(jnp.bfloat16)


def product(a, lanes, x, margin, stacked, edge_stacked):
    right = x[pl.ds(pl.multiple_of(a * PITCH, 16), POINTS), lanes]
    total = jnp.dot(stacked[...], right, preferred_element_type=jnp.float32)
    return total + jnp.dot(edge_stacked[...], margin[a, :, lanes], preferred_element_type=jnp.float32)


def shared_terms(x, margin, stacked, edge_stacked, fifth, fifth_sent, tails, extra):
    def one(a, _):
        total = product(a, slice(512, 768), x, margin, stacked, edge_stacked)
        rows = pl.ds(pl.multiple_of(a * TAP_ROWS, 16), TAP_ROWS)
        fifth[rows, :] = total[:, :LANES]
        fifth_sent[rows, :] = total[:, :LANES].astype(jnp.bfloat16)
        tails[a, :, 0:TAP_ROWS] = jnp.transpose(total[:, LANES:])[0:8, :]
        return 0

    lax.fori_loop(0, TAPS, one, 0)
    spare = ROWS - TAPS * TAP_ROWS
    fifth[TAPS * TAP_ROWS : ROWS, :] = jnp.zeros((spare, LANES), jnp.float32)
    fifth_sent[TAPS * TAP_ROWS : ROWS, :] = jnp.zeros((spare, LANES), jnp.bfloat16)
    extra[...] = jnp.zeros((16, 512), jnp.float32)
    for a in range(TAPS):
        extra[a : a + 1, 0:TAP_ROWS] = tails[a, 0:1, 0:TAP_ROWS]
    extra[TAPS : TAPS + 1, 0:TAP_ROWS] = tails[2, 1:2, 0:TAP_ROWS]


def weight_terms(half, x, margin, stacked, edge_stacked, extra, into):
    lanes = pl.ds(pl.multiple_of(half * 256, 256), 256)

    def one(a, _):
        total = product(a, lanes, x, margin, stacked, edge_stacked).astype(into.dtype)
        rows = pl.ds(pl.multiple_of(a * TAP_ROWS, 16), TAP_ROWS)
        for k in range(2):
            into[k, rows, :] = total[:, k * LANES : (k + 1) * LANES]
        return 0

    lax.fori_loop(0, TAPS, one, 0)
    first = TAPS * TAP_ROWS
    more = extra[:, lanes].astype(into.dtype)
    for k in range(2):
        into[k, first : first + 16, :] = more[:, k * LANES : (k + 1) * LANES]
        into[k, first + 16 : ROWS, :] = jnp.zeros((ROWS - first - 16, LANES), into.dtype)


def own_scores(starts, score_rx, owned):
    lane = lax.broadcasted_iota(jnp.int32, (8, LANES), 1)
    row = lax.broadcasted_iota(jnp.int32, (8, LANES), 0)
    me = lax.axis_index("member")
    first, count = starts[me], starts[me + 1] - starts[me]
    wanted = jnp.where(row < count, first + row, -1)
    total = jnp.zeros((8, LANES), jnp.float32)
    for q in range(MEMBERS):
        pair = score_rx[q]
        low = jnp.where(lane < LON_DEV, pair, 0.0)
        high = jnp.where(lane < LON_DEV, pltpu.roll(pair, LANES - PITCH, 1), 0.0)
        total = total + jnp.where(wanted == 2 * q, low, 0.0) + jnp.where(wanted == 2 * q + 1, high, 0.0)
    owned[...] = total


def whole_kernel(
    raw_hbm, w_hbm, observed_hbm, places_hbm, picks_hbm, bias, widths, starts, out, grad_out, owned, *scratch
):
    raw, w, observed, places, picks, x, tile, wide, vectors, target, packed, local = scratch[:12]
    scratch = scratch[12:]
    (
        staged, edges, halo, margin, taps, edge_taps, to_score, values, gradients, gathered, score, score_rx,
        stacked, edge_stacked, theirs, mine, fifth, fifth_sent, tails, extra, near_send, near_recv,
    ) = scratch[:22]
    core_rx, rest = scratch[22:25], scratch[25:]
    cur = [rest[3 * k : 3 * k + 3] for k in range(PARTS)]
    rxs = [rest[8 + 3 * k : 11 + 3 * k] for k in range(PARTS)]
    shared, send_sems, recv_sems = rest[16:19]
    at = position()
    member, lon = lax.axis_index("member"), lax.axis_index("lon")
    ahead = (member, lax.rem(lon + 1, GROUPS))
    behind = (member, lax.rem(lon + GROUPS - 1, GROUPS))
    others = [lax.rem(member + delta, MEMBERS) for delta in range(1, MEMBERS)]

    loads = [
        pltpu.make_async_copy(source, target_ref, local.at[n])
        for n, (source, target_ref) in enumerate(
            ((raw_hbm, raw), (picks_hbm, picks), (w_hbm, w), (places_hbm, places), (observed_hbm, observed))
        )
    ]
    for load in loads:
        load.start()
    barrier, count = greet(at)
    stage_columns(bias, widths, tile, vectors)
    loads[0].wait()
    stage_field(raw, x)
    loads[1].wait()
    edge = jnp.dot(picks[...], x[...], preferred_element_type=jnp.float32).astype(jnp.bfloat16)
    edges[0] = edge[:PITCH]
    edges[1] = edge[PITCH:]
    pl.semaphore_wait(barrier, count)
    send_to(edges.at[0], halo.at[0], near_send.at[0], near_recv.at[0], ahead)
    send_to(edges.at[1], halo.at[1], near_send.at[1], near_recv.at[1], behind)
    loads[2].wait()
    stage_weight(w, staged)
    forward_own(x, staged, taps)
    loads[3].wait()
    loads[4].wait()
    stage_target(observed, wide, target)
    finish(halo.at[0], near_send.at[0], near_recv.at[0], at).wait()
    finish(halo.at[1], near_send.at[1], near_recv.at[1], at).wait()
    stage_margin(halo, margin)
    forward_margin(margin, staged, edge_taps)
    outputs = convolved(taps, edge_taps, places, vectors[...][:, 0:1])
    for q in range(MEMBERS):
        to_score[q, :, 0:CHUNK] = outputs[:, q * CHUNK : (q + 1) * CHUNK].astype(jnp.bfloat16)
        to_score[q, :, CHUNK:LANES] = jnp.zeros((CHAN, LANES - CHUNK), jnp.bfloat16)
    for there in others:
        send_to(to_score.at[there], values.at[member], near_send.at[2], near_recv.at[2], (there, lon))
    values[member] = to_score[member]
    finish(values.at[0:7], near_send.at[2], near_recv.at[2], at).wait_recv()
    kernel_terms(values, target, vectors, gradients, score)
    for there in others:
        send_to(gradients.at[there], gathered.at[member], near_send.at[3], near_recv.at[3], (there, lon))
    for there in others:
        send_to(score, score_rx.at[member], near_send.at[4], near_recv.at[4], (there, lon))
    gathered[member] = gradients[member]
    score_rx[member] = score[...]
    finish(gathered.at[0:7], near_send.at[3], near_recv.at[3], at).wait_recv()
    stack_gradient(gathered, packed, stacked, edge_stacked, places)
    core, partner = at["core"], moved(at, "core", 1)
    shared_terms(x, margin, stacked, edge_stacked, fifth, fifth_sent, tails, extra)
    source = fifth_sent.at[pl.ds(pl.multiple_of((1 - core) * 1024, 16), 1024)]
    send(source, core_rx[2], send_sems.at[2, 0], recv_sems.at[2, 0], partner)
    weight_terms(1 - core, x, margin, stacked, edge_stacked, extra, theirs)
    for k in range(2):
        send(theirs.at[k], core_rx[k], send_sems.at[k, 0], recv_sems.at[k, 0], partner)
    add_core(at, 2, fifth, core_rx, cur, send_sems, recv_sems)
    launch(at, 2, 0, cur, rxs, send_sems, recv_sems)
    weight_terms(core, x, margin, stacked, edge_stacked, extra, mine)
    for k in range(2):
        add_core(at, k, mine, core_rx, cur, send_sems, recv_sems)
        launch(at, k, 0, cur, rxs, send_sems, recv_sems)
    write_gradient(packed, grad_out)
    finish(score_rx.at[0:7], near_send.at[4], near_recv.at[4], at).wait_recv()
    own_scores(starts, score_rx, owned)
    all_reduce(at, out, core_rx, cur, rxs, shared, send_sems, recv_sems)
    finish(values.at[0:7], near_send.at[2], near_recv.at[2], at).wait_send()
    finish(gathered.at[0:7], near_send.at[3], near_recv.at[3], at).wait_send()
    finish(score_rx.at[0:7], near_send.at[4], near_recv.at[4], at).wait_send()


def kernel_scratch():
    chunk = (MEMBERS, CHAN, LANES)
    return [
        pltpu.VMEM((LAT + 4, LON_DEV, CIN), jnp.bfloat16),
        pltpu.VMEM((TAPS, TAPS, COUT, CIN), jnp.bfloat16),
        pltpu.VMEM((LON_DEV, LAT, COUT), jnp.float32),
        pltpu.VMEM((TAPS, 4 * LAT, POINTS), jnp.bfloat16),
        pltpu.VMEM((2 * PITCH, (LAT + 4) * PITCH), jnp.bfloat16),
        pltpu.VMEM(((LAT + 4) * PITCH, COLS), jnp.bfloat16),
        pltpu.VMEM((8, LANES), jnp.float32),
        pltpu.VMEM((LANES, LANES), jnp.float32),
        pltpu.VMEM((CHAN, LANES), jnp.float32),
        pltpu.VMEM((CHAN, LANES), jnp.float32),
        pltpu.VMEM((CHAN, POINTS), jnp.bfloat16),
        pltpu.SemaphoreType.DMA((5,)),
        pltpu.VMEM((TAPS * TAP_ROWS, COLS), jnp.bfloat16),
        pltpu.VMEM((2, PITCH, COLS), jnp.bfloat16),
        pltpu.VMEM((2, PITCH, COLS), jnp.bfloat16),
        pltpu.VMEM((TAPS, 64, COLS), jnp.bfloat16),
        pltpu.VMEM((TAP_ROWS, POINTS), jnp.float32),
        pltpu.VMEM((TAP_ROWS, 64), jnp.float32),
        pltpu.VMEM(chunk, jnp.bfloat16),
        pltpu.VMEM(chunk, jnp.bfloat16),
        pltpu.VMEM(chunk, jnp.bfloat16),
        pltpu.VMEM(chunk, jnp.bfloat16),
        pltpu.VMEM((8, LANES), jnp.float32),
        pltpu.VMEM((MEMBERS, 8, LANES), jnp.float32),
        pltpu.VMEM((TAP_ROWS, POINTS), jnp.bfloat16),
        pltpu.VMEM((TAP_ROWS, 64), jnp.bfloat16),
        pltpu.VMEM((2, ROWS, LANES), jnp.bfloat16),
        pltpu.VMEM((2, ROWS, LANES), jnp.float32),
        pltpu.VMEM((ROWS, LANES), jnp.float32),
        pltpu.VMEM((ROWS, LANES), jnp.bfloat16),
        pltpu.VMEM((TAPS, 8, 512), jnp.float32),
        pltpu.VMEM((16, 512), jnp.float32),
        pltpu.SemaphoreType.DMA((5,)),
        pltpu.SemaphoreType.DMA((5,)),
    ] + reduce_scratch()


def finish_kernel(main, extra, weight_grad, bias_grad):
    factor = 1.0 / math.sqrt(MEMBERS * LAT * LON_DEV * GROUPS)
    a = pl.program_id(0)
    more = extra[...].astype(jnp.float32) * factor
    number = lax.broadcasted_iota(jnp.int32, (16, WIDE), 0)
    last = jnp.sum(jnp.where(number == a, more, 0.0), axis=0, keepdims=True)
    last = jnp.transpose(jnp.broadcast_to(last[:, 0:512], (8, 512)))
    for b in range(TAPS):
        weight_grad[0, b, :, 0:WIDE] = (
            main[b * CHAN : (b + 1) * CHAN, :].astype(jnp.float32)[:COUT, :] * factor
        )
        weight_grad[0, b, :, WIDE:CIN] = last[b * CHAN : b * CHAN + COUT, 0:1]
    bias_grad[...] = more[TAPS : TAPS + 1, 2 * CHAN : 2 * CHAN + COUT]


def body(fields, weight, out_bias, observed, widths, owner_start):
    vmem = pl.BlockSpec(memory_space=pltpu.VMEM)
    hbm = pl.BlockSpec(memory_space=pl.ANY)
    summed, grad, owned = pl.pallas_call(
        whole_kernel,
        out_shape=[
            jax.ShapeDtypeStruct((ROWS, WIDE), jnp.bfloat16),
            jax.ShapeDtypeStruct((LON_DEV, LAT, COUT), jnp.bfloat16),
            jax.ShapeDtypeStruct((8, LANES), jnp.float32),
        ],
        in_specs=[hbm] * 5 + [vmem] * 2 + [pl.BlockSpec(memory_space=pltpu.SMEM)],
        out_specs=[vmem] * 3,
        scratch_shapes=kernel_scratch(),
        compiler_params=pltpu.CompilerParams(
            collective_id=1, has_side_effects=True, vmem_limit_bytes=56 * 1024 * 1024
        ),
        cost_estimate=pl.CostEstimate(flops=6 << 30, bytes_accessed=16 << 20, transcendentals=1 << 20),
    )(
        jnp.transpose(fields[0], (1, 2, 0)), weight, jnp.transpose(observed, (2, 1, 0)),
        jnp.asarray(margin_places(), jnp.bfloat16), jnp.asarray(edge_picks(), jnp.bfloat16),
        out_bias.reshape(1, COUT), widths.reshape(1, COUT), owner_start[0],
    )
    weight_grad, bias_grad = pl.pallas_call(
        finish_kernel,
        grid=(TAPS,),
        out_shape=[
            jax.ShapeDtypeStruct((TAPS, TAPS, COUT, CIN), jnp.float32),
            jax.ShapeDtypeStruct((1, COUT), jnp.float32),
        ],
        in_specs=[
            pl.BlockSpec((TAP_ROWS, WIDE), lambda a: (a, 0)),
            pl.BlockSpec((16, WIDE), lambda a: (TAPS * TAP_ROWS // 16, 0)),
        ],
        out_specs=[
            pl.BlockSpec((1, TAPS, COUT, CIN), lambda a: (a, 0, 0, 0)),
            pl.BlockSpec((1, COUT), lambda a: (0, 0)),
        ],
        compiler_params=pltpu.CompilerParams(vmem_limit_bytes=12 * 1024 * 1024),
    )(summed, summed)
    bias_grad = bias_grad.reshape(COUT)
    out_grad = jnp.transpose(grad, (2, 1, 0))[None]
    owned_score = owned[:CAP, :LON_DEV].reshape(1, 1, CAP * LON_DEV)
    return (out_grad, owned_score, weight_grad, bias_grad)


def solution(mesh):
    in_specs = (P("member", None, None, "lon"), P(), P(), P(None, None, "lon"), P(), P("lon", None))
    out_specs = (P("member", None, None, "lon"), P("lon", "member", None), P(), P())
    return jax.shard_map(body, mesh=mesh, in_specs=in_specs, out_specs=out_specs, check_vma=False)
```

```python
import math

import jax
import jax.numpy as jnp
import numpy as np
from jax import lax
from jax.experimental import pallas as pl
from jax.experimental.pallas import tpu as pltpu
from jax.sharding import PartitionSpec as P

MESH = pl.DeviceIdType.MESH
MEMBERS = 8
GROUPS = 32
TAPS = 5
CIN = 641
COUT = 73
CHAN = 80
LAT = 16
LON_DEV = 45
PITCH = 48
POINTS = LAT * PITCH
CHUNK = 2 * PITCH
CAP = 6
TAP_ROWS = TAPS * CHAN
NT = (((1,), (1,)), ((), ()))
ROWS = 2048
LANES = 128
PARTS = 3
COLS = 768
WIDE = 640
PART_ROWS = (2048, 2048, 1024)
ORDERS = (("x", "y", "z"), ("y", "x", "z"), ("z", "x", "y"))


def position():
    member = lax.axis_index("member")
    lon = lax.axis_index("lon")
    return {
        "x": (lon // 16) * 2 + member % 2,
        "y": member // 2,
        "z": (lon // 2) % 8,
        "core": lon % 2,
    }


EXTENT = {"x": 4, "y": 4, "z": 8, "core": 2}


def device(at):
    return (at["y"] * 2 + at["x"] % 2, (at["x"] // 2) * 16 + at["z"] * 2 + at["core"])


def moved(at, axis, delta):
    there = dict(at)
    there[axis] = lax.rem(at[axis] + delta, EXTENT[axis])
    return there


def send(src, dst, send_sem, recv_sem, at):
    copy = pltpu.make_async_remote_copy(
        src_ref=src, dst_ref=dst, send_sem=send_sem, recv_sem=recv_sem,
        device_id=device(at), device_id_type=MESH,
    )
    copy.start()


def send_to(src, dst, send_sem, recv_sem, there):
    copy = pltpu.make_async_remote_copy(
        src_ref=src, dst_ref=dst, send_sem=send_sem, recv_sem=recv_sem,
        device_id=there, device_id_type=MESH,
    )
    copy.start()


def finish(ref, send_sem, recv_sem, at):
    copy = pltpu.make_async_remote_copy(
        src_ref=ref, dst_ref=ref, send_sem=send_sem, recv_sem=recv_sem,
        device_id=device(at), device_id_type=MESH,
    )
    return copy


def greet(at):
    barrier = pltpu.get_barrier_semaphore()
    count = 0
    for axis in ("core", "x", "y", "z"):
        for delta in range(1, EXTENT[axis]):
            pl.semaphore_signal(
                barrier, inc=1, device_id=device(moved(at, axis, delta)), device_id_type=MESH
            )
            count += 1
    member, lon = lax.axis_index("member"), lax.axis_index("lon")
    for delta in range(1, MEMBERS):
        there = (lax.rem(member + delta, MEMBERS), lon)
        pl.semaphore_signal(barrier, inc=1, device_id=there, device_id_type=MESH)
        count += 1
    for delta in (1, GROUPS - 1):
        there = (member, lax.rem(lon + delta, GROUPS))
        pl.semaphore_signal(barrier, inc=1, device_id=there, device_id_type=MESH)
        count += 1
    return barrier, count


def stage_rows(k):
    rows, sizes = PART_ROWS[k], []
    for axis in ORDERS[k][: 2 if k == 2 else 3]:
        rows //= EXTENT[axis]
        sizes.append(rows)
    return sizes


SIZES = [stage_rows(k) for k in range(PARTS)]


def place(at, out, k, row, rows):
    if k == 2:
        return out.at[pl.ds(pl.multiple_of(at["core"] * 1024 + row, 16), rows), 512:640]
    lane = pl.multiple_of((2 * at["core"] + k) * LANES, LANES)
    return out.at[pl.ds(pl.multiple_of(row, 16), rows), pl.ds(lane, LANES)]


def launch(at, k, s, cur, rxs, send_sems, recv_sems):
    axis, rows = ORDERS[k][s], SIZES[k][s]
    for delta in range(1, EXTENT[axis]):
        there = moved(at, axis, delta)
        source = cur[k][s].at[pl.ds(pl.multiple_of(there[axis] * rows, 16), rows)]
        send(source, rxs[k][s].at[delta - 1], send_sems.at[k, s + 1], recv_sems.at[k, s + 1], there)


def add_core(at, k, mine, core_rx, cur, send_sems, recv_sems):
    finish(core_rx[k], send_sems.at[k, 0], recv_sems.at[k, 0], at).wait_recv()
    step = 256

    def add(i, _):
        here = pl.ds(pl.multiple_of(i * step, step), step)
        if k == 2:
            own = mine[pl.ds(pl.multiple_of(at["core"] * 1024 + i * step, step), step), :]
        else:
            own = mine[k, here, :]
        cur[k][0][here, :] = (own + core_rx[k][here, :].astype(jnp.float32)).astype(jnp.bfloat16)
        return 0

    lax.fori_loop(0, PART_ROWS[k] // step, add, 0)


def gather(at, out, k, s, row, send_sems, recv_sems):
    axis = ORDERS[k][s]
    block = place(at, out, k, row, SIZES[k][s])
    for delta in range(1, EXTENT[axis]):
        send(block, block, send_sems.at[k, 4 + s], recv_sems.at[k, 4 + s], moved(at, axis, delta))


def spread(at, out, k, dy, dx, send_sem, recv_sem, there):
    first, second = ORDERS[k][0], ORDERS[k][1]
    row = lax.rem(at[first] + 4 - dx, 4) * SIZES[k][0] + lax.rem(at[second] + 4 - dy, 4) * SIZES[k][1]
    block = place(at, out, k, row, SIZES[k][1])
    if there is None:
        finish(block, send_sem, recv_sem, at).wait_recv()
    else:
        send(block, block, send_sem, recv_sem, there)


def all_reduce(at, out, core_rx, cur, rxs, shared, send_sems, recv_sems, mid_recv, far_recv):
    row = [0] * PARTS
    partner = moved(at, "core", 1)
    for s in range(3):
        for k in (2, 0, 1):
            if k == 2 and s == 2:
                finish(shared.at[0:3], send_sems.at[k, 3], recv_sems.at[k, 3], at).wait_recv()
                total = shared[0].astype(jnp.float32)
                for y in range(1, 4):
                    total = total + shared[y].astype(jnp.float32)
                place(at, out, k, row[k], 32)[...] = total.astype(jnp.bfloat16)
                gather(at, out, k, 1, row[k], send_sems, recv_sems)
                continue
            axis, rows = ORDERS[k][s], SIZES[k][s]
            finish(rxs[k][s], send_sems.at[k, s + 1], recv_sems.at[k, s + 1], at).wait_recv()
            row[k] = row[k] + at[axis] * rows
            base = pl.multiple_of(at[axis] * rows, 16)
            step = min(rows, 128)

            def add(i, _, k=k, s=s, axis=axis, base=base, step=step):
                total = cur[k][s][pl.ds(pl.multiple_of(base + i * step, 16), step), :].astype(jnp.float32)
                here = pl.ds(pl.multiple_of(i * step, 16), step)
                for slot in range(EXTENT[axis] - 1):
                    total = total + rxs[k][s][slot, here, :].astype(jnp.float32)
                total = total.astype(jnp.bfloat16)
                if k == 2 and s == 1:
                    shared[at["y"]] = total
                elif s == 2:
                    place(at, out, k, row[k], step)[...] = total
                else:
                    cur[k][s + 1][here, :] = total
                return 0

            if rows == step:
                add(0, 0)
            else:
                lax.fori_loop(0, rows // step, add, 0)
            if k == 2 and s == 1:
                for delta in range(1, 4):
                    own = shared.at[at["y"]]
                    send(own, own, send_sems.at[k, 3], recv_sems.at[k, 3], moved(at, "y", delta))
            elif s == 2:
                gather(at, out, k, 2, row[k], send_sems, recv_sems)
            else:
                launch(at, k, s + 1, cur, rxs, send_sems, recv_sems)
    def arrived(k, s):
        finish(rxs[k][s], send_sems.at[k, 4 + s], recv_sems.at[k, 4 + s], at).wait_recv()

    def onward(k, dy):
        first = ORDERS[k][0]
        for dx in (2, 1, 3):
            spread(at, out, k, dy, 0, send_sems.at[k, 4], far_recv.at[k, 4 * dx + dy], moved(at, first, dx))
        spread(at, out, k, dy, 0, send_sems.at[k, 7], recv_sems.at[k, 7], partner)

    for k in range(2):
        arrived(k, 2)
        for dy in (2, 1, 3):
            there = moved(at, ORDERS[k][1], dy)
            spread(at, out, k, 0, 0, send_sems.at[k, 5], mid_recv.at[k, dy], there)
        onward(k, 0)
    arrived(2, 1)
    row[2] = row[2] - at["x"] * SIZES[2][1]
    gather(at, out, 2, 0, row[2], send_sems, recv_sems)
    for dy in (1, 3, 2):
        for k in range(2):
            spread(at, out, k, dy, 0, send_sems.at[k, 5], mid_recv.at[k, dy], None)
            onward(k, dy)
    for dy in (0, 1, 3, 2):
        if dy == 2:
            arrived(2, 0)
            block = place(at, out, 2, 0, PART_ROWS[2])
            send(block, block, send_sems.at[2, 7], recv_sems.at[2, 7], partner)
        for dx in (1, 3, 2):
            for k in range(2):
                spread(at, out, k, dy, dx, send_sems.at[k, 4], far_recv.at[k, 4 * dx + dy], None)
                spread(at, out, k, dy, dx, send_sems.at[k, 7], recv_sems.at[k, 7], partner)
    for k in (2, 0, 1):
        finish(core_rx[k], send_sems.at[k, 7], recv_sems.at[k, 7], partner).wait_recv()
    for k in range(PARTS):
        finish(core_rx[k], send_sems.at[k, 0], recv_sems.at[k, 0], partner).wait_send()
        finish(core_rx[k], send_sems.at[k, 7], recv_sems.at[k, 7], partner).wait_send()
        for s in range(len(SIZES[k])):
            finish(rxs[k][s], send_sems.at[k, s + 1], recv_sems.at[k, s + 1], partner).wait_send()
            finish(rxs[k][s], send_sems.at[k, s + 4], recv_sems.at[k, s + 4], partner).wait_send()
    finish(shared.at[0:3], send_sems.at[2, 3], recv_sems.at[2, 3], partner).wait_send()


def reduce_scratch():
    shapes = [pltpu.VMEM((PART_ROWS[k], LANES), jnp.bfloat16) for k in range(PARTS)]
    for k in range(PARTS):
        rows = PART_ROWS[k]
        for size in SIZES[k]:
            shapes.append(pltpu.VMEM((rows, LANES), jnp.bfloat16))
            rows = size
    for k in range(PARTS):
        for axis, size in zip(ORDERS[k], SIZES[k]):
            shapes.append(pltpu.VMEM((EXTENT[axis] - 1, size, LANES), jnp.bfloat16))
    shapes.append(pltpu.VMEM((4, 32, LANES), jnp.bfloat16))
    shapes += [pltpu.SemaphoreType.DMA((PARTS, 8)), pltpu.SemaphoreType.DMA((PARTS, 8))]
    shapes += [pltpu.SemaphoreType.DMA((2, 4)), pltpu.SemaphoreType.DMA((2, 16))]
    return shapes


def edge_picks():
    picks = np.zeros((2, PITCH, (LAT + 4) * PITCH), np.float32)
    for side, first in ((0, LON_DEV - 2), (1, 0)):
        for i in range(LAT + 4):
            for h in range(2):
                picks[side, 2 * i + h, i * PITCH + first + h] = 1.0
    return picks.reshape(2 * PITCH, -1)


def margin_places():
    places = np.zeros((TAPS, 2, LAT, 2, LAT, PITCH), np.float32)
    for b in range(TAPS):
        for side, first in ((0, -2), (1, LON_DEV)):
            for h in range(2):
                j = first + h - b + 2
                if 0 <= j < LON_DEV:
                    for i in range(LAT):
                        places[b, side, i, h, i, j] = 1.0
    return places.reshape(TAPS, 4 * LAT, POINTS)


def stage_field(raw, x):
    lane = lax.broadcasted_iota(jnp.int32, (PITCH, LANES), 1)
    row = lax.broadcasted_iota(jnp.int32, (PITCH, LANES), 0)
    tail = jnp.where((lane == CIN - 640) & (row < LON_DEV), 1.0, 0.0).astype(jnp.bfloat16)
    zeros = jnp.zeros((16, COLS), jnp.bfloat16)

    def one(i, _):
        base = pl.multiple_of(i * PITCH, 16)
        x[pl.ds(base + 32, 16), :] = zeros
        x[pl.ds(base, PITCH), 640:COLS] = tail
        x[pl.ds(base, LON_DEV), 0:CIN] = raw[i]
        return 0

    lax.fori_loop(0, LAT + 4, one, 0)


def stage_columns(bias, widths, tile, vectors):
    tile[...] = jnp.ones((8, LANES), jnp.float32)
    tile[0:1, 0:COUT] = bias[...]
    tile[1:2, 0:COUT] = widths[...]
    vectors[:, 0:8] = jnp.transpose(tile[...])[0:CHAN, :]


def stage_target(observed, wide, target):
    spots = LON_DEV * LAT
    point = lax.broadcasted_iota(jnp.int32, (LANES, spots), 0)
    spot = lax.broadcasted_iota(jnp.int32, (LANES, spots), 1)
    second = (point >= PITCH).astype(jnp.int32)
    wanted = (point - PITCH * second) * LAT + 2 * lax.axis_index("member") + second
    chosen = ((spot == wanted) & (point < CHUNK)).astype(jnp.float32)
    wide[...] = jnp.zeros((LANES, LANES), jnp.float32)
    wide[:, 0:COUT] = jnp.dot(
        chosen, observed[...].reshape(spots, COUT),
        precision=lax.Precision.HIGHEST, preferred_element_type=jnp.float32,
    )
    target[...] = jnp.transpose(wide[...])[0:CHAN, :]


def write_gradient(packed, grad_out):
    spots = LON_DEV * LAT
    spot = lax.broadcasted_iota(jnp.int32, (spots, POINTS), 0)
    point = lax.broadcasted_iota(jnp.int32, (spots, POINTS), 1)
    wanted = (spot & (LAT - 1)) * PITCH + (spot >> 4)
    moves = jnp.where(point == wanted, 1.0, 0.0).astype(jnp.bfloat16)
    moved_grad = lax.dot_general(moves, packed[...], NT, preferred_element_type=jnp.float32)
    grad_out[...] = moved_grad.astype(jnp.bfloat16).reshape(LON_DEV, LAT, CHAN)[:, :, :COUT]


def stage_weight(w, staged):
    zeros = jnp.zeros((16, COLS), jnp.bfloat16)
    tail = jnp.zeros((64, COLS - 640), jnp.bfloat16)

    def one(a, _):
        for b in range(TAPS):
            base = pl.multiple_of(a * TAP_ROWS + b * CHAN, 16)
            staged[pl.ds(base + 64, 16), :] = zeros
            staged[pl.ds(base, 64), 640:COLS] = tail
            staged[pl.ds(base, COUT), 0:CIN] = w[a, b]
        return 0

    lax.fori_loop(0, TAPS, one, 0)


def forward_own(x, staged, taps):
    for n in range(3):
        lanes = slice(n * 256, n * 256 + 256)

        def one(a, total, n=n):
            rows = pl.ds(pl.multiple_of(a * PITCH + n * 256, 16), 256)
            left = staged[pl.ds(pl.multiple_of(a * TAP_ROWS, 16), TAP_ROWS), :]
            return total + lax.dot_general(left, x[rows, :], NT, preferred_element_type=jnp.float32)

        taps[:, lanes] = lax.fori_loop(0, TAPS, one, jnp.zeros((TAP_ROWS, 256), jnp.float32))


def stage_margin(halo, margin):
    left = halo[0].astype(jnp.float32)
    right = halo[1].astype(jnp.float32)
    for a in range(TAPS):
        margin[a, 0:32, :] = left[2 * a : 2 * a + 32, :].astype(jnp.bfloat16)
        margin[a, 32:64, :] = right[2 * a : 2 * a + 32, :].astype(jnp.bfloat16)


def forward_margin(margin, staged, edge_taps):
    def one(a, total):
        left = staged[pl.ds(pl.multiple_of(a * TAP_ROWS, 16), TAP_ROWS), :]
        return total + lax.dot_general(left, margin[a], NT, preferred_element_type=jnp.float32)

    edge_taps[...] = lax.fori_loop(0, TAPS, one, jnp.zeros((TAP_ROWS, 64), jnp.float32))


def convolved(taps, edge_taps, places, bias):
    total = jnp.broadcast_to(bias, (CHAN, POINTS))
    for b in range(TAPS):
        rows = slice(b * CHAN, b * CHAN + CHAN)
        part = taps[rows, :]
        total = total + (part if b == 2 else pltpu.roll(part, (2 - b) % POINTS, 1))
        if b != 2:
            total = total + jnp.dot(
                edge_taps[rows, :], places[b].astype(jnp.float32),
                precision=lax.Precision.HIGHEST, preferred_element_type=jnp.float32,
            )
    return total


def kernel_terms(values, target, vectors, gradients, score):
    lane = lax.broadcasted_iota(jnp.int32, (16, LANES), 1)
    real = (lane < LON_DEV) | ((lane >= PITCH) & (lane < PITCH + LON_DEV))

    def block(t, score_sum):
        rows = pl.ds(pl.multiple_of(t * 16, 16), 16)
        members = [values[m, rows, :].astype(jnp.float32) for m in range(MEMBERS)]
        width = vectors[rows, :][:, 1:2]
        inverse = jnp.broadcast_to(1.0 / (width * width), (16, LANES))
        half = -0.5 * inverse
        goal = target[rows, :]
        pulls = [jnp.zeros((16, LANES), jnp.float32) for _ in range(MEMBERS)]
        pair_sum = jnp.zeros((16, LANES), jnp.float32)
        for m in range(MEMBERS):
            for n in range(m + 1, MEMBERS):
                spread = members[m] - members[n]
                kernel_pair = jnp.exp(spread * spread * half)
                pair_sum = pair_sum + kernel_pair
                pull = kernel_pair * spread
                pulls[m] = pulls[m] + pull
                pulls[n] = pulls[n] - pull
        obs_sum = jnp.zeros((16, LANES), jnp.float32)
        for m in range(MEMBERS):
            misfit = members[m] - goal
            kernel_obs = jnp.exp(misfit * misfit * half)
            obs_sum = obs_sum + kernel_obs
            gradient = inverse * (misfit * kernel_obs - pulls[m] * (1.0 / MEMBERS))
            gradients[m, rows, :] = jnp.where(real, gradient, 0.0).astype(jnp.bfloat16)
        per_channel = (MEMBERS + 2.0 * pair_sum) * (1.0 / (2 * MEMBERS * MEMBERS)) - obs_sum * (1.0 / MEMBERS)
        channel = t * 16 + lax.broadcasted_iota(jnp.int32, (16, LANES), 0)
        return score_sum + jnp.where(channel < COUT, per_channel, 0.0)

    total = lax.fori_loop(0, CHAN // 16, block, jnp.zeros((16, LANES), jnp.float32))
    score[...] = jnp.broadcast_to(jnp.sum(total, axis=0, keepdims=True) * (1.0 / COUT), (8, LANES))


def stack_gradient(gathered, packed_grad, stacked, edge_stacked, places):
    grad = jnp.concatenate(
        [gathered[q].astype(jnp.float32)[:, :CHUNK] for q in range(MEMBERS)], axis=1
    )
    packed = grad.astype(jnp.bfloat16)
    packed_grad[...] = packed
    for b in range(TAPS):
        rows = slice(b * CHAN, b * CHAN + CHAN)
        if b == 2:
            stacked[rows, :] = packed
            edge_stacked[rows, :] = jnp.zeros((CHAN, 64), jnp.bfloat16)
        else:
            stacked[rows, :] = pltpu.roll(grad, (b - 2) % POINTS, 1).astype(jnp.bfloat16)
            edge = lax.dot_general(packed, places[b], NT, preferred_element_type=jnp.float32)
            edge_stacked[rows, :] = edge.astype(jnp.bfloat16)


def product(a, lanes, x, margin, stacked, edge_stacked):
    right = x[pl.ds(pl.multiple_of(a * PITCH, 16), POINTS), lanes]
    total = jnp.dot(stacked[...], right, preferred_element_type=jnp.float32)
    return total + jnp.dot(edge_stacked[...], margin[a, :, lanes], preferred_element_type=jnp.float32)


def shared_terms(x, margin, stacked, edge_stacked, fifth, fifth_sent, tails):
    def one(a, _):
        total = product(a, slice(512, 768), x, margin, stacked, edge_stacked)
        rows = pl.ds(pl.multiple_of(a * TAP_ROWS, 16), TAP_ROWS)
        fifth[rows, :] = total[:, :LANES]
        fifth_sent[rows, :] = total[:, :LANES].astype(jnp.bfloat16)
        tails[a, :, 0:TAP_ROWS] = jnp.transpose(total[:, LANES:])[0:8, :]
        return 0

    tails[...] = jnp.zeros((TAPS, 8, 512), jnp.float32)
    lax.fori_loop(0, TAPS, one, 0)
    spare = ROWS - TAPS * TAP_ROWS
    fifth[TAPS * TAP_ROWS : ROWS, :] = jnp.zeros((spare, LANES), jnp.float32)
    for n in range(TAPS + 1):
        a, channel = (n, 0) if n < TAPS else (2, 1)
        for q in range(4):
            row = TAPS * TAP_ROWS + 4 * n + q
            fifth[row : row + 1, :] = tails[a, channel : channel + 1, q * LANES : (q + 1) * LANES]
    fifth_sent[TAPS * TAP_ROWS : ROWS, :] = fifth[TAPS * TAP_ROWS : ROWS, :].astype(jnp.bfloat16)


def weight_terms(half, x, margin, stacked, edge_stacked, into):
    lanes = pl.ds(pl.multiple_of(half * 256, 256), 256)

    def one(a, _):
        total = product(a, lanes, x, margin, stacked, edge_stacked).astype(into.dtype)
        rows = pl.ds(pl.multiple_of(a * TAP_ROWS, 16), TAP_ROWS)
        for k in range(2):
            into[k, rows, :] = total[:, k * LANES : (k + 1) * LANES]
        return 0

    lax.fori_loop(0, TAPS, one, 0)
    first = TAPS * TAP_ROWS
    for k in range(2):
        into[k, first:ROWS, :] = jnp.zeros((ROWS - first, LANES), into.dtype)


def own_scores(starts, score_rx, owned):
    lane = lax.broadcasted_iota(jnp.int32, (8, LANES), 1)
    row = lax.broadcasted_iota(jnp.int32, (8, LANES), 0)
    me = lax.axis_index("member")
    first, count = starts[me], starts[me + 1] - starts[me]
    wanted = jnp.where(row < count, first + row, -1)
    total = jnp.zeros((8, LANES), jnp.float32)
    for q in range(MEMBERS):
        pair = score_rx[q]
        low = jnp.where(lane < LON_DEV, pair, 0.0)
        high = jnp.where(lane < LON_DEV, pltpu.roll(pair, LANES - PITCH, 1), 0.0)
        total = total + jnp.where(wanted == 2 * q, low, 0.0) + jnp.where(wanted == 2 * q + 1, high, 0.0)
    owned[...] = jnp.concatenate([total[s : s + 1, 0:LON_DEV] for s in range(CAP)], axis=1)


def whole_kernel(
    raw_hbm, w_hbm, observed_hbm, places_hbm, picks_hbm, bias, widths, starts, out, grad_out, owned, *scratch
):
    raw, w, observed, places, picks, x, tile, wide, vectors, target, packed, local = scratch[:12]
    scratch = scratch[12:]
    (
        staged, edges, halo, margin, taps, edge_taps, to_score, values, gradients, gathered, score, score_rx,
        stacked, edge_stacked, theirs, mine, fifth, fifth_sent, tails, near_send, near_recv,
    ) = scratch[:21]
    core_rx, rest = scratch[21:24], scratch[24:]
    cur = [rest[3 * k : 3 * k + 3] for k in range(PARTS)]
    rxs = [rest[8 + 3 * k : 11 + 3 * k] for k in range(PARTS)]
    shared, send_sems, recv_sems, mid_recv, far_recv = rest[16:21]
    at = position()
    member, lon = lax.axis_index("member"), lax.axis_index("lon")
    ahead = (member, lax.rem(lon + 1, GROUPS))
    behind = (member, lax.rem(lon + GROUPS - 1, GROUPS))
    others = [lax.rem(member + delta, MEMBERS) for delta in range(1, MEMBERS)]

    loads = [
        pltpu.make_async_copy(source, target_ref, local.at[n])
        for n, (source, target_ref) in enumerate(
            ((raw_hbm, raw), (picks_hbm, picks), (w_hbm, w), (places_hbm, places), (observed_hbm, observed))
        )
    ]
    for load in loads:
        load.start()
    barrier, count = greet(at)
    stage_columns(bias, widths, tile, vectors)
    loads[0].wait()
    stage_field(raw, x)
    loads[1].wait()
    edge = jnp.dot(picks[...], x[...], preferred_element_type=jnp.float32).astype(jnp.bfloat16)
    edges[0] = edge[:PITCH]
    edges[1] = edge[PITCH:]
    loads[2].wait()
    stage_weight(w, staged)
    pl.semaphore_wait(barrier, count)
    send_to(edges.at[0], halo.at[0], near_send.at[0], near_recv.at[0], ahead)
    send_to(edges.at[1], halo.at[1], near_send.at[1], near_recv.at[1], behind)
    forward_own(x, staged, taps)
    loads[3].wait()
    loads[4].wait()
    stage_target(observed, wide, target)
    finish(halo.at[0], near_send.at[0], near_recv.at[0], at).wait()
    finish(halo.at[1], near_send.at[1], near_recv.at[1], at).wait()
    stage_margin(halo, margin)
    forward_margin(margin, staged, edge_taps)
    outputs = convolved(taps, edge_taps, places, vectors[...][:, 0:1])
    for q in range(MEMBERS):
        to_score[q, :, 0:CHUNK] = outputs[:, q * CHUNK : (q + 1) * CHUNK].astype(jnp.bfloat16)
        to_score[q, :, CHUNK:LANES] = jnp.zeros((CHAN, LANES - CHUNK), jnp.bfloat16)
    for there in others:
        send_to(to_score.at[there], values.at[member], near_send.at[2], near_recv.at[2], (there, lon))
    values[member] = to_score[member]
    finish(values.at[0:7], near_send.at[2], near_recv.at[2], at).wait_recv()
    kernel_terms(values, target, vectors, gradients, score)
    for there in others:
        send_to(gradients.at[there], gathered.at[member], near_send.at[3], near_recv.at[3], (there, lon))
    for there in others:
        send_to(score, score_rx.at[member], near_send.at[4], near_recv.at[4], (there, lon))
    gathered[member] = gradients[member]
    score_rx[member] = score[...]
    finish(gathered.at[0:7], near_send.at[3], near_recv.at[3], at).wait_recv()
    stack_gradient(gathered, packed, stacked, edge_stacked, places)
    core, partner = at["core"], moved(at, "core", 1)
    weight_terms(1 - core, x, margin, stacked, edge_stacked, theirs)
    for k in range(2):
        send(theirs.at[k], core_rx[k], send_sems.at[k, 0], recv_sems.at[k, 0], partner)
    shared_terms(x, margin, stacked, edge_stacked, fifth, fifth_sent, tails)
    source = fifth_sent.at[pl.ds(pl.multiple_of((1 - core) * 1024, 16), 1024)]
    send(source, core_rx[2], send_sems.at[2, 0], recv_sems.at[2, 0], partner)
    weight_terms(core, x, margin, stacked, edge_stacked, mine)
    for k, own in ((0, mine), (1, mine), (2, fifth)):
        add_core(at, k, own, core_rx, cur, send_sems, recv_sems)
        launch(at, k, 0, cur, rxs, send_sems, recv_sems)
    write_gradient(packed, grad_out)
    finish(score_rx.at[0:7], near_send.at[4], near_recv.at[4], at).wait_recv()
    own_scores(starts, score_rx, owned)
    all_reduce(at, out, core_rx, cur, rxs, shared, send_sems, recv_sems, mid_recv, far_recv)
    finish(values.at[0:7], near_send.at[2], near_recv.at[2], at).wait_send()
    finish(gathered.at[0:7], near_send.at[3], near_recv.at[3], at).wait_send()
    finish(score_rx.at[0:7], near_send.at[4], near_recv.at[4], at).wait_send()


def kernel_scratch():
    chunk = (MEMBERS, CHAN, LANES)
    return [
        pltpu.VMEM((LAT + 4, LON_DEV, CIN), jnp.bfloat16),
        pltpu.VMEM((TAPS, TAPS, COUT, CIN), jnp.bfloat16),
        pltpu.VMEM((LON_DEV, LAT, COUT), jnp.float32),
        pltpu.VMEM((TAPS, 4 * LAT, POINTS), jnp.bfloat16),
        pltpu.VMEM((2 * PITCH, (LAT + 4) * PITCH), jnp.bfloat16),
        pltpu.VMEM(((LAT + 4) * PITCH, COLS), jnp.bfloat16),
        pltpu.VMEM((8, LANES), jnp.float32),
        pltpu.VMEM((LANES, LANES), jnp.float32),
        pltpu.VMEM((CHAN, LANES), jnp.float32),
        pltpu.VMEM((CHAN, LANES), jnp.float32),
        pltpu.VMEM((CHAN, POINTS), jnp.bfloat16),
        pltpu.SemaphoreType.DMA((5,)),
        pltpu.VMEM((TAPS * TAP_ROWS, COLS), jnp.bfloat16),
        pltpu.VMEM((2, PITCH, COLS), jnp.bfloat16),
        pltpu.VMEM((2, PITCH, COLS), jnp.bfloat16),
        pltpu.VMEM((TAPS, 64, COLS), jnp.bfloat16),
        pltpu.VMEM((TAP_ROWS, POINTS), jnp.float32),
        pltpu.VMEM((TAP_ROWS, 64), jnp.float32),
        pltpu.VMEM(chunk, jnp.bfloat16),
        pltpu.VMEM(chunk, jnp.bfloat16),
        pltpu.VMEM(chunk, jnp.bfloat16),
        pltpu.VMEM(chunk, jnp.bfloat16),
        pltpu.VMEM((8, LANES), jnp.float32),
        pltpu.VMEM((MEMBERS, 8, LANES), jnp.float32),
        pltpu.VMEM((TAP_ROWS, POINTS), jnp.bfloat16),
        pltpu.VMEM((TAP_ROWS, 64), jnp.bfloat16),
        pltpu.VMEM((2, ROWS, LANES), jnp.bfloat16),
        pltpu.VMEM((2, ROWS, LANES), jnp.float32),
        pltpu.VMEM((ROWS, LANES), jnp.float32),
        pltpu.VMEM((ROWS, LANES), jnp.bfloat16),
        pltpu.VMEM((TAPS, 8, 512), jnp.float32),
        pltpu.SemaphoreType.DMA((5,)),
        pltpu.SemaphoreType.DMA((5,)),
    ] + reduce_scratch()


def finish_kernel(main, low, high, weight_grad, bias_grad):
    factor = 1.0 / math.sqrt(MEMBERS * LAT * LON_DEV * GROUPS)
    a = pl.program_id(0)
    more = jnp.concatenate([low[...].astype(jnp.float32), high[...].astype(jnp.float32)], axis=0) * factor
    number = lax.broadcasted_iota(jnp.int32, (32, LANES), 0)
    pieces = [
        jnp.sum(jnp.where(number == 4 * a + q, more, 0.0), axis=0, keepdims=True) for q in range(4)
    ]
    last = jnp.transpose(jnp.broadcast_to(jnp.concatenate(pieces, axis=1), (8, 512)))
    for b in range(TAPS):
        weight_grad[0, b, :, 0:WIDE] = (
            main[b * CHAN : (b + 1) * CHAN, :].astype(jnp.float32)[:COUT, :] * factor
        )
        weight_grad[0, b, :, WIDE:CIN] = last[b * CHAN : b * CHAN + COUT, 0:1]
    bias = jnp.concatenate([more[4 * TAPS + q : 4 * TAPS + q + 1, :] for q in range(4)], axis=1)
    bias_grad[...] = bias[:, 2 * CHAN : 2 * CHAN + COUT]


def body(fields, weight, out_bias, observed, widths, owner_start):
    vmem = pl.BlockSpec(memory_space=pltpu.VMEM)
    hbm = pl.BlockSpec(memory_space=pl.ANY)
    summed, grad, owned = pl.pallas_call(
        whole_kernel,
        out_shape=[
            jax.ShapeDtypeStruct((ROWS, WIDE), jnp.bfloat16),
            jax.ShapeDtypeStruct((LON_DEV, LAT, COUT), jnp.bfloat16),
            jax.ShapeDtypeStruct((1, CAP * LON_DEV), jnp.float32),
        ],
        in_specs=[hbm] * 5 + [vmem] * 2 + [pl.BlockSpec(memory_space=pltpu.SMEM)],
        out_specs=[vmem] * 3,
        scratch_shapes=kernel_scratch(),
        compiler_params=pltpu.CompilerParams(
            collective_id=1, has_side_effects=True, vmem_limit_bytes=56 * 1024 * 1024
        ),
        cost_estimate=pl.CostEstimate(flops=6 << 30, bytes_accessed=16 << 20, transcendentals=1 << 20),
    )(
        jnp.transpose(fields[0], (1, 2, 0)), weight, jnp.transpose(observed, (2, 1, 0)),
        jnp.asarray(margin_places(), jnp.bfloat16), jnp.asarray(edge_picks(), jnp.bfloat16),
        out_bias.reshape(1, COUT), widths.reshape(1, COUT), owner_start[0],
    )
    weight_grad, bias_grad = pl.pallas_call(
        finish_kernel,
        grid=(TAPS,),
        out_shape=[
            jax.ShapeDtypeStruct((TAPS, TAPS, COUT, CIN), jnp.float32),
            jax.ShapeDtypeStruct((1, COUT), jnp.float32),
        ],
        in_specs=[
            pl.BlockSpec((TAP_ROWS, WIDE), lambda a: (a, 0)),
            pl.BlockSpec((16, LANES), lambda a: (TAPS * TAP_ROWS // 16, 4)),
            pl.BlockSpec((16, LANES), lambda a: (TAPS * TAP_ROWS // 16 + 1, 4)),
        ],
        out_specs=[
            pl.BlockSpec((1, TAPS, COUT, CIN), lambda a: (a, 0, 0, 0)),
            pl.BlockSpec((1, COUT), lambda a: (0, 0)),
        ],
        compiler_params=pltpu.CompilerParams(vmem_limit_bytes=58 * 1024 * 1024),
    )(summed, summed, summed)
    bias_grad = bias_grad.reshape(COUT)
    out_grad = jnp.transpose(grad, (2, 1, 0))[None]
    owned_score = owned.reshape(1, 1, CAP * LON_DEV)
    return (out_grad, owned_score, weight_grad, bias_grad)


def solution(mesh):
    in_specs = (P("member", None, None, "lon"), P(), P(), P(None, None, "lon"), P(), P("lon", None))
    out_specs = (P("member", None, None, "lon"), P("lon", "member", None), P(), P())
    return jax.shard_map(body, mesh=mesh, in_specs=in_specs, out_specs=out_specs, check_vma=False)
```

```python
import math

import jax
import jax.numpy as jnp
import numpy as np
from jax import lax
from jax.experimental import pallas as pl
from jax.experimental.pallas import tpu as pltpu
from jax.sharding import PartitionSpec as P

MESH = pl.DeviceIdType.MESH
MEMBERS = 8
GROUPS = 32
TAPS = 5
CIN = 641
COUT = 73
CHAN = 80
LAT = 16
LON_DEV = 45
PITCH = 48
POINTS = LAT * PITCH
CHUNK = 2 * PITCH
CAP = 6
TAP_ROWS = TAPS * CHAN
NT = (((1,), (1,)), ((), ()))
ROWS = 2048
LANES = 128
PARTS = 3
COLS = 768
WIDE = 640
PART_ROWS = (2048, 2048, 1024)
ORDERS = (("x", "y", "z"), ("y", "x", "z"), ("z", "x", "y"))


def position():
    member = lax.axis_index("member")
    lon = lax.axis_index("lon")
    return {
        "x": (lon // 16) * 2 + member % 2,
        "y": member // 2,
        "z": (lon // 2) % 8,
        "core": lon % 2,
    }


EXTENT = {"x": 4, "y": 4, "z": 8, "core": 2}


def device(at):
    return (at["y"] * 2 + at["x"] % 2, (at["x"] // 2) * 16 + at["z"] * 2 + at["core"])


def moved(at, axis, delta):
    there = dict(at)
    there[axis] = lax.rem(at[axis] + delta, EXTENT[axis])
    return there


def send(src, dst, send_sem, recv_sem, at):
    copy = pltpu.make_async_remote_copy(
        src_ref=src, dst_ref=dst, send_sem=send_sem, recv_sem=recv_sem,
        device_id=device(at), device_id_type=MESH,
    )
    copy.start()


def send_to(src, dst, send_sem, recv_sem, there):
    copy = pltpu.make_async_remote_copy(
        src_ref=src, dst_ref=dst, send_sem=send_sem, recv_sem=recv_sem,
        device_id=there, device_id_type=MESH,
    )
    copy.start()


def finish(ref, send_sem, recv_sem, at):
    copy = pltpu.make_async_remote_copy(
        src_ref=ref, dst_ref=ref, send_sem=send_sem, recv_sem=recv_sem,
        device_id=device(at), device_id_type=MESH,
    )
    return copy


def greet(at):
    barrier = pltpu.get_barrier_semaphore()
    count = 0
    for axis in ("core", "x", "y", "z"):
        for delta in range(1, EXTENT[axis]):
            pl.semaphore_signal(
                barrier, inc=1, device_id=device(moved(at, axis, delta)), device_id_type=MESH
            )
            count += 1
    member, lon = lax.axis_index("member"), lax.axis_index("lon")
    for delta in range(1, MEMBERS):
        there = (lax.rem(member + delta, MEMBERS), lon)
        pl.semaphore_signal(barrier, inc=1, device_id=there, device_id_type=MESH)
        count += 1
    for delta in (1, GROUPS - 1):
        there = (member, lax.rem(lon + delta, GROUPS))
        pl.semaphore_signal(barrier, inc=1, device_id=there, device_id_type=MESH)
        count += 1
    return barrier, count


def stage_rows(k):
    rows, sizes = PART_ROWS[k], []
    for axis in ORDERS[k][: 2 if k == 2 else 3]:
        rows //= EXTENT[axis]
        sizes.append(rows)
    return sizes


SIZES = [stage_rows(k) for k in range(PARTS)]


def place(at, out, k, row, rows):
    if k == 2:
        return out.at[4, pl.ds(pl.multiple_of(at["core"] * 1024 + row, 16), rows), :]
    return out.at[2 * at["core"] + k, pl.ds(pl.multiple_of(row, 16), rows), :]


def launch(at, k, s, cur, rxs, send_sems, recv_sems):
    axis, rows = ORDERS[k][s], SIZES[k][s]
    for delta in range(1, EXTENT[axis]):
        there = moved(at, axis, delta)
        source = cur[k][s].at[pl.ds(pl.multiple_of(there[axis] * rows, 16), rows)]
        send(source, rxs[k][s].at[delta - 1], send_sems.at[k, s + 1], recv_sems.at[k, s + 1], there)


def add_core(at, k, mine, core_rx, cur, send_sems, recv_sems):
    finish(core_rx[k], send_sems.at[k, 0], recv_sems.at[k, 0], at).wait_recv()
    step = 256

    def add(i, _):
        here = pl.ds(pl.multiple_of(i * step, step), step)
        if k == 2:
            own = mine[pl.ds(pl.multiple_of(at["core"] * 1024 + i * step, step), step), :]
        else:
            own = mine[k, here, :]
        cur[k][0][here, :] = (own + core_rx[k][here, :].astype(jnp.float32)).astype(jnp.bfloat16)
        return 0

    lax.fori_loop(0, PART_ROWS[k] // step, add, 0)


def gather(at, out, k, s, row, send_sems, recv_sems):
    axis = ORDERS[k][s]
    block = place(at, out, k, row, SIZES[k][s])
    for delta in range(1, EXTENT[axis]):
        send(block, block, send_sems.at[k, 4 + s], recv_sems.at[k, 4 + s], moved(at, axis, delta))


def spread(at, out, k, dy, dx, send_sem, recv_sem, there):
    first, second = ORDERS[k][0], ORDERS[k][1]
    row = lax.rem(at[first] + 4 - dx, 4) * SIZES[k][0] + lax.rem(at[second] + 4 - dy, 4) * SIZES[k][1]
    block = place(at, out, k, row, SIZES[k][1])
    if there is None:
        finish(block, send_sem, recv_sem, at).wait_recv()
    else:
        send(block, block, send_sem, recv_sem, there)


def all_reduce(at, out, core_rx, cur, rxs, shared, send_sems, recv_sems, mid_recv, far_recv):
    row = [0] * PARTS
    partner = moved(at, "core", 1)
    for s in range(3):
        for k in (2, 0, 1):
            if k == 2 and s == 2:
                finish(shared.at[0:3], send_sems.at[k, 3], recv_sems.at[k, 3], at).wait_recv()
                total = shared[0].astype(jnp.float32)
                for y in range(1, 4):
                    total = total + shared[y].astype(jnp.float32)
                place(at, out, k, row[k], 32)[...] = total.astype(jnp.bfloat16)
                gather(at, out, k, 1, row[k], send_sems, recv_sems)
                continue
            axis, rows = ORDERS[k][s], SIZES[k][s]
            finish(rxs[k][s], send_sems.at[k, s + 1], recv_sems.at[k, s + 1], at).wait_recv()
            row[k] = row[k] + at[axis] * rows
            base = pl.multiple_of(at[axis] * rows, 16)
            step = min(rows, 128)

            def add(i, _, k=k, s=s, axis=axis, base=base, step=step):
                total = cur[k][s][pl.ds(pl.multiple_of(base + i * step, 16), step), :].astype(jnp.float32)
                here = pl.ds(pl.multiple_of(i * step, 16), step)
                for slot in range(EXTENT[axis] - 1):
                    total = total + rxs[k][s][slot, here, :].astype(jnp.float32)
                total = total.astype(jnp.bfloat16)
                if k == 2 and s == 1:
                    shared[at["y"]] = total
                elif s == 2:
                    place(at, out, k, row[k], step)[...] = total
                else:
                    cur[k][s + 1][here, :] = total
                return 0

            if rows == step:
                add(0, 0)
            else:
                lax.fori_loop(0, rows // step, add, 0)
            if k == 2 and s == 1:
                for delta in range(1, 4):
                    own = shared.at[at["y"]]
                    send(own, own, send_sems.at[k, 3], recv_sems.at[k, 3], moved(at, "y", delta))
            elif s == 2:
                gather(at, out, k, 2, row[k], send_sems, recv_sems)
            else:
                launch(at, k, s + 1, cur, rxs, send_sems, recv_sems)
    def arrived(k, s):
        finish(rxs[k][s], send_sems.at[k, 4 + s], recv_sems.at[k, 4 + s], at).wait_recv()

    def onward(k, dy):
        first = ORDERS[k][0]
        for dx in (2, 1, 3):
            spread(at, out, k, dy, 0, send_sems.at[k, 4], far_recv.at[k, 4 * dx + dy], moved(at, first, dx))
        spread(at, out, k, dy, 0, send_sems.at[k, 7], recv_sems.at[k, 7], partner)

    for k in range(2):
        arrived(k, 2)
        for dy in (2, 1, 3):
            there = moved(at, ORDERS[k][1], dy)
            spread(at, out, k, 0, 0, send_sems.at[k, 5], mid_recv.at[k, dy], there)
        onward(k, 0)
    arrived(2, 1)
    row[2] = row[2] - at["x"] * SIZES[2][1]
    gather(at, out, 2, 0, row[2], send_sems, recv_sems)
    for dy in (1, 3, 2):
        for k in range(2):
            spread(at, out, k, dy, 0, send_sems.at[k, 5], mid_recv.at[k, dy], None)
            onward(k, dy)
    for dy in (0, 1, 3, 2):
        if dy == 2:
            arrived(2, 0)
            block = place(at, out, 2, 0, PART_ROWS[2])
            send(block, block, send_sems.at[2, 7], recv_sems.at[2, 7], partner)
        for dx in (1, 3, 2):
            for k in range(2):
                spread(at, out, k, dy, dx, send_sems.at[k, 4], far_recv.at[k, 4 * dx + dy], None)
                spread(at, out, k, dy, dx, send_sems.at[k, 7], recv_sems.at[k, 7], partner)
    for k in (2, 0, 1):
        finish(core_rx[k], send_sems.at[k, 7], recv_sems.at[k, 7], partner).wait_recv()
    for k in range(PARTS):
        finish(core_rx[k], send_sems.at[k, 0], recv_sems.at[k, 0], partner).wait_send()
        finish(core_rx[k], send_sems.at[k, 7], recv_sems.at[k, 7], partner).wait_send()
        for s in range(len(SIZES[k])):
            finish(rxs[k][s], send_sems.at[k, s + 1], recv_sems.at[k, s + 1], partner).wait_send()
            finish(rxs[k][s], send_sems.at[k, s + 4], recv_sems.at[k, s + 4], partner).wait_send()
    finish(shared.at[0:3], send_sems.at[2, 3], recv_sems.at[2, 3], partner).wait_send()


def reduce_scratch():
    shapes = [pltpu.VMEM((PART_ROWS[k], LANES), jnp.bfloat16) for k in range(PARTS)]
    for k in range(PARTS):
        rows = PART_ROWS[k]
        for size in SIZES[k]:
            shapes.append(pltpu.VMEM((rows, LANES), jnp.bfloat16))
            rows = size
    for k in range(PARTS):
        for axis, size in zip(ORDERS[k], SIZES[k]):
            shapes.append(pltpu.VMEM((EXTENT[axis] - 1, size, LANES), jnp.bfloat16))
    shapes.append(pltpu.VMEM((4, 32, LANES), jnp.bfloat16))
    shapes += [pltpu.SemaphoreType.DMA((PARTS, 8)), pltpu.SemaphoreType.DMA((PARTS, 8))]
    shapes += [pltpu.SemaphoreType.DMA((2, 4)), pltpu.SemaphoreType.DMA((2, 16))]
    return shapes


def edge_picks():
    picks = np.zeros((2, PITCH, (LAT + 4) * PITCH), np.float32)
    for side, first in ((0, LON_DEV - 2), (1, 0)):
        for i in range(LAT + 4):
            for h in range(2):
                picks[side, 2 * i + h, i * PITCH + first + h] = 1.0
    return picks.reshape(2 * PITCH, -1)


def margin_places():
    places = np.zeros((TAPS, 2, LAT, 2, LAT, PITCH), np.float32)
    for b in range(TAPS):
        for side, first in ((0, -2), (1, LON_DEV)):
            for h in range(2):
                j = first + h - b + 2
                if 0 <= j < LON_DEV:
                    for i in range(LAT):
                        places[b, side, i, h, i, j] = 1.0
    return places.reshape(TAPS, 4 * LAT, POINTS)


def stage_field(raw, x):
    lane = lax.broadcasted_iota(jnp.int32, (PITCH, LANES), 1)
    row = lax.broadcasted_iota(jnp.int32, (PITCH, LANES), 0)
    tail = jnp.where((lane == CIN - 640) & (row < LON_DEV), 1.0, 0.0).astype(jnp.bfloat16)
    zeros = jnp.zeros((16, COLS), jnp.bfloat16)

    def one(i, _):
        base = pl.multiple_of(i * PITCH, 16)
        x[pl.ds(base + 32, 16), :] = zeros
        x[pl.ds(base, PITCH), 640:COLS] = tail
        x[pl.ds(base, LON_DEV), 0:CIN] = raw[i]
        return 0

    lax.fori_loop(0, LAT + 4, one, 0)


def stage_columns(bias, widths, tile, vectors):
    tile[...] = jnp.ones((8, LANES), jnp.float32)
    tile[0:1, 0:COUT] = bias[...]
    tile[1:2, 0:COUT] = widths[...]
    vectors[:, 0:8] = jnp.transpose(tile[...])[0:CHAN, :]


def stage_target(observed, wide, target):
    spots = LON_DEV * LAT
    point = lax.broadcasted_iota(jnp.int32, (LANES, spots), 0)
    spot = lax.broadcasted_iota(jnp.int32, (LANES, spots), 1)
    second = (point >= PITCH).astype(jnp.int32)
    wanted = (point - PITCH * second) * LAT + 2 * lax.axis_index("member") + second
    chosen = ((spot == wanted) & (point < CHUNK)).astype(jnp.float32)
    wide[...] = jnp.zeros((LANES, LANES), jnp.float32)
    wide[:, 0:COUT] = jnp.dot(
        chosen, observed[...].reshape(spots, COUT),
        precision=lax.Precision.HIGHEST, preferred_element_type=jnp.float32,
    )
    target[...] = jnp.transpose(wide[...])[0:CHAN, :]


def write_gradient(packed, grad_out):
    spots = LON_DEV * LAT
    spot = lax.broadcasted_iota(jnp.int32, (spots, POINTS), 0)
    point = lax.broadcasted_iota(jnp.int32, (spots, POINTS), 1)
    wanted = (spot & (LAT - 1)) * PITCH + (spot >> 4)
    moves = jnp.where(point == wanted, 1.0, 0.0).astype(jnp.bfloat16)
    moved_grad = lax.dot_general(moves, packed[...], NT, preferred_element_type=jnp.float32)
    grad_out[...] = moved_grad.astype(jnp.bfloat16).reshape(LON_DEV, LAT, CHAN)[:, :, :COUT]


def stage_weight(w, staged):
    zeros = jnp.zeros((16, COLS), jnp.bfloat16)
    tail = jnp.zeros((64, COLS - 640), jnp.bfloat16)

    def one(a, _):
        for b in range(TAPS):
            base = pl.multiple_of(a * TAP_ROWS + b * CHAN, 16)
            staged[pl.ds(base + 64, 16), :] = zeros
            staged[pl.ds(base, 64), 640:COLS] = tail
            staged[pl.ds(base, COUT), 0:CIN] = w[a, b]
        return 0

    lax.fori_loop(0, TAPS, one, 0)


def forward_own(x, staged, taps):
    for n in range(3):
        lanes = slice(n * 256, n * 256 + 256)

        def one(a, total, n=n):
            rows = pl.ds(pl.multiple_of(a * PITCH + n * 256, 16), 256)
            left = staged[pl.ds(pl.multiple_of(a * TAP_ROWS, 16), TAP_ROWS), :]
            return total + lax.dot_general(left, x[rows, :], NT, preferred_element_type=jnp.float32)

        taps[:, lanes] = lax.fori_loop(0, TAPS, one, jnp.zeros((TAP_ROWS, 256), jnp.float32))


def stage_margin(halo, margin):
    left = halo[0].astype(jnp.float32)
    right = halo[1].astype(jnp.float32)
    for a in range(TAPS):
        margin[a, 0:32, :] = left[2 * a : 2 * a + 32, :].astype(jnp.bfloat16)
        margin[a, 32:64, :] = right[2 * a : 2 * a + 32, :].astype(jnp.bfloat16)


def forward_margin(margin, staged, edge_taps):
    def one(a, total):
        left = staged[pl.ds(pl.multiple_of(a * TAP_ROWS, 16), TAP_ROWS), :]
        return total + lax.dot_general(left, margin[a], NT, preferred_element_type=jnp.float32)

    edge_taps[...] = lax.fori_loop(0, TAPS, one, jnp.zeros((TAP_ROWS, 64), jnp.float32))


def convolved(taps, edge_taps, places, bias):
    total = jnp.broadcast_to(bias, (CHAN, POINTS))
    for b in range(TAPS):
        rows = slice(b * CHAN, b * CHAN + CHAN)
        part = taps[rows, :]
        total = total + (part if b == 2 else pltpu.roll(part, (2 - b) % POINTS, 1))
        if b != 2:
            total = total + jnp.dot(
                edge_taps[rows, :], places[b].astype(jnp.float32),
                precision=lax.Precision.HIGHEST, preferred_element_type=jnp.float32,
            )
    return total


def kernel_terms(values, target, vectors, gradients, score):
    lane = lax.broadcasted_iota(jnp.int32, (16, LANES), 1)
    real = (lane < LON_DEV) | ((lane >= PITCH) & (lane < PITCH + LON_DEV))

    def block(t, score_sum):
        rows = pl.ds(pl.multiple_of(t * 16, 16), 16)
        members = [values[m, rows, :].astype(jnp.float32) for m in range(MEMBERS)]
        width = vectors[rows, :][:, 1:2]
        inverse = jnp.broadcast_to(1.0 / (width * width), (16, LANES))
        half = -0.5 * inverse
        goal = target[rows, :]
        pulls = [jnp.zeros((16, LANES), jnp.float32) for _ in range(MEMBERS)]
        pair_sum = jnp.zeros((16, LANES), jnp.float32)
        for m in range(MEMBERS):
            for n in range(m + 1, MEMBERS):
                spread = members[m] - members[n]
                kernel_pair = jnp.exp(spread * spread * half)
                pair_sum = pair_sum + kernel_pair
                pull = kernel_pair * spread
                pulls[m] = pulls[m] + pull
                pulls[n] = pulls[n] - pull
        obs_sum = jnp.zeros((16, LANES), jnp.float32)
        for m in range(MEMBERS):
            misfit = members[m] - goal
            kernel_obs = jnp.exp(misfit * misfit * half)
            obs_sum = obs_sum + kernel_obs
            gradient = inverse * (misfit * kernel_obs - pulls[m] * (1.0 / MEMBERS))
            gradients[m, rows, :] = jnp.where(real, gradient, 0.0).astype(jnp.bfloat16)
        per_channel = (MEMBERS + 2.0 * pair_sum) * (1.0 / (2 * MEMBERS * MEMBERS)) - obs_sum * (1.0 / MEMBERS)
        channel = t * 16 + lax.broadcasted_iota(jnp.int32, (16, LANES), 0)
        return score_sum + jnp.where(channel < COUT, per_channel, 0.0)

    total = lax.fori_loop(0, CHAN // 16, block, jnp.zeros((16, LANES), jnp.float32))
    score[...] = jnp.broadcast_to(jnp.sum(total, axis=0, keepdims=True) * (1.0 / COUT), (8, LANES))


def stack_gradient(gathered, packed_grad, stacked, edge_stacked, places):
    grad = jnp.concatenate(
        [gathered[q].astype(jnp.float32)[:, :CHUNK] for q in range(MEMBERS)], axis=1
    )
    packed = grad.astype(jnp.bfloat16)
    packed_grad[...] = packed
    for b in range(TAPS):
        rows = slice(b * CHAN, b * CHAN + CHAN)
        if b == 2:
            stacked[rows, :] = packed
            edge_stacked[rows, :] = jnp.zeros((CHAN, 64), jnp.bfloat16)
        else:
            stacked[rows, :] = pltpu.roll(grad, (b - 2) % POINTS, 1).astype(jnp.bfloat16)
            edge = lax.dot_general(packed, places[b], NT, preferred_element_type=jnp.float32)
            edge_stacked[rows, :] = edge.astype(jnp.bfloat16)


def product(a, lanes, x, margin, stacked, edge_stacked):
    right = x[pl.ds(pl.multiple_of(a * PITCH, 16), POINTS), lanes]
    total = jnp.dot(stacked[...], right, preferred_element_type=jnp.float32)
    return total + jnp.dot(edge_stacked[...], margin[a, :, lanes], preferred_element_type=jnp.float32)


def shared_terms(x, margin, stacked, edge_stacked, fifth, fifth_sent, tails):
    def one(a, _):
        total = product(a, slice(512, 768), x, margin, stacked, edge_stacked)
        rows = pl.ds(pl.multiple_of(a * TAP_ROWS, 16), TAP_ROWS)
        fifth[rows, :] = total[:, :LANES]
        fifth_sent[rows, :] = total[:, :LANES].astype(jnp.bfloat16)
        tails[a, :, 0:TAP_ROWS] = jnp.transpose(total[:, LANES:])[0:8, :]
        return 0

    tails[...] = jnp.zeros((TAPS, 8, 512), jnp.float32)
    lax.fori_loop(0, TAPS, one, 0)
    spare = ROWS - TAPS * TAP_ROWS
    fifth[TAPS * TAP_ROWS : ROWS, :] = jnp.zeros((spare, LANES), jnp.float32)
    for n in range(TAPS + 1):
        a, channel = (n, 0) if n < TAPS else (2, 1)
        for q in range(4):
            row = TAPS * TAP_ROWS + 4 * n + q
            fifth[row : row + 1, :] = tails[a, channel : channel + 1, q * LANES : (q + 1) * LANES]
    fifth_sent[TAPS * TAP_ROWS : ROWS, :] = fifth[TAPS * TAP_ROWS : ROWS, :].astype(jnp.bfloat16)


def weight_terms(half, x, margin, stacked, edge_stacked, into):
    lanes = pl.ds(pl.multiple_of(half * 256, 256), 256)

    def one(a, _):
        total = product(a, lanes, x, margin, stacked, edge_stacked).astype(into.dtype)
        rows = pl.ds(pl.multiple_of(a * TAP_ROWS, 16), TAP_ROWS)
        for k in range(2):
            into[k, rows, :] = total[:, k * LANES : (k + 1) * LANES]
        return 0

    lax.fori_loop(0, TAPS, one, 0)
    first = TAPS * TAP_ROWS
    for k in range(2):
        into[k, first:ROWS, :] = jnp.zeros((ROWS - first, LANES), into.dtype)


def own_scores(starts, score_rx, owned):
    lane = lax.broadcasted_iota(jnp.int32, (8, LANES), 1)
    row = lax.broadcasted_iota(jnp.int32, (8, LANES), 0)
    me = lax.axis_index("member")
    first, count = starts[me], starts[me + 1] - starts[me]
    wanted = jnp.where(row < count, first + row, -1)
    total = jnp.zeros((8, LANES), jnp.float32)
    for q in range(MEMBERS):
        pair = score_rx[q]
        low = jnp.where(lane < LON_DEV, pair, 0.0)
        high = jnp.where(lane < LON_DEV, pltpu.roll(pair, LANES - PITCH, 1), 0.0)
        total = total + jnp.where(wanted == 2 * q, low, 0.0) + jnp.where(wanted == 2 * q + 1, high, 0.0)
    owned[...] = jnp.concatenate([total[s : s + 1, 0:LON_DEV] for s in range(CAP)], axis=1)


def whole_kernel(
    raw_hbm, w_hbm, observed_hbm, places_hbm, picks_hbm, bias, widths, starts, out, grad_out, owned, *scratch
):
    raw, w, observed, places, picks, x, tile, wide, vectors, target, packed, local = scratch[:12]
    scratch = scratch[12:]
    (
        staged, edges, halo, margin, taps, edge_taps, to_score, values, gradients, gathered, score, score_rx,
        stacked, edge_stacked, theirs, mine, fifth, fifth_sent, tails, near_send, near_recv,
    ) = scratch[:21]
    core_rx, rest = scratch[21:24], scratch[24:]
    cur = [rest[3 * k : 3 * k + 3] for k in range(PARTS)]
    rxs = [rest[8 + 3 * k : 11 + 3 * k] for k in range(PARTS)]
    shared, send_sems, recv_sems, mid_recv, far_recv = rest[16:21]
    at = position()
    member, lon = lax.axis_index("member"), lax.axis_index("lon")
    ahead = (member, lax.rem(lon + 1, GROUPS))
    behind = (member, lax.rem(lon + GROUPS - 1, GROUPS))
    others = [lax.rem(member + delta, MEMBERS) for delta in range(1, MEMBERS)]

    loads = [
        pltpu.make_async_copy(source, target_ref, local.at[n])
        for n, (source, target_ref) in enumerate(
            ((raw_hbm, raw), (picks_hbm, picks), (w_hbm, w), (places_hbm, places), (observed_hbm, observed))
        )
    ]
    for load in loads:
        load.start()
    barrier, count = greet(at)
    stage_columns(bias, widths, tile, vectors)
    loads[0].wait()
    stage_field(raw, x)
    loads[1].wait()
    edge = jnp.dot(picks[...], x[...], preferred_element_type=jnp.float32).astype(jnp.bfloat16)
    edges[0] = edge[:PITCH]
    edges[1] = edge[PITCH:]
    loads[2].wait()
    stage_weight(w, staged)
    pl.semaphore_wait(barrier, count)
    send_to(edges.at[0], halo.at[0], near_send.at[0], near_recv.at[0], ahead)
    send_to(edges.at[1], halo.at[1], near_send.at[1], near_recv.at[1], behind)
    forward_own(x, staged, taps)
    loads[3].wait()
    loads[4].wait()
    stage_target(observed, wide, target)
    finish(halo.at[0], near_send.at[0], near_recv.at[0], at).wait()
    finish(halo.at[1], near_send.at[1], near_recv.at[1], at).wait()
    stage_margin(halo, margin)
    forward_margin(margin, staged, edge_taps)
    outputs = convolved(taps, edge_taps, places, vectors[...][:, 0:1])
    for q in range(MEMBERS):
        to_score[q, :, 0:CHUNK] = outputs[:, q * CHUNK : (q + 1) * CHUNK].astype(jnp.bfloat16)
        to_score[q, :, CHUNK:LANES] = jnp.zeros((CHAN, LANES - CHUNK), jnp.bfloat16)
    for there in others:
        send_to(to_score.at[there], values.at[member], near_send.at[2], near_recv.at[2], (there, lon))
    values[member] = to_score[member]
    finish(values.at[0:7], near_send.at[2], near_recv.at[2], at).wait_recv()
    kernel_terms(values, target, vectors, gradients, score)
    for there in others:
        send_to(gradients.at[there], gathered.at[member], near_send.at[3], near_recv.at[3], (there, lon))
    for there in others:
        send_to(score, score_rx.at[member], near_send.at[4], near_recv.at[4], (there, lon))
    gathered[member] = gradients[member]
    score_rx[member] = score[...]
    finish(gathered.at[0:7], near_send.at[3], near_recv.at[3], at).wait_recv()
    stack_gradient(gathered, packed, stacked, edge_stacked, places)
    core, partner = at["core"], moved(at, "core", 1)
    weight_terms(1 - core, x, margin, stacked, edge_stacked, theirs)
    for k in range(2):
        send(theirs.at[k], core_rx[k], send_sems.at[k, 0], recv_sems.at[k, 0], partner)
    shared_terms(x, margin, stacked, edge_stacked, fifth, fifth_sent, tails)
    source = fifth_sent.at[pl.ds(pl.multiple_of((1 - core) * 1024, 16), 1024)]
    send(source, core_rx[2], send_sems.at[2, 0], recv_sems.at[2, 0], partner)
    weight_terms(core, x, margin, stacked, edge_stacked, mine)
    for k, own in ((0, mine), (1, mine), (2, fifth)):
        add_core(at, k, own, core_rx, cur, send_sems, recv_sems)
        launch(at, k, 0, cur, rxs, send_sems, recv_sems)
    write_gradient(packed, grad_out)
    finish(score_rx.at[0:7], near_send.at[4], near_recv.at[4], at).wait_recv()
    own_scores(starts, score_rx, owned)
    all_reduce(at, out, core_rx, cur, rxs, shared, send_sems, recv_sems, mid_recv, far_recv)
    finish(values.at[0:7], near_send.at[2], near_recv.at[2], at).wait_send()
    finish(gathered.at[0:7], near_send.at[3], near_recv.at[3], at).wait_send()
    finish(score_rx.at[0:7], near_send.at[4], near_recv.at[4], at).wait_send()


def kernel_scratch():
    chunk = (MEMBERS, CHAN, LANES)
    return [
        pltpu.VMEM((LAT + 4, LON_DEV, CIN), jnp.bfloat16),
        pltpu.VMEM((TAPS, TAPS, COUT, CIN), jnp.bfloat16),
        pltpu.VMEM((LON_DEV, LAT, COUT), jnp.float32),
        pltpu.VMEM((TAPS, 4 * LAT, POINTS), jnp.bfloat16),
        pltpu.VMEM((2 * PITCH, (LAT + 4) * PITCH), jnp.bfloat16),
        pltpu.VMEM(((LAT + 4) * PITCH, COLS), jnp.bfloat16),
        pltpu.VMEM((8, LANES), jnp.float32),
        pltpu.VMEM((LANES, LANES), jnp.float32),
        pltpu.VMEM((CHAN, LANES), jnp.float32),
        pltpu.VMEM((CHAN, LANES), jnp.float32),
        pltpu.VMEM((CHAN, POINTS), jnp.bfloat16),
        pltpu.SemaphoreType.DMA((5,)),
        pltpu.VMEM((TAPS * TAP_ROWS, COLS), jnp.bfloat16),
        pltpu.VMEM((2, PITCH, COLS), jnp.bfloat16),
        pltpu.VMEM((2, PITCH, COLS), jnp.bfloat16),
        pltpu.VMEM((TAPS, 64, COLS), jnp.bfloat16),
        pltpu.VMEM((TAP_ROWS, POINTS), jnp.float32),
        pltpu.VMEM((TAP_ROWS, 64), jnp.float32),
        pltpu.VMEM(chunk, jnp.bfloat16),
        pltpu.VMEM(chunk, jnp.bfloat16),
        pltpu.VMEM(chunk, jnp.bfloat16),
        pltpu.VMEM(chunk, jnp.bfloat16),
        pltpu.VMEM((8, LANES), jnp.float32),
        pltpu.VMEM((MEMBERS, 8, LANES), jnp.float32),
        pltpu.VMEM((TAP_ROWS, POINTS), jnp.bfloat16),
        pltpu.VMEM((TAP_ROWS, 64), jnp.bfloat16),
        pltpu.VMEM((2, ROWS, LANES), jnp.bfloat16),
        pltpu.VMEM((2, ROWS, LANES), jnp.float32),
        pltpu.VMEM((ROWS, LANES), jnp.float32),
        pltpu.VMEM((ROWS, LANES), jnp.bfloat16),
        pltpu.VMEM((TAPS, 8, 512), jnp.float32),
        pltpu.SemaphoreType.DMA((5,)),
        pltpu.SemaphoreType.DMA((5,)),
    ] + reduce_scratch()


def finish_kernel(
    summed, grad_in, owned_in, weight_grad, grad_out, owned_out, bias_grad, main, wide, in_sems, out_sems, pass_sems
):
    factor = 1.0 / math.sqrt(MEMBERS * LAT * LON_DEV * GROUPS)
    passed = [
        pltpu.make_async_copy(grad_in, grad_out, pass_sems.at[0]),
        pltpu.make_async_copy(owned_in, owned_out, pass_sems.at[1]),
    ]
    first = TAPS * TAP_ROWS
    tail = (TAPS - 1, slice(first, ROWS))
    loads = [pltpu.make_async_copy(summed.at[tail], main.at[tail], in_sems.at[TAPS])]
    for a in range(TAPS):
        rows = (slice(None), slice(a * TAP_ROWS, (a + 1) * TAP_ROWS))
        loads.append(pltpu.make_async_copy(summed.at[rows], main.at[rows], in_sems.at[a]))
    for copy in loads + passed:
        copy.start()
    loads[0].wait()
    more = main[TAPS - 1, first:ROWS, :].astype(jnp.float32) * factor
    bias = jnp.concatenate([more[4 * TAPS + q : 4 * TAPS + q + 1, :] for q in range(4)], axis=1)
    bias_grad[...] = bias[:, 2 * CHAN : 2 * CHAN + COUT]
    stores = []
    for a in range(TAPS):
        last = jnp.concatenate([more[4 * a + q : 4 * a + q + 1, :] for q in range(4)], axis=1)
        last = jnp.transpose(jnp.broadcast_to(last, (8, 512)))
        loads[a + 1].wait()
        for b in range(TAPS):
            base, n = a * TAP_ROWS + b * CHAN, a * TAPS + b
            for block in range(TAPS):
                part = main[block, base : base + CHAN, :].astype(jnp.float32) * factor
                wide[n, :, block * LANES : (block + 1) * LANES] = part[:COUT]
            wide[n, :, WIDE:CIN] = last[b * CHAN : b * CHAN + COUT, 0:1]
            stores.append(pltpu.make_async_copy(wide.at[n], weight_grad.at[n], out_sems.at[n]))
            stores[-1].start()
    for copy in stores + passed:
        copy.wait()


def body(fields, weight, out_bias, observed, widths, owner_start):
    vmem = pl.BlockSpec(memory_space=pltpu.VMEM)
    hbm = pl.BlockSpec(memory_space=pl.ANY)
    summed, grad, owned = pl.pallas_call(
        whole_kernel,
        out_shape=[
            jax.ShapeDtypeStruct((TAPS, ROWS, LANES), jnp.bfloat16),
            jax.ShapeDtypeStruct((LON_DEV, LAT, COUT), jnp.bfloat16),
            jax.ShapeDtypeStruct((1, CAP * LON_DEV), jnp.float32),
        ],
        in_specs=[hbm] * 5 + [vmem] * 2 + [pl.BlockSpec(memory_space=pltpu.SMEM)],
        out_specs=[vmem] * 3,
        scratch_shapes=kernel_scratch(),
        compiler_params=pltpu.CompilerParams(
            collective_id=1, has_side_effects=True, vmem_limit_bytes=56 * 1024 * 1024
        ),
        cost_estimate=pl.CostEstimate(flops=6 << 30, bytes_accessed=16 << 20, transcendentals=1 << 20),
    )(
        jnp.transpose(fields[0], (1, 2, 0)), weight, jnp.transpose(observed, (2, 1, 0)),
        jnp.asarray(margin_places(), jnp.bfloat16), jnp.asarray(edge_picks(), jnp.bfloat16),
        out_bias.reshape(1, COUT), widths.reshape(1, COUT), owner_start[0],
    )
    weight_grad, grad, owned, bias_grad = pl.pallas_call(
        finish_kernel,
        out_shape=[
            jax.ShapeDtypeStruct((TAPS * TAPS, COUT, CIN), jnp.float32),
            jax.ShapeDtypeStruct((LON_DEV, LAT, COUT), jnp.bfloat16),
            jax.ShapeDtypeStruct((1, CAP * LON_DEV), jnp.float32),
            jax.ShapeDtypeStruct((1, COUT), jnp.float32),
        ],
        in_specs=[hbm] * 3,
        out_specs=[hbm] * 3 + [vmem],
        scratch_shapes=[
            pltpu.VMEM((TAPS, ROWS, LANES), jnp.bfloat16),
            pltpu.VMEM((TAPS * TAPS, COUT, CIN), jnp.float32),
            pltpu.SemaphoreType.DMA((TAPS + 1,)),
            pltpu.SemaphoreType.DMA((TAPS * TAPS,)),
            pltpu.SemaphoreType.DMA((2,)),
        ],
        compiler_params=pltpu.CompilerParams(vmem_limit_bytes=58 * 1024 * 1024),
    )(summed, grad, owned)
    weight_grad = weight_grad.reshape(TAPS, TAPS, COUT, CIN)
    bias_grad = bias_grad.reshape(COUT)
    out_grad = jnp.transpose(grad, (2, 1, 0))[None]
    owned_score = owned.reshape(1, 1, CAP * LON_DEV)
    return (out_grad, owned_score, weight_grad, bias_grad)


def solution(mesh):
    in_specs = (P("member", None, None, "lon"), P(), P(), P(None, None, "lon"), P(), P("lon", None))
    out_specs = (P("member", None, None, "lon"), P("lon", "member", None), P(), P())
    return jax.shard_map(body, mesh=mesh, in_specs=in_specs, out_specs=out_specs, check_vma=False)
```

```python
import math

import jax
import jax.numpy as jnp
import numpy as np
from jax import lax
from jax.experimental import pallas as pl
from jax.experimental.pallas import tpu as pltpu
from jax.sharding import PartitionSpec as P

MESH = pl.DeviceIdType.MESH
MEMBERS = 8
GROUPS = 32
TAPS = 5
CIN = 641
COUT = 73
CHAN = 80
LAT = 16
LON_DEV = 45
PITCH = 48
POINTS = LAT * PITCH
CHUNK = 2 * PITCH
CAP = 6
TAP_ROWS = TAPS * CHAN
NT = (((1,), (1,)), ((), ()))
ROWS = 2048
LANES = 128
PARTS = 3
COLS = 768
WIDE = 640
PART_ROWS = (2048, 2048, 1024)
ORDERS = (("x", "y", "z"), ("y", "x", "z"), ("z", "x", "y"))


def position():
    member = lax.axis_index("member")
    lon = lax.axis_index("lon")
    return {
        "x": (lon // 16) * 2 + member % 2,
        "y": member // 2,
        "z": (lon // 2) % 8,
        "core": lon % 2,
    }


EXTENT = {"x": 4, "y": 4, "z": 8, "core": 2}


def device(at):
    return (at["y"] * 2 + at["x"] % 2, (at["x"] // 2) * 16 + at["z"] * 2 + at["core"])


def moved(at, axis, delta):
    there = dict(at)
    there[axis] = lax.rem(at[axis] + delta, EXTENT[axis])
    return there


def send(src, dst, send_sem, recv_sem, at):
    copy = pltpu.make_async_remote_copy(
        src_ref=src, dst_ref=dst, send_sem=send_sem, recv_sem=recv_sem,
        device_id=device(at), device_id_type=MESH,
    )
    copy.start()


def send_to(src, dst, send_sem, recv_sem, there):
    copy = pltpu.make_async_remote_copy(
        src_ref=src, dst_ref=dst, send_sem=send_sem, recv_sem=recv_sem,
        device_id=there, device_id_type=MESH,
    )
    copy.start()


def finish(ref, send_sem, recv_sem, at):
    copy = pltpu.make_async_remote_copy(
        src_ref=ref, dst_ref=ref, send_sem=send_sem, recv_sem=recv_sem,
        device_id=device(at), device_id_type=MESH,
    )
    return copy


def greet(at):
    barrier = pltpu.get_barrier_semaphore()
    count = 0
    for axis in ("core", "x", "y", "z"):
        for delta in range(1, EXTENT[axis]):
            pl.semaphore_signal(
                barrier, inc=1, device_id=device(moved(at, axis, delta)), device_id_type=MESH
            )
            count += 1
    member, lon = lax.axis_index("member"), lax.axis_index("lon")
    for delta in range(1, MEMBERS):
        there = (lax.rem(member + delta, MEMBERS), lon)
        pl.semaphore_signal(barrier, inc=1, device_id=there, device_id_type=MESH)
        count += 1
    for delta in (1, GROUPS - 1):
        there = (member, lax.rem(lon + delta, GROUPS))
        pl.semaphore_signal(barrier, inc=1, device_id=there, device_id_type=MESH)
        count += 1
    return barrier, count


def stage_rows(k):
    rows, sizes = PART_ROWS[k], []
    for axis in ORDERS[k][: 2 if k == 2 else 3]:
        rows //= EXTENT[axis]
        sizes.append(rows)
    return sizes


SIZES = [stage_rows(k) for k in range(PARTS)]


def place(at, out, k, row, rows):
    if k == 2:
        return out.at[pl.ds(pl.multiple_of(at["core"] * 1024 + row, 16), rows), 512:640]
    lane = pl.multiple_of((2 * at["core"] + k) * LANES, LANES)
    return out.at[pl.ds(pl.multiple_of(row, 16), rows), pl.ds(lane, LANES)]


def launch(at, k, s, cur, rxs, send_sems, recv_sems):
    axis, rows = ORDERS[k][s], SIZES[k][s]
    for delta in range(1, EXTENT[axis]):
        there = moved(at, axis, delta)
        source = cur[k][s].at[pl.ds(pl.multiple_of(there[axis] * rows, 16), rows)]
        send(source, rxs[k][s].at[delta - 1], send_sems.at[k, s + 1], recv_sems.at[k, s + 1], there)


def add_core(at, k, mine, core_rx, cur, send_sems, recv_sems):
    finish(core_rx[k], send_sems.at[k, 0], recv_sems.at[k, 0], at).wait_recv()
    step = 256

    def add(i, _):
        here = pl.ds(pl.multiple_of(i * step, step), step)
        if k == 2:
            own = mine[pl.ds(pl.multiple_of(at["core"] * 1024 + i * step, step), step), :]
        else:
            own = mine[k, here, :]
        cur[k][0][here, :] = (own + core_rx[k][here, :].astype(jnp.float32)).astype(jnp.bfloat16)
        return 0

    lax.fori_loop(0, PART_ROWS[k] // step, add, 0)


def gather(at, out, k, s, row, send_sems, recv_sems):
    axis = ORDERS[k][s]
    block = place(at, out, k, row, SIZES[k][s])
    for delta in range(1, EXTENT[axis]):
        send(block, block, send_sems.at[k, 4 + s], recv_sems.at[k, 4 + s], moved(at, axis, delta))


def spread(at, out, k, dy, dx, send_sem, recv_sem, there):
    first, second = ORDERS[k][0], ORDERS[k][1]
    row = lax.rem(at[first] + 4 - dx, 4) * SIZES[k][0] + lax.rem(at[second] + 4 - dy, 4) * SIZES[k][1]
    block = place(at, out, k, row, SIZES[k][1])
    if there is None:
        finish(block, send_sem, recv_sem, at).wait_recv()
    else:
        send(block, block, send_sem, recv_sem, there)


def all_reduce(at, out, core_rx, cur, rxs, shared, send_sems, recv_sems, mid_recv, far_recv):
    row = [0] * PARTS
    partner = moved(at, "core", 1)
    for s in range(3):
        for k in (2, 0, 1) if s == 2 else (0, 1, 2):
            if k == 2 and s == 2:
                finish(shared.at[0:3], send_sems.at[k, 3], recv_sems.at[k, 3], at).wait_recv()
                total = shared[0].astype(jnp.float32)
                for y in range(1, 4):
                    total = total + shared[y].astype(jnp.float32)
                place(at, out, k, row[k], 32)[...] = total.astype(jnp.bfloat16)
                gather(at, out, k, 1, row[k], send_sems, recv_sems)
                continue
            axis, rows = ORDERS[k][s], SIZES[k][s]
            finish(rxs[k][s], send_sems.at[k, s + 1], recv_sems.at[k, s + 1], at).wait_recv()
            row[k] = row[k] + at[axis] * rows
            base = pl.multiple_of(at[axis] * rows, 16)
            step = min(rows, 128)

            def add(i, _, k=k, s=s, axis=axis, base=base, step=step):
                total = cur[k][s][pl.ds(pl.multiple_of(base + i * step, 16), step), :].astype(jnp.float32)
                here = pl.ds(pl.multiple_of(i * step, 16), step)
                for slot in range(EXTENT[axis] - 1):
                    total = total + rxs[k][s][slot, here, :].astype(jnp.float32)
                total = total.astype(jnp.bfloat16)
                if k == 2 and s == 1:
                    shared[at["y"]] = total
                elif s == 2:
                    place(at, out, k, row[k], step)[...] = total
                else:
                    cur[k][s + 1][here, :] = total
                return 0

            if rows == step:
                add(0, 0)
            else:
                lax.fori_loop(0, rows // step, add, 0)
            if k == 2 and s == 1:
                for delta in range(1, 4):
                    own = shared.at[at["y"]]
                    send(own, own, send_sems.at[k, 3], recv_sems.at[k, 3], moved(at, "y", delta))
            elif s == 2:
                gather(at, out, k, 2, row[k], send_sems, recv_sems)
            else:
                launch(at, k, s + 1, cur, rxs, send_sems, recv_sems)
    def arrived(k, s):
        finish(rxs[k][s], send_sems.at[k, 4 + s], recv_sems.at[k, 4 + s], at).wait_recv()

    def onward(k, dy):
        first = ORDERS[k][0]
        for dx in (2, 1, 3):
            spread(at, out, k, dy, 0, send_sems.at[k, 4], far_recv.at[k, 4 * dx + dy], moved(at, first, dx))
        spread(at, out, k, dy, 0, send_sems.at[k, 7], recv_sems.at[k, 7], partner)

    arrived(2, 1)
    row[2] = row[2] - at["x"] * SIZES[2][1]
    gather(at, out, 2, 0, row[2], send_sems, recv_sems)
    for k in range(2):
        arrived(k, 2)
        for dy in (2, 1, 3):
            there = moved(at, ORDERS[k][1], dy)
            spread(at, out, k, 0, 0, send_sems.at[k, 5], mid_recv.at[k, dy], there)
        onward(k, 0)
    for dy in (1, 3, 2):
        for k in range(2):
            spread(at, out, k, dy, 0, send_sems.at[k, 5], mid_recv.at[k, dy], None)
            onward(k, dy)
    for dy in (0, 1, 3, 2):
        if dy == 2:
            arrived(2, 0)
            block = place(at, out, 2, 0, PART_ROWS[2])
            send(block, block, send_sems.at[2, 7], recv_sems.at[2, 7], partner)
        for dx in (1, 3, 2):
            for k in range(2):
                spread(at, out, k, dy, dx, send_sems.at[k, 4], far_recv.at[k, 4 * dx + dy], None)
                spread(at, out, k, dy, dx, send_sems.at[k, 7], recv_sems.at[k, 7], partner)
    for k in (2, 0, 1):
        finish(core_rx[k], send_sems.at[k, 7], recv_sems.at[k, 7], partner).wait_recv()
    for k in range(PARTS):
        finish(core_rx[k], send_sems.at[k, 0], recv_sems.at[k, 0], partner).wait_send()
        finish(core_rx[k], send_sems.at[k, 7], recv_sems.at[k, 7], partner).wait_send()
        for s in range(len(SIZES[k])):
            finish(rxs[k][s], send_sems.at[k, s + 1], recv_sems.at[k, s + 1], partner).wait_send()
            finish(rxs[k][s], send_sems.at[k, s + 4], recv_sems.at[k, s + 4], partner).wait_send()
    finish(shared.at[0:3], send_sems.at[2, 3], recv_sems.at[2, 3], partner).wait_send()


def reduce_scratch():
    shapes = [pltpu.VMEM((PART_ROWS[k], LANES), jnp.bfloat16) for k in range(PARTS)]
    for k in range(PARTS):
        rows = PART_ROWS[k]
        for size in SIZES[k]:
            shapes.append(pltpu.VMEM((rows, LANES), jnp.bfloat16))
            rows = size
    for k in range(PARTS):
        for axis, size in zip(ORDERS[k], SIZES[k]):
            shapes.append(pltpu.VMEM((EXTENT[axis] - 1, size, LANES), jnp.bfloat16))
    shapes.append(pltpu.VMEM((4, 32, LANES), jnp.bfloat16))
    shapes += [pltpu.SemaphoreType.DMA((PARTS, 8)), pltpu.SemaphoreType.DMA((PARTS, 8))]
    shapes += [pltpu.SemaphoreType.DMA((2, 4)), pltpu.SemaphoreType.DMA((2, 16))]
    return shapes


def edge_picks():
    picks = np.zeros((2, PITCH, (LAT + 4) * PITCH), np.float32)
    for side, first in ((0, LON_DEV - 2), (1, 0)):
        for i in range(LAT + 4):
            for h in range(2):
                picks[side, 2 * i + h, i * PITCH + first + h] = 1.0
    return picks.reshape(2 * PITCH, -1)


def margin_places():
    places = np.zeros((TAPS, 2, LAT, 2, LAT, PITCH), np.float32)
    for b in range(TAPS):
        for side, first in ((0, -2), (1, LON_DEV)):
            for h in range(2):
                j = first + h - b + 2
                if 0 <= j < LON_DEV:
                    for i in range(LAT):
                        places[b, side, i, h, i, j] = 1.0
    return places.reshape(TAPS, 4 * LAT, POINTS)


def stage_field(raw, x):
    lane = lax.broadcasted_iota(jnp.int32, (PITCH, LANES), 1)
    row = lax.broadcasted_iota(jnp.int32, (PITCH, LANES), 0)
    tail = jnp.where((lane == CIN - 640) & (row < LON_DEV), 1.0, 0.0).astype(jnp.bfloat16)
    zeros = jnp.zeros((16, COLS), jnp.bfloat16)

    def one(i, _):
        base = pl.multiple_of(i * PITCH, 16)
        x[pl.ds(base + 32, 16), :] = zeros
        x[pl.ds(base, PITCH), 640:COLS] = tail
        x[pl.ds(base, LON_DEV), 0:CIN] = raw[i]
        return 0

    lax.fori_loop(0, LAT + 4, one, 0)


def stage_columns(bias, widths, tile, vectors):
    tile[...] = jnp.ones((8, LANES), jnp.float32)
    tile[0:1, 0:COUT] = bias[...]
    tile[1:2, 0:COUT] = widths[...]
    vectors[:, 0:8] = jnp.transpose(tile[...])[0:CHAN, :]


def stage_target(observed, wide, target):
    spots = LON_DEV * LAT
    point = lax.broadcasted_iota(jnp.int32, (LANES, spots), 0)
    spot = lax.broadcasted_iota(jnp.int32, (LANES, spots), 1)
    second = (point >= PITCH).astype(jnp.int32)
    wanted = (point - PITCH * second) * LAT + 2 * lax.axis_index("member") + second
    chosen = ((spot == wanted) & (point < CHUNK)).astype(jnp.float32)
    wide[...] = jnp.zeros((LANES, LANES), jnp.float32)
    wide[:, 0:COUT] = jnp.dot(
        chosen, observed[...].reshape(spots, COUT),
        precision=lax.Precision.HIGHEST, preferred_element_type=jnp.float32,
    )
    target[...] = jnp.transpose(wide[...])[0:CHAN, :]


def write_gradient(packed, grad_out):
    spots = LON_DEV * LAT
    spot = lax.broadcasted_iota(jnp.int32, (spots, POINTS), 0)
    point = lax.broadcasted_iota(jnp.int32, (spots, POINTS), 1)
    wanted = (spot & (LAT - 1)) * PITCH + (spot >> 4)
    moves = jnp.where(point == wanted, 1.0, 0.0).astype(jnp.bfloat16)
    moved_grad = lax.dot_general(moves, packed[...], NT, preferred_element_type=jnp.float32)
    grad_out[...] = moved_grad.astype(jnp.bfloat16).reshape(LON_DEV, LAT, CHAN)[:, :, :COUT]


def stage_weight(w, staged):
    zeros = jnp.zeros((16, COLS), jnp.bfloat16)
    tail = jnp.zeros((64, COLS - 640), jnp.bfloat16)

    def one(a, _):
        for b in range(TAPS):
            base = pl.multiple_of(a * TAP_ROWS + b * CHAN, 16)
            staged[pl.ds(base + 64, 16), :] = zeros
            staged[pl.ds(base, 64), 640:COLS] = tail
            staged[pl.ds(base, COUT), 0:CIN] = w[a, b]
        return 0

    lax.fori_loop(0, TAPS, one, 0)


def forward_own(x, staged, taps):
    for n in range(3):
        lanes = slice(n * 256, n * 256 + 256)

        def one(a, total, n=n):
            rows = pl.ds(pl.multiple_of(a * PITCH + n * 256, 16), 256)
            left = staged[pl.ds(pl.multiple_of(a * TAP_ROWS, 16), TAP_ROWS), :]
            return total + lax.dot_general(left, x[rows, :], NT, preferred_element_type=jnp.float32)

        taps[:, lanes] = lax.fori_loop(0, TAPS, one, jnp.zeros((TAP_ROWS, 256), jnp.float32))


def stage_margin(halo, margin):
    left = halo[0].astype(jnp.float32)
    right = halo[1].astype(jnp.float32)
    for a in range(TAPS):
        margin[a, 0:32, :] = left[2 * a : 2 * a + 32, :].astype(jnp.bfloat16)
        margin[a, 32:64, :] = right[2 * a : 2 * a + 32, :].astype(jnp.bfloat16)


def forward_margin(margin, staged, edge_taps):
    def one(a, total):
        left = staged[pl.ds(pl.multiple_of(a * TAP_ROWS, 16), TAP_ROWS), :]
        return total + lax.dot_general(left, margin[a], NT, preferred_element_type=jnp.float32)

    edge_taps[...] = lax.fori_loop(0, TAPS, one, jnp.zeros((TAP_ROWS, 64), jnp.float32))


def convolved(taps, edge_taps, places, bias):
    total = jnp.broadcast_to(bias, (CHAN, POINTS))
    for b in range(TAPS):
        rows = slice(b * CHAN, b * CHAN + CHAN)
        part = taps[rows, :]
        total = total + (part if b == 2 else pltpu.roll(part, (2 - b) % POINTS, 1))
        if b != 2:
            total = total + jnp.dot(
                edge_taps[rows, :], places[b].astype(jnp.float32),
                precision=lax.Precision.HIGHEST, preferred_element_type=jnp.float32,
            )
    return total


def kernel_terms(values, target, vectors, gradients, score):
    lane = lax.broadcasted_iota(jnp.int32, (16, LANES), 1)
    real = (lane < LON_DEV) | ((lane >= PITCH) & (lane < PITCH + LON_DEV))

    def block(t, score_sum):
        rows = pl.ds(pl.multiple_of(t * 16, 16), 16)
        members = [values[m, rows, :].astype(jnp.float32) for m in range(MEMBERS)]
        width = vectors[rows, :][:, 1:2]
        inverse = jnp.broadcast_to(1.0 / (width * width), (16, LANES))
        half = -0.5 * inverse
        goal = target[rows, :]
        pulls = [jnp.zeros((16, LANES), jnp.float32) for _ in range(MEMBERS)]
        pair_sum = jnp.zeros((16, LANES), jnp.float32)
        for m in range(MEMBERS):
            for n in range(m + 1, MEMBERS):
                spread = members[m] - members[n]
                kernel_pair = jnp.exp(spread * spread * half)
                pair_sum = pair_sum + kernel_pair
                pull = kernel_pair * spread
                pulls[m] = pulls[m] + pull
                pulls[n] = pulls[n] - pull
        obs_sum = jnp.zeros((16, LANES), jnp.float32)
        for m in range(MEMBERS):
            misfit = members[m] - goal
            kernel_obs = jnp.exp(misfit * misfit * half)
            obs_sum = obs_sum + kernel_obs
            gradient = inverse * (misfit * kernel_obs - pulls[m] * (1.0 / MEMBERS))
            gradients[m, rows, :] = jnp.where(real, gradient, 0.0).astype(jnp.bfloat16)
        per_channel = (MEMBERS + 2.0 * pair_sum) * (1.0 / (2 * MEMBERS * MEMBERS)) - obs_sum * (1.0 / MEMBERS)
        channel = t * 16 + lax.broadcasted_iota(jnp.int32, (16, LANES), 0)
        return score_sum + jnp.where(channel < COUT, per_channel, 0.0)

    total = lax.fori_loop(0, CHAN // 16, block, jnp.zeros((16, LANES), jnp.float32))
    score[...] = jnp.broadcast_to(jnp.sum(total, axis=0, keepdims=True) * (1.0 / COUT), (8, LANES))


def stack_gradient(gathered, packed_grad, stacked, edge_stacked, places):
    grad = jnp.concatenate(
        [gathered[q].astype(jnp.float32)[:, :CHUNK] for q in range(MEMBERS)], axis=1
    )
    packed = grad.astype(jnp.bfloat16)
    packed_grad[...] = packed
    for b in range(TAPS):
        rows = slice(b * CHAN, b * CHAN + CHAN)
        if b == 2:
            stacked[rows, :] = packed
            edge_stacked[rows, :] = jnp.zeros((CHAN, 64), jnp.bfloat16)
        else:
            stacked[rows, :] = pltpu.roll(grad, (b - 2) % POINTS, 1).astype(jnp.bfloat16)
            edge = lax.dot_general(packed, places[b], NT, preferred_element_type=jnp.float32)
            edge_stacked[rows, :] = edge.astype(jnp.bfloat16)


def product(a, lanes, x, margin, stacked, edge_stacked):
    right = x[pl.ds(pl.multiple_of(a * PITCH, 16), POINTS), lanes]
    total = jnp.dot(stacked[...], right, preferred_element_type=jnp.float32)
    return total + jnp.dot(edge_stacked[...], margin[a, :, lanes], preferred_element_type=jnp.float32)


def shared_terms(x, margin, stacked, edge_stacked, fifth, fifth_sent, tails):
    def one(a, _):
        total = product(a, slice(512, 768), x, margin, stacked, edge_stacked)
        rows = pl.ds(pl.multiple_of(a * TAP_ROWS, 16), TAP_ROWS)
        fifth[rows, :] = total[:, :LANES]
        fifth_sent[rows, :] = total[:, :LANES].astype(jnp.bfloat16)
        tails[a, :, 0:TAP_ROWS] = jnp.transpose(total[:, LANES:])[0:8, :]
        return 0

    tails[...] = jnp.zeros((TAPS, 8, 512), jnp.float32)
    lax.fori_loop(0, TAPS, one, 0)
    spare = ROWS - TAPS * TAP_ROWS
    fifth[TAPS * TAP_ROWS : ROWS, :] = jnp.zeros((spare, LANES), jnp.float32)
    for n in range(TAPS + 1):
        a, channel = (n, 0) if n < TAPS else (2, 1)
        for q in range(4):
            row = TAPS * TAP_ROWS + 4 * n + q
            fifth[row : row + 1, :] = tails[a, channel : channel + 1, q * LANES : (q + 1) * LANES]
    fifth_sent[TAPS * TAP_ROWS : ROWS, :] = fifth[TAPS * TAP_ROWS : ROWS, :].astype(jnp.bfloat16)


def weight_terms(half, x, margin, stacked, edge_stacked, into):
    lanes = pl.ds(pl.multiple_of(half * 256, 256), 256)

    def one(a, _):
        total = product(a, lanes, x, margin, stacked, edge_stacked).astype(into.dtype)
        rows = pl.ds(pl.multiple_of(a * TAP_ROWS, 16), TAP_ROWS)
        for k in range(2):
            into[k, rows, :] = total[:, k * LANES : (k + 1) * LANES]
        return 0

    lax.fori_loop(0, TAPS, one, 0)
    first = TAPS * TAP_ROWS
    for k in range(2):
        into[k, first:ROWS, :] = jnp.zeros((ROWS - first, LANES), into.dtype)


def own_scores(starts, score_rx, owned):
    lane = lax.broadcasted_iota(jnp.int32, (8, LANES), 1)
    row = lax.broadcasted_iota(jnp.int32, (8, LANES), 0)
    me = lax.axis_index("member")
    first, count = starts[me], starts[me + 1] - starts[me]
    wanted = jnp.where(row < count, first + row, -1)
    total = jnp.zeros((8, LANES), jnp.float32)
    for q in range(MEMBERS):
        pair = score_rx[q]
        low = jnp.where(lane < LON_DEV, pair, 0.0)
        high = jnp.where(lane < LON_DEV, pltpu.roll(pair, LANES - PITCH, 1), 0.0)
        total = total + jnp.where(wanted == 2 * q, low, 0.0) + jnp.where(wanted == 2 * q + 1, high, 0.0)
    owned[...] = jnp.concatenate([total[s : s + 1, 0:LON_DEV] for s in range(CAP)], axis=1)


def whole_kernel(
    raw_hbm, w_hbm, observed_hbm, places_hbm, picks_hbm, bias, widths, starts, out, grad_out, owned, *scratch
):
    raw, w, observed, places, picks, x, tile, wide, vectors, target, packed, local = scratch[:12]
    scratch = scratch[12:]
    (
        staged, edges, halo, margin, taps, edge_taps, to_score, values, gradients, gathered, score, score_rx,
        stacked, edge_stacked, theirs, mine, fifth, fifth_sent, tails, near_send, near_recv,
    ) = scratch[:21]
    core_rx, rest = scratch[21:24], scratch[24:]
    cur = [rest[3 * k : 3 * k + 3] for k in range(PARTS)]
    rxs = [rest[8 + 3 * k : 11 + 3 * k] for k in range(PARTS)]
    shared, send_sems, recv_sems, mid_recv, far_recv = rest[16:21]
    at = position()
    member, lon = lax.axis_index("member"), lax.axis_index("lon")
    ahead = (member, lax.rem(lon + 1, GROUPS))
    behind = (member, lax.rem(lon + GROUPS - 1, GROUPS))
    others = [lax.rem(member + delta, MEMBERS) for delta in range(1, MEMBERS)]

    loads = [
        pltpu.make_async_copy(source, target_ref, local.at[n])
        for n, (source, target_ref) in enumerate(
            ((raw_hbm, raw), (picks_hbm, picks), (w_hbm, w), (places_hbm, places), (observed_hbm, observed))
        )
    ]
    for load in loads:
        load.start()
    barrier, count = greet(at)
    stage_columns(bias, widths, tile, vectors)
    loads[0].wait()
    stage_field(raw, x)
    loads[1].wait()
    edge = jnp.dot(picks[...], x[...], preferred_element_type=jnp.float32).astype(jnp.bfloat16)
    edges[0] = edge[:PITCH]
    edges[1] = edge[PITCH:]
    loads[2].wait()
    stage_weight(w, staged)
    pl.semaphore_wait(barrier, count)
    send_to(edges.at[0], halo.at[0], near_send.at[0], near_recv.at[0], ahead)
    send_to(edges.at[1], halo.at[1], near_send.at[1], near_recv.at[1], behind)
    forward_own(x, staged, taps)
    loads[3].wait()
    loads[4].wait()
    stage_target(observed, wide, target)
    finish(halo.at[0], near_send.at[0], near_recv.at[0], at).wait()
    finish(halo.at[1], near_send.at[1], near_recv.at[1], at).wait()
    stage_margin(halo, margin)
    forward_margin(margin, staged, edge_taps)
    outputs = convolved(taps, edge_taps, places, vectors[...][:, 0:1])
    for q in range(MEMBERS):
        to_score[q, :, 0:CHUNK] = outputs[:, q * CHUNK : (q + 1) * CHUNK].astype(jnp.bfloat16)
        to_score[q, :, CHUNK:LANES] = jnp.zeros((CHAN, LANES - CHUNK), jnp.bfloat16)
    for there in others:
        send_to(to_score.at[there], values.at[member], near_send.at[2], near_recv.at[2], (there, lon))
    values[member] = to_score[member]
    finish(values.at[0:7], near_send.at[2], near_recv.at[2], at).wait_recv()
    kernel_terms(values, target, vectors, gradients, score)
    for there in others:
        send_to(gradients.at[there], gathered.at[member], near_send.at[3], near_recv.at[3], (there, lon))
    for there in others:
        send_to(score, score_rx.at[member], near_send.at[4], near_recv.at[4], (there, lon))
    gathered[member] = gradients[member]
    score_rx[member] = score[...]
    finish(gathered.at[0:7], near_send.at[3], near_recv.at[3], at).wait_recv()
    stack_gradient(gathered, packed, stacked, edge_stacked, places)
    core, partner = at["core"], moved(at, "core", 1)
    weight_terms(1 - core, x, margin, stacked, edge_stacked, theirs)
    for k in range(2):
        send(theirs.at[k], core_rx[k], send_sems.at[k, 0], recv_sems.at[k, 0], partner)
    shared_terms(x, margin, stacked, edge_stacked, fifth, fifth_sent, tails)
    source = fifth_sent.at[pl.ds(pl.multiple_of((1 - core) * 1024, 16), 1024)]
    send(source, core_rx[2], send_sems.at[2, 0], recv_sems.at[2, 0], partner)
    weight_terms(core, x, margin, stacked, edge_stacked, mine)
    for k, own in ((0, mine), (1, mine), (2, fifth)):
        add_core(at, k, own, core_rx, cur, send_sems, recv_sems)
        launch(at, k, 0, cur, rxs, send_sems, recv_sems)
    write_gradient(packed, grad_out)
    finish(score_rx.at[0:7], near_send.at[4], near_recv.at[4], at).wait_recv()
    own_scores(starts, score_rx, owned)
    all_reduce(at, out, core_rx, cur, rxs, shared, send_sems, recv_sems, mid_recv, far_recv)
    finish(values.at[0:7], near_send.at[2], near_recv.at[2], at).wait_send()
    finish(gathered.at[0:7], near_send.at[3], near_recv.at[3], at).wait_send()
    finish(score_rx.at[0:7], near_send.at[4], near_recv.at[4], at).wait_send()


def kernel_scratch():
    chunk = (MEMBERS, CHAN, LANES)
    return [
        pltpu.VMEM((LAT + 4, LON_DEV, CIN), jnp.bfloat16),
        pltpu.VMEM((TAPS, TAPS, COUT, CIN), jnp.bfloat16),
        pltpu.VMEM((LON_DEV, LAT, COUT), jnp.float32),
        pltpu.VMEM((TAPS, 4 * LAT, POINTS), jnp.bfloat16),
        pltpu.VMEM((2 * PITCH, (LAT + 4) * PITCH), jnp.bfloat16),
        pltpu.VMEM(((LAT + 4) * PITCH, COLS), jnp.bfloat16),
        pltpu.VMEM((8, LANES), jnp.float32),
        pltpu.VMEM((LANES, LANES), jnp.float32),
        pltpu.VMEM((CHAN, LANES), jnp.float32),
        pltpu.VMEM((CHAN, LANES), jnp.float32),
        pltpu.VMEM((CHAN, POINTS), jnp.bfloat16),
        pltpu.SemaphoreType.DMA((5,)),
        pltpu.VMEM((TAPS * TAP_ROWS, COLS), jnp.bfloat16),
        pltpu.VMEM((2, PITCH, COLS), jnp.bfloat16),
        pltpu.VMEM((2, PITCH, COLS), jnp.bfloat16),
        pltpu.VMEM((TAPS, 64, COLS), jnp.bfloat16),
        pltpu.VMEM((TAP_ROWS, POINTS), jnp.float32),
        pltpu.VMEM((TAP_ROWS, 64), jnp.float32),
        pltpu.VMEM(chunk, jnp.bfloat16),
        pltpu.VMEM(chunk, jnp.bfloat16),
        pltpu.VMEM(chunk, jnp.bfloat16),
        pltpu.VMEM(chunk, jnp.bfloat16),
        pltpu.VMEM((8, LANES), jnp.float32),
        pltpu.VMEM((MEMBERS, 8, LANES), jnp.float32),
        pltpu.VMEM((TAP_ROWS, POINTS), jnp.bfloat16),
        pltpu.VMEM((TAP_ROWS, 64), jnp.bfloat16),
        pltpu.VMEM((2, ROWS, LANES), jnp.bfloat16),
        pltpu.VMEM((2, ROWS, LANES), jnp.float32),
        pltpu.VMEM((ROWS, LANES), jnp.float32),
        pltpu.VMEM((ROWS, LANES), jnp.bfloat16),
        pltpu.VMEM((TAPS, 8, 512), jnp.float32),
        pltpu.SemaphoreType.DMA((5,)),
        pltpu.SemaphoreType.DMA((5,)),
    ] + reduce_scratch()


def finish_kernel(main, low, high, grad_in, owned_in, weight_grad, bias_grad, grad_out, owned_out, sems):
    passed = [
        pltpu.make_async_copy(grad_in, grad_out, sems.at[0]),
        pltpu.make_async_copy(owned_in, owned_out, sems.at[1]),
    ]

    @pl.when(pl.program_id(0) == 0)
    def _():
        for copy in passed:
            copy.start()

    factor = 1.0 / math.sqrt(MEMBERS * LAT * LON_DEV * GROUPS)
    a = pl.program_id(0)
    more = jnp.concatenate([low[...].astype(jnp.float32), high[...].astype(jnp.float32)], axis=0) * factor
    number = lax.broadcasted_iota(jnp.int32, (32, LANES), 0)
    pieces = [
        jnp.sum(jnp.where(number == 4 * a + q, more, 0.0), axis=0, keepdims=True) for q in range(4)
    ]
    last = jnp.transpose(jnp.broadcast_to(jnp.concatenate(pieces, axis=1), (8, 512)))
    for b in range(TAPS):
        weight_grad[0, b, :, 0:WIDE] = (
            main[b * CHAN : (b + 1) * CHAN, :].astype(jnp.float32)[:COUT, :] * factor
        )
        weight_grad[0, b, :, WIDE:CIN] = last[b * CHAN : b * CHAN + COUT, 0:1]
    bias = jnp.concatenate([more[4 * TAPS + q : 4 * TAPS + q + 1, :] for q in range(4)], axis=1)
    bias_grad[...] = bias[:, 2 * CHAN : 2 * CHAN + COUT]

    @pl.when(pl.program_id(0) == TAPS - 1)
    def _():
        for copy in passed:
            copy.wait()


def body(fields, weight, out_bias, observed, widths, owner_start):
    vmem = pl.BlockSpec(memory_space=pltpu.VMEM)
    hbm = pl.BlockSpec(memory_space=pl.ANY)
    summed, grad, owned = pl.pallas_call(
        whole_kernel,
        out_shape=[
            jax.ShapeDtypeStruct((ROWS, WIDE), jnp.bfloat16),
            jax.ShapeDtypeStruct((LON_DEV, LAT, COUT), jnp.bfloat16),
            jax.ShapeDtypeStruct((1, CAP * LON_DEV), jnp.float32),
        ],
        in_specs=[hbm] * 5 + [vmem] * 2 + [pl.BlockSpec(memory_space=pltpu.SMEM)],
        out_specs=[vmem] * 3,
        scratch_shapes=kernel_scratch(),
        compiler_params=pltpu.CompilerParams(
            collective_id=1, has_side_effects=True, vmem_limit_bytes=56 * 1024 * 1024
        ),
        cost_estimate=pl.CostEstimate(flops=6 << 30, bytes_accessed=16 << 20, transcendentals=1 << 20),
    )(
        jnp.transpose(fields[0], (1, 2, 0)), weight, jnp.transpose(observed, (2, 1, 0)),
        jnp.asarray(margin_places(), jnp.bfloat16), jnp.asarray(edge_picks(), jnp.bfloat16),
        out_bias.reshape(1, COUT), widths.reshape(1, COUT), owner_start[0],
    )
    weight_grad, bias_grad, grad, owned = pl.pallas_call(
        finish_kernel,
        grid=(TAPS,),
        out_shape=[
            jax.ShapeDtypeStruct((TAPS, TAPS, COUT, CIN), jnp.float32),
            jax.ShapeDtypeStruct((1, COUT), jnp.float32),
            jax.ShapeDtypeStruct((LON_DEV, LAT, COUT), jnp.bfloat16),
            jax.ShapeDtypeStruct((1, CAP * LON_DEV), jnp.float32),
        ],
        in_specs=[
            pl.BlockSpec((TAP_ROWS, WIDE), lambda a: (a, 0)),
            pl.BlockSpec((16, LANES), lambda a: (TAPS * TAP_ROWS // 16, 4)),
            pl.BlockSpec((16, LANES), lambda a: (TAPS * TAP_ROWS // 16 + 1, 4)),
            hbm,
            hbm,
        ],
        out_specs=[
            pl.BlockSpec((1, TAPS, COUT, CIN), lambda a: (a, 0, 0, 0)),
            pl.BlockSpec((1, COUT), lambda a: (0, 0)),
            hbm,
            hbm,
        ],
        scratch_shapes=[pltpu.SemaphoreType.DMA((2,))],
        compiler_params=pltpu.CompilerParams(vmem_limit_bytes=58 * 1024 * 1024),
    )(summed, summed, summed, grad, owned)
    bias_grad = bias_grad.reshape(COUT)
    out_grad = jnp.transpose(grad, (2, 1, 0))[None]
    owned_score = owned.reshape(1, 1, CAP * LON_DEV)
    return (out_grad, owned_score, weight_grad, bias_grad)


def solution(mesh):
    in_specs = (P("member", None, None, "lon"), P(), P(), P(None, None, "lon"), P(), P("lon", None))
    out_specs = (P("member", None, None, "lon"), P("lon", "member", None), P(), P())
    return jax.shard_map(body, mesh=mesh, in_specs=in_specs, out_specs=out_specs, check_vma=False)
```

```python
import math

import jax
import jax.numpy as jnp
import numpy as np
from jax import lax
from jax.experimental import pallas as pl
from jax.experimental.pallas import tpu as pltpu
from jax.sharding import PartitionSpec as P

MESH = pl.DeviceIdType.MESH
MEMBERS = 8
GROUPS = 32
TAPS = 5
CIN = 641
COUT = 73
CHAN = 80
LAT = 16
LON_DEV = 45
PITCH = 48
POINTS = LAT * PITCH
CHUNK = 2 * PITCH
CAP = 6
TAP_ROWS = TAPS * CHAN
NT = (((1,), (1,)), ((), ()))
ROWS = 2048
LANES = 128
PARTS = 3
COLS = 768
WIDE = 640
PART_ROWS = (2048, 2048, 1024)
ORDERS = (("x", "y", "z"), ("y", "x", "z"), ("z", "x", "y"))


def position():
    member = lax.axis_index("member")
    lon = lax.axis_index("lon")
    return {
        "x": (lon // 16) * 2 + member % 2,
        "y": member // 2,
        "z": (lon // 2) % 8,
        "core": lon % 2,
    }


EXTENT = {"x": 4, "y": 4, "z": 8, "core": 2}


def device(at):
    return (at["y"] * 2 + at["x"] % 2, (at["x"] // 2) * 16 + at["z"] * 2 + at["core"])


def moved(at, axis, delta):
    there = dict(at)
    there[axis] = lax.rem(at[axis] + delta, EXTENT[axis])
    return there


def send(src, dst, send_sem, recv_sem, at):
    copy = pltpu.make_async_remote_copy(
        src_ref=src, dst_ref=dst, send_sem=send_sem, recv_sem=recv_sem,
        device_id=device(at), device_id_type=MESH,
    )
    copy.start()


def send_to(src, dst, send_sem, recv_sem, there):
    copy = pltpu.make_async_remote_copy(
        src_ref=src, dst_ref=dst, send_sem=send_sem, recv_sem=recv_sem,
        device_id=there, device_id_type=MESH,
    )
    copy.start()


def finish(ref, send_sem, recv_sem, at):
    copy = pltpu.make_async_remote_copy(
        src_ref=ref, dst_ref=ref, send_sem=send_sem, recv_sem=recv_sem,
        device_id=device(at), device_id_type=MESH,
    )
    return copy


def greet(at):
    barrier = pltpu.get_barrier_semaphore()
    count = 0
    for axis in ("core", "x", "y", "z"):
        for delta in range(1, EXTENT[axis]):
            pl.semaphore_signal(
                barrier, inc=1, device_id=device(moved(at, axis, delta)), device_id_type=MESH
            )
            count += 1
    member, lon = lax.axis_index("member"), lax.axis_index("lon")
    for delta in range(1, MEMBERS):
        there = (lax.rem(member + delta, MEMBERS), lon)
        pl.semaphore_signal(barrier, inc=1, device_id=there, device_id_type=MESH)
        count += 1
    for delta in (1, GROUPS - 1):
        there = (member, lax.rem(lon + delta, GROUPS))
        pl.semaphore_signal(barrier, inc=1, device_id=there, device_id_type=MESH)
        count += 1
    return barrier, count


def stage_rows(k):
    rows, sizes = PART_ROWS[k], []
    for axis in ORDERS[k][: 2 if k == 2 else 3]:
        rows //= EXTENT[axis]
        sizes.append(rows)
    return sizes


SIZES = [stage_rows(k) for k in range(PARTS)]


def place(at, out, k, row, rows):
    if k == 2:
        return out.at[4, pl.ds(pl.multiple_of(at["core"] * 1024 + row, 16), rows), :]
    return out.at[2 * at["core"] + k, pl.ds(pl.multiple_of(row, 16), rows), :]


def launch(at, k, s, cur, rxs, send_sems, recv_sems):
    axis, rows = ORDERS[k][s], SIZES[k][s]
    for delta in range(1, EXTENT[axis]):
        there = moved(at, axis, delta)
        source = cur[k][s].at[pl.ds(pl.multiple_of(there[axis] * rows, 16), rows)]
        send(source, rxs[k][s].at[delta - 1], send_sems.at[k, s + 1], recv_sems.at[k, s + 1], there)


def add_core(at, k, mine, core_rx, cur, send_sems, recv_sems):
    finish(core_rx[k], send_sems.at[k, 0], recv_sems.at[k, 0], at).wait_recv()
    step = 256

    def add(i, _):
        here = pl.ds(pl.multiple_of(i * step, step), step)
        if k == 2:
            own = mine[pl.ds(pl.multiple_of(at["core"] * 1024 + i * step, step), step), :]
        else:
            own = mine[k, here, :]
        cur[k][0][here, :] = (own + core_rx[k][here, :].astype(jnp.float32)).astype(jnp.bfloat16)
        return 0

    lax.fori_loop(0, PART_ROWS[k] // step, add, 0)


def gather(at, out, k, s, row, send_sems, recv_sems):
    axis = ORDERS[k][s]
    block = place(at, out, k, row, SIZES[k][s])
    for delta in range(1, EXTENT[axis]):
        send(block, block, send_sems.at[k, 4 + s], recv_sems.at[k, 4 + s], moved(at, axis, delta))


def spread(at, out, k, dy, dx, send_sem, recv_sem, there):
    first, second = ORDERS[k][0], ORDERS[k][1]
    row = lax.rem(at[first] + 4 - dx, 4) * SIZES[k][0] + lax.rem(at[second] + 4 - dy, 4) * SIZES[k][1]
    block = place(at, out, k, row, SIZES[k][1])
    if there is None:
        finish(block, send_sem, recv_sem, at).wait_recv()
    else:
        send(block, block, send_sem, recv_sem, there)


def all_reduce(at, out, core_rx, cur, rxs, shared, send_sems, recv_sems, mid_recv, far_recv):
    row = [0] * PARTS
    partner = moved(at, "core", 1)
    for s in range(3):
        for k in (2, 0, 1) if s == 2 else (0, 1, 2):
            if k == 2 and s == 2:
                finish(shared.at[0:3], send_sems.at[k, 3], recv_sems.at[k, 3], at).wait_recv()
                total = shared[0].astype(jnp.float32)
                for y in range(1, 4):
                    total = total + shared[y].astype(jnp.float32)
                place(at, out, k, row[k], 32)[...] = total.astype(jnp.bfloat16)
                gather(at, out, k, 1, row[k], send_sems, recv_sems)
                continue
            axis, rows = ORDERS[k][s], SIZES[k][s]
            finish(rxs[k][s], send_sems.at[k, s + 1], recv_sems.at[k, s + 1], at).wait_recv()
            row[k] = row[k] + at[axis] * rows
            base = pl.multiple_of(at[axis] * rows, 16)
            step = min(rows, 128)

            def add(i, _, k=k, s=s, axis=axis, base=base, step=step):
                total = cur[k][s][pl.ds(pl.multiple_of(base + i * step, 16), step), :].astype(jnp.float32)
                here = pl.ds(pl.multiple_of(i * step, 16), step)
                for slot in range(EXTENT[axis] - 1):
                    total = total + rxs[k][s][slot, here, :].astype(jnp.float32)
                total = total.astype(jnp.bfloat16)
                if k == 2 and s == 1:
                    shared[at["y"]] = total
                elif s == 2:
                    place(at, out, k, row[k], step)[...] = total
                else:
                    cur[k][s + 1][here, :] = total
                return 0

            if rows == step:
                add(0, 0)
            else:
                lax.fori_loop(0, rows // step, add, 0)
            if k == 2 and s == 1:
                for delta in range(1, 4):
                    own = shared.at[at["y"]]
                    send(own, own, send_sems.at[k, 3], recv_sems.at[k, 3], moved(at, "y", delta))
            elif s == 2:
                gather(at, out, k, 2, row[k], send_sems, recv_sems)
            else:
                launch(at, k, s + 1, cur, rxs, send_sems, recv_sems)
    def arrived(k, s):
        finish(rxs[k][s], send_sems.at[k, 4 + s], recv_sems.at[k, 4 + s], at).wait_recv()

    def onward(k, dy):
        first = ORDERS[k][0]
        for dx in (2, 1, 3):
            spread(at, out, k, dy, 0, send_sems.at[k, 4], far_recv.at[k, 4 * dx + dy], moved(at, first, dx))
        spread(at, out, k, dy, 0, send_sems.at[k, 7], recv_sems.at[k, 7], partner)

    arrived(2, 1)
    row[2] = row[2] - at["x"] * SIZES[2][1]
    gather(at, out, 2, 0, row[2], send_sems, recv_sems)
    for k in range(2):
        arrived(k, 2)
        for dy in (2, 1, 3):
            there = moved(at, ORDERS[k][1], dy)
            spread(at, out, k, 0, 0, send_sems.at[k, 5], mid_recv.at[k, dy], there)
        onward(k, 0)
    for dy in (1, 3, 2):
        for k in range(2):
            spread(at, out, k, dy, 0, send_sems.at[k, 5], mid_recv.at[k, dy], None)
            onward(k, dy)
    for dy in (0, 1, 3, 2):
        if dy == 2:
            arrived(2, 0)
            block = place(at, out, 2, 0, PART_ROWS[2])
            send(block, block, send_sems.at[2, 7], recv_sems.at[2, 7], partner)
        for dx in (1, 3, 2):
            for k in range(2):
                spread(at, out, k, dy, dx, send_sems.at[k, 4], far_recv.at[k, 4 * dx + dy], None)
                spread(at, out, k, dy, dx, send_sems.at[k, 7], recv_sems.at[k, 7], partner)
    for k in (2, 0, 1):
        finish(core_rx[k], send_sems.at[k, 7], recv_sems.at[k, 7], partner).wait_recv()
    for k in range(PARTS):
        finish(core_rx[k], send_sems.at[k, 0], recv_sems.at[k, 0], partner).wait_send()
        finish(core_rx[k], send_sems.at[k, 7], recv_sems.at[k, 7], partner).wait_send()
        for s in range(len(SIZES[k])):
            finish(rxs[k][s], send_sems.at[k, s + 1], recv_sems.at[k, s + 1], partner).wait_send()
            finish(rxs[k][s], send_sems.at[k, s + 4], recv_sems.at[k, s + 4], partner).wait_send()
    finish(shared.at[0:3], send_sems.at[2, 3], recv_sems.at[2, 3], partner).wait_send()


def reduce_scratch():
    shapes = [pltpu.VMEM((PART_ROWS[k], LANES), jnp.bfloat16) for k in range(PARTS)]
    for k in range(PARTS):
        rows = PART_ROWS[k]
        for size in SIZES[k]:
            shapes.append(pltpu.VMEM((rows, LANES), jnp.bfloat16))
            rows = size
    for k in range(PARTS):
        for axis, size in zip(ORDERS[k], SIZES[k]):
            shapes.append(pltpu.VMEM((EXTENT[axis] - 1, size, LANES), jnp.bfloat16))
    shapes.append(pltpu.VMEM((4, 32, LANES), jnp.bfloat16))
    shapes += [pltpu.SemaphoreType.DMA((PARTS, 8)), pltpu.SemaphoreType.DMA((PARTS, 8))]
    shapes += [pltpu.SemaphoreType.DMA((2, 4)), pltpu.SemaphoreType.DMA((2, 16))]
    return shapes


def edge_picks():
    picks = np.zeros((2, PITCH, (LAT + 4) * PITCH), np.float32)
    for side, first in ((0, LON_DEV - 2), (1, 0)):
        for i in range(LAT + 4):
            for h in range(2):
                picks[side, 2 * i + h, i * PITCH + first + h] = 1.0
    return picks.reshape(2 * PITCH, -1)


def margin_places():
    places = np.zeros((TAPS, 2, LAT, 2, LAT, PITCH), np.float32)
    for b in range(TAPS):
        for side, first in ((0, -2), (1, LON_DEV)):
            for h in range(2):
                j = first + h - b + 2
                if 0 <= j < LON_DEV:
                    for i in range(LAT):
                        places[b, side, i, h, i, j] = 1.0
    return places.reshape(TAPS, 4 * LAT, POINTS)


def stage_field(raw, x):
    lane = lax.broadcasted_iota(jnp.int32, (PITCH, LANES), 1)
    row = lax.broadcasted_iota(jnp.int32, (PITCH, LANES), 0)
    tail = jnp.where((lane == CIN - 640) & (row < LON_DEV), 1.0, 0.0).astype(jnp.bfloat16)
    zeros = jnp.zeros((16, COLS), jnp.bfloat16)

    def one(i, _):
        base = pl.multiple_of(i * PITCH, 16)
        x[pl.ds(base + 32, 16), :] = zeros
        x[pl.ds(base, PITCH), 640:COLS] = tail
        x[pl.ds(base, LON_DEV), 0:CIN] = raw[i]
        return 0

    lax.fori_loop(0, LAT + 4, one, 0)


def stage_columns(bias, widths, tile, vectors):
    tile[...] = jnp.ones((8, LANES), jnp.float32)
    tile[0:1, 0:COUT] = bias[...]
    tile[1:2, 0:COUT] = widths[...]
    vectors[:, 0:8] = jnp.transpose(tile[...])[0:CHAN, :]


def stage_target(observed, wide, target):
    spots = LON_DEV * LAT
    point = lax.broadcasted_iota(jnp.int32, (LANES, spots), 0)
    spot = lax.broadcasted_iota(jnp.int32, (LANES, spots), 1)
    second = (point >= PITCH).astype(jnp.int32)
    wanted = (point - PITCH * second) * LAT + 2 * lax.axis_index("member") + second
    chosen = ((spot == wanted) & (point < CHUNK)).astype(jnp.float32)
    wide[...] = jnp.zeros((LANES, LANES), jnp.float32)
    wide[:, 0:COUT] = jnp.dot(
        chosen, observed[...].reshape(spots, COUT),
        precision=lax.Precision.HIGHEST, preferred_element_type=jnp.float32,
    )
    target[...] = jnp.transpose(wide[...])[0:CHAN, :]


def write_gradient(packed, grad_out):
    spots = LON_DEV * LAT
    spot = lax.broadcasted_iota(jnp.int32, (spots, POINTS), 0)
    point = lax.broadcasted_iota(jnp.int32, (spots, POINTS), 1)
    wanted = (spot & (LAT - 1)) * PITCH + (spot >> 4)
    moves = jnp.where(point == wanted, 1.0, 0.0).astype(jnp.bfloat16)
    moved_grad = lax.dot_general(moves, packed[...], NT, preferred_element_type=jnp.float32)
    grad_out[...] = moved_grad.astype(jnp.bfloat16).reshape(LON_DEV, LAT, CHAN)[:, :, :COUT]


def stage_weight(w, staged):
    zeros = jnp.zeros((16, COLS), jnp.bfloat16)
    tail = jnp.zeros((64, COLS - 640), jnp.bfloat16)

    def one(a, _):
        for b in range(TAPS):
            base = pl.multiple_of(a * TAP_ROWS + b * CHAN, 16)
            staged[pl.ds(base + 64, 16), :] = zeros
            staged[pl.ds(base, 64), 640:COLS] = tail
            staged[pl.ds(base, COUT), 0:CIN] = w[a, b]
        return 0

    lax.fori_loop(0, TAPS, one, 0)


def forward_own(x, staged, taps):
    for n in range(3):
        lanes = slice(n * 256, n * 256 + 256)

        def one(a, total, n=n):
            rows = pl.ds(pl.multiple_of(a * PITCH + n * 256, 16), 256)
            left = staged[pl.ds(pl.multiple_of(a * TAP_ROWS, 16), TAP_ROWS), :]
            return total + lax.dot_general(left, x[rows, :], NT, preferred_element_type=jnp.float32)

        taps[:, lanes] = lax.fori_loop(0, TAPS, one, jnp.zeros((TAP_ROWS, 256), jnp.float32))


def stage_margin(halo, margin):
    left = halo[0].astype(jnp.float32)
    right = halo[1].astype(jnp.float32)
    for a in range(TAPS):
        margin[a, 0:32, :] = left[2 * a : 2 * a + 32, :].astype(jnp.bfloat16)
        margin[a, 32:64, :] = right[2 * a : 2 * a + 32, :].astype(jnp.bfloat16)


def forward_margin(margin, staged, edge_taps):
    def one(a, total):
        left = staged[pl.ds(pl.multiple_of(a * TAP_ROWS, 16), TAP_ROWS), :]
        return total + lax.dot_general(left, margin[a], NT, preferred_element_type=jnp.float32)

    edge_taps[...] = lax.fori_loop(0, TAPS, one, jnp.zeros((TAP_ROWS, 64), jnp.float32))


def convolved(taps, edge_taps, places, bias):
    total = jnp.broadcast_to(bias, (CHAN, POINTS))
    for b in range(TAPS):
        rows = slice(b * CHAN, b * CHAN + CHAN)
        part = taps[rows, :]
        total = total + (part if b == 2 else pltpu.roll(part, (2 - b) % POINTS, 1))
        if b != 2:
            total = total + jnp.dot(
                edge_taps[rows, :], places[b].astype(jnp.float32),
                precision=lax.Precision.HIGHEST, preferred_element_type=jnp.float32,
            )
    return total


def kernel_terms(values, target, vectors, gradients, score):
    lane = lax.broadcasted_iota(jnp.int32, (16, LANES), 1)
    real = (lane < LON_DEV) | ((lane >= PITCH) & (lane < PITCH + LON_DEV))

    def block(t, score_sum):
        rows = pl.ds(pl.multiple_of(t * 16, 16), 16)
        members = [values[m, rows, :].astype(jnp.float32) for m in range(MEMBERS)]
        width = vectors[rows, :][:, 1:2]
        inverse = jnp.broadcast_to(1.0 / (width * width), (16, LANES))
        half = -0.5 * inverse
        goal = target[rows, :]
        pulls = [jnp.zeros((16, LANES), jnp.float32) for _ in range(MEMBERS)]
        pair_sum = jnp.zeros((16, LANES), jnp.float32)
        for m in range(MEMBERS):
            for n in range(m + 1, MEMBERS):
                spread = members[m] - members[n]
                kernel_pair = jnp.exp(spread * spread * half)
                pair_sum = pair_sum + kernel_pair
                pull = kernel_pair * spread
                pulls[m] = pulls[m] + pull
                pulls[n] = pulls[n] - pull
        obs_sum = jnp.zeros((16, LANES), jnp.float32)
        for m in range(MEMBERS):
            misfit = members[m] - goal
            kernel_obs = jnp.exp(misfit * misfit * half)
            obs_sum = obs_sum + kernel_obs
            gradient = inverse * (misfit * kernel_obs - pulls[m] * (1.0 / MEMBERS))
            gradients[m, rows, :] = jnp.where(real, gradient, 0.0).astype(jnp.bfloat16)
        per_channel = (MEMBERS + 2.0 * pair_sum) * (1.0 / (2 * MEMBERS * MEMBERS)) - obs_sum * (1.0 / MEMBERS)
        channel = t * 16 + lax.broadcasted_iota(jnp.int32, (16, LANES), 0)
        return score_sum + jnp.where(channel < COUT, per_channel, 0.0)

    total = lax.fori_loop(0, CHAN // 16, block, jnp.zeros((16, LANES), jnp.float32))
    score[...] = jnp.broadcast_to(jnp.sum(total, axis=0, keepdims=True) * (1.0 / COUT), (8, LANES))


def stack_gradient(gathered, packed_grad, stacked, edge_stacked, places):
    grad = jnp.concatenate(
        [gathered[q].astype(jnp.float32)[:, :CHUNK] for q in range(MEMBERS)], axis=1
    )
    packed = grad.astype(jnp.bfloat16)
    packed_grad[...] = packed
    for b in range(TAPS):
        rows = slice(b * CHAN, b * CHAN + CHAN)
        if b == 2:
            stacked[rows, :] = packed
            edge_stacked[rows, :] = jnp.zeros((CHAN, 64), jnp.bfloat16)
        else:
            stacked[rows, :] = pltpu.roll(grad, (b - 2) % POINTS, 1).astype(jnp.bfloat16)
            edge = lax.dot_general(packed, places[b], NT, preferred_element_type=jnp.float32)
            edge_stacked[rows, :] = edge.astype(jnp.bfloat16)


def product(a, lanes, x, margin, stacked, edge_stacked):
    right = x[pl.ds(pl.multiple_of(a * PITCH, 16), POINTS), lanes]
    total = jnp.dot(stacked[...], right, preferred_element_type=jnp.float32)
    return total + jnp.dot(edge_stacked[...], margin[a, :, lanes], preferred_element_type=jnp.float32)


def shared_terms(x, margin, stacked, edge_stacked, fifth, fifth_sent, tails):
    def one(a, _):
        total = product(a, slice(512, 768), x, margin, stacked, edge_stacked)
        rows = pl.ds(pl.multiple_of(a * TAP_ROWS, 16), TAP_ROWS)
        fifth[rows, :] = total[:, :LANES]
        fifth_sent[rows, :] = total[:, :LANES].astype(jnp.bfloat16)
        tails[a, :, 0:TAP_ROWS] = jnp.transpose(total[:, LANES:])[0:8, :]
        return 0

    tails[...] = jnp.zeros((TAPS, 8, 512), jnp.float32)
    lax.fori_loop(0, TAPS, one, 0)
    spare = ROWS - TAPS * TAP_ROWS
    fifth[TAPS * TAP_ROWS : ROWS, :] = jnp.zeros((spare, LANES), jnp.float32)
    for n in range(TAPS + 1):
        a, channel = (n, 0) if n < TAPS else (2, 1)
        for q in range(4):
            row = TAPS * TAP_ROWS + 4 * n + q
            fifth[row : row + 1, :] = tails[a, channel : channel + 1, q * LANES : (q + 1) * LANES]
    fifth_sent[TAPS * TAP_ROWS : ROWS, :] = fifth[TAPS * TAP_ROWS : ROWS, :].astype(jnp.bfloat16)


def weight_terms(half, x, margin, stacked, edge_stacked, into):
    lanes = pl.ds(pl.multiple_of(half * 256, 256), 256)

    def one(a, _):
        total = product(a, lanes, x, margin, stacked, edge_stacked).astype(into.dtype)
        rows = pl.ds(pl.multiple_of(a * TAP_ROWS, 16), TAP_ROWS)
        for k in range(2):
            into[k, rows, :] = total[:, k * LANES : (k + 1) * LANES]
        return 0

    lax.fori_loop(0, TAPS, one, 0)
    first = TAPS * TAP_ROWS
    for k in range(2):
        into[k, first:ROWS, :] = jnp.zeros((ROWS - first, LANES), into.dtype)


def own_scores(starts, score_rx, owned):
    lane = lax.broadcasted_iota(jnp.int32, (8, LANES), 1)
    row = lax.broadcasted_iota(jnp.int32, (8, LANES), 0)
    me = lax.axis_index("member")
    first, count = starts[me], starts[me + 1] - starts[me]
    wanted = jnp.where(row < count, first + row, -1)
    total = jnp.zeros((8, LANES), jnp.float32)
    for q in range(MEMBERS):
        pair = score_rx[q]
        low = jnp.where(lane < LON_DEV, pair, 0.0)
        high = jnp.where(lane < LON_DEV, pltpu.roll(pair, LANES - PITCH, 1), 0.0)
        total = total + jnp.where(wanted == 2 * q, low, 0.0) + jnp.where(wanted == 2 * q + 1, high, 0.0)
    owned[...] = jnp.concatenate([total[s : s + 1, 0:LON_DEV] for s in range(CAP)], axis=1)


def whole_kernel(
    raw_hbm, w_hbm, observed_hbm, places_hbm, picks_hbm, bias, widths, starts, out, grad_out, owned, *scratch
):
    raw, w, observed, places, picks, x, tile, wide, vectors, target, packed, local = scratch[:12]
    scratch = scratch[12:]
    (
        staged, edges, halo, margin, taps, edge_taps, to_score, values, gradients, gathered, score, score_rx,
        stacked, edge_stacked, theirs, mine, fifth, fifth_sent, tails, near_send, near_recv,
    ) = scratch[:21]
    core_rx, rest = scratch[21:24], scratch[24:]
    cur = [rest[3 * k : 3 * k + 3] for k in range(PARTS)]
    rxs = [rest[8 + 3 * k : 11 + 3 * k] for k in range(PARTS)]
    shared, send_sems, recv_sems, mid_recv, far_recv = rest[16:21]
    at = position()
    member, lon = lax.axis_index("member"), lax.axis_index("lon")
    ahead = (member, lax.rem(lon + 1, GROUPS))
    behind = (member, lax.rem(lon + GROUPS - 1, GROUPS))
    others = [lax.rem(member + delta, MEMBERS) for delta in range(1, MEMBERS)]

    loads = [
        pltpu.make_async_copy(source, target_ref, local.at[n])
        for n, (source, target_ref) in enumerate(
            ((raw_hbm, raw), (picks_hbm, picks), (w_hbm, w), (places_hbm, places), (observed_hbm, observed))
        )
    ]
    for load in loads:
        load.start()
    barrier, count = greet(at)
    stage_columns(bias, widths, tile, vectors)
    loads[0].wait()
    stage_field(raw, x)
    loads[1].wait()
    edge = jnp.dot(picks[...], x[...], preferred_element_type=jnp.float32).astype(jnp.bfloat16)
    edges[0] = edge[:PITCH]
    edges[1] = edge[PITCH:]
    loads[2].wait()
    stage_weight(w, staged)
    pl.semaphore_wait(barrier, count)
    send_to(edges.at[0], halo.at[0], near_send.at[0], near_recv.at[0], ahead)
    send_to(edges.at[1], halo.at[1], near_send.at[1], near_recv.at[1], behind)
    forward_own(x, staged, taps)
    loads[3].wait()
    loads[4].wait()
    stage_target(observed, wide, target)
    finish(halo.at[0], near_send.at[0], near_recv.at[0], at).wait()
    finish(halo.at[1], near_send.at[1], near_recv.at[1], at).wait()
    stage_margin(halo, margin)
    forward_margin(margin, staged, edge_taps)
    outputs = convolved(taps, edge_taps, places, vectors[...][:, 0:1])
    for q in range(MEMBERS):
        to_score[q, :, 0:CHUNK] = outputs[:, q * CHUNK : (q + 1) * CHUNK].astype(jnp.bfloat16)
        to_score[q, :, CHUNK:LANES] = jnp.zeros((CHAN, LANES - CHUNK), jnp.bfloat16)
    for there in others:
        send_to(to_score.at[there], values.at[member], near_send.at[2], near_recv.at[2], (there, lon))
    values[member] = to_score[member]
    finish(values.at[0:7], near_send.at[2], near_recv.at[2], at).wait_recv()
    kernel_terms(values, target, vectors, gradients, score)
    for there in others:
        send_to(gradients.at[there], gathered.at[member], near_send.at[3], near_recv.at[3], (there, lon))
    for there in others:
        send_to(score, score_rx.at[member], near_send.at[4], near_recv.at[4], (there, lon))
    gathered[member] = gradients[member]
    score_rx[member] = score[...]
    finish(gathered.at[0:7], near_send.at[3], near_recv.at[3], at).wait_recv()
    stack_gradient(gathered, packed, stacked, edge_stacked, places)
    core, partner = at["core"], moved(at, "core", 1)
    weight_terms(1 - core, x, margin, stacked, edge_stacked, theirs)
    for k in range(2):
        send(theirs.at[k], core_rx[k], send_sems.at[k, 0], recv_sems.at[k, 0], partner)
    shared_terms(x, margin, stacked, edge_stacked, fifth, fifth_sent, tails)
    source = fifth_sent.at[pl.ds(pl.multiple_of((1 - core) * 1024, 16), 1024)]
    send(source, core_rx[2], send_sems.at[2, 0], recv_sems.at[2, 0], partner)
    weight_terms(core, x, margin, stacked, edge_stacked, mine)
    for k, own in ((0, mine), (1, mine), (2, fifth)):
        add_core(at, k, own, core_rx, cur, send_sems, recv_sems)
        launch(at, k, 0, cur, rxs, send_sems, recv_sems)
    write_gradient(packed, grad_out)
    finish(score_rx.at[0:7], near_send.at[4], near_recv.at[4], at).wait_recv()
    own_scores(starts, score_rx, owned)
    all_reduce(at, out, core_rx, cur, rxs, shared, send_sems, recv_sems, mid_recv, far_recv)
    finish(values.at[0:7], near_send.at[2], near_recv.at[2], at).wait_send()
    finish(gathered.at[0:7], near_send.at[3], near_recv.at[3], at).wait_send()
    finish(score_rx.at[0:7], near_send.at[4], near_recv.at[4], at).wait_send()


def kernel_scratch():
    chunk = (MEMBERS, CHAN, LANES)
    return [
        pltpu.VMEM((LAT + 4, LON_DEV, CIN), jnp.bfloat16),
        pltpu.VMEM((TAPS, TAPS, COUT, CIN), jnp.bfloat16),
        pltpu.VMEM((LON_DEV, LAT, COUT), jnp.float32),
        pltpu.VMEM((TAPS, 4 * LAT, POINTS), jnp.bfloat16),
        pltpu.VMEM((2 * PITCH, (LAT + 4) * PITCH), jnp.bfloat16),
        pltpu.VMEM(((LAT + 4) * PITCH, COLS), jnp.bfloat16),
        pltpu.VMEM((8, LANES), jnp.float32),
        pltpu.VMEM((LANES, LANES), jnp.float32),
        pltpu.VMEM((CHAN, LANES), jnp.float32),
        pltpu.VMEM((CHAN, LANES), jnp.float32),
        pltpu.VMEM((CHAN, POINTS), jnp.bfloat16),
        pltpu.SemaphoreType.DMA((5,)),
        pltpu.VMEM((TAPS * TAP_ROWS, COLS), jnp.bfloat16),
        pltpu.VMEM((2, PITCH, COLS), jnp.bfloat16),
        pltpu.VMEM((2, PITCH, COLS), jnp.bfloat16),
        pltpu.VMEM((TAPS, 64, COLS), jnp.bfloat16),
        pltpu.VMEM((TAP_ROWS, POINTS), jnp.float32),
        pltpu.VMEM((TAP_ROWS, 64), jnp.float32),
        pltpu.VMEM(chunk, jnp.bfloat16),
        pltpu.VMEM(chunk, jnp.bfloat16),
        pltpu.VMEM(chunk, jnp.bfloat16),
        pltpu.VMEM(chunk, jnp.bfloat16),
        pltpu.VMEM((8, LANES), jnp.float32),
        pltpu.VMEM((MEMBERS, 8, LANES), jnp.float32),
        pltpu.VMEM((TAP_ROWS, POINTS), jnp.bfloat16),
        pltpu.VMEM((TAP_ROWS, 64), jnp.bfloat16),
        pltpu.VMEM((2, ROWS, LANES), jnp.bfloat16),
        pltpu.VMEM((2, ROWS, LANES), jnp.float32),
        pltpu.VMEM((ROWS, LANES), jnp.float32),
        pltpu.VMEM((ROWS, LANES), jnp.bfloat16),
        pltpu.VMEM((TAPS, 8, 512), jnp.float32),
        pltpu.SemaphoreType.DMA((5,)),
        pltpu.SemaphoreType.DMA((5,)),
    ] + reduce_scratch()


def finish_kernel(
    summed, weight_grad, bias_grad, main, wide, in_sems, out_sems
):
    factor = 1.0 / math.sqrt(MEMBERS * LAT * LON_DEV * GROUPS)
    first = TAPS * TAP_ROWS
    tail = (TAPS - 1, slice(first, ROWS))
    loads = [pltpu.make_async_copy(summed.at[tail], main.at[tail], in_sems.at[TAPS])]
    for a in range(TAPS):
        rows = (slice(None), slice(a * TAP_ROWS, (a + 1) * TAP_ROWS))
        loads.append(pltpu.make_async_copy(summed.at[rows], main.at[rows], in_sems.at[a]))
    for copy in loads:
        copy.start()
    loads[0].wait()
    more = main[TAPS - 1, first:ROWS, :].astype(jnp.float32) * factor
    bias = jnp.concatenate([more[4 * TAPS + q : 4 * TAPS + q + 1, :] for q in range(4)], axis=1)
    bias_grad[...] = bias[:, 2 * CHAN : 2 * CHAN + COUT]
    stores = []
    for a in range(TAPS):
        last = jnp.concatenate([more[4 * a + q : 4 * a + q + 1, :] for q in range(4)], axis=1)
        last = jnp.transpose(jnp.broadcast_to(last, (8, 512)))
        loads[a + 1].wait()
        for b in range(TAPS):
            base, n = a * TAP_ROWS + b * CHAN, a * TAPS + b
            for block in range(TAPS):
                part = main[block, base : base + CHAN, :].astype(jnp.float32) * factor
                wide[n, :, block * LANES : (block + 1) * LANES] = part[:COUT]
            wide[n, :, WIDE:CIN] = last[b * CHAN : b * CHAN + COUT, 0:1]
            stores.append(pltpu.make_async_copy(wide.at[n], weight_grad.at[n], out_sems.at[n]))
            stores[-1].start()
    for copy in stores:
        copy.wait()


def body(fields, weight, out_bias, observed, widths, owner_start):
    vmem = pl.BlockSpec(memory_space=pltpu.VMEM)
    hbm = pl.BlockSpec(memory_space=pl.ANY)
    summed, grad, owned = pl.pallas_call(
        whole_kernel,
        out_shape=[
            jax.ShapeDtypeStruct((TAPS, ROWS, LANES), jnp.bfloat16),
            jax.ShapeDtypeStruct((LON_DEV, LAT, COUT), jnp.bfloat16),
            jax.ShapeDtypeStruct((1, CAP * LON_DEV), jnp.float32),
        ],
        in_specs=[hbm] * 5 + [vmem] * 2 + [pl.BlockSpec(memory_space=pltpu.SMEM)],
        out_specs=[vmem] * 3,
        scratch_shapes=kernel_scratch(),
        compiler_params=pltpu.CompilerParams(
            collective_id=1, has_side_effects=True, vmem_limit_bytes=56 * 1024 * 1024
        ),
        cost_estimate=pl.CostEstimate(flops=6 << 30, bytes_accessed=16 << 20, transcendentals=1 << 20),
    )(
        jnp.transpose(fields[0], (1, 2, 0)), weight, jnp.transpose(observed, (2, 1, 0)),
        jnp.asarray(margin_places(), jnp.bfloat16), jnp.asarray(edge_picks(), jnp.bfloat16),
        out_bias.reshape(1, COUT), widths.reshape(1, COUT), owner_start[0],
    )
    weight_grad, bias_grad = pl.pallas_call(
        finish_kernel,
        out_shape=[
            jax.ShapeDtypeStruct((TAPS * TAPS, COUT, CIN), jnp.float32),
            jax.ShapeDtypeStruct((1, COUT), jnp.float32),
        ],
        in_specs=[hbm],
        out_specs=[hbm, vmem],
        scratch_shapes=[
            pltpu.VMEM((TAPS, ROWS, LANES), jnp.bfloat16),
            pltpu.VMEM((TAPS * TAPS, COUT, CIN), jnp.float32),
            pltpu.SemaphoreType.DMA((TAPS + 1,)),
            pltpu.SemaphoreType.DMA((TAPS * TAPS,)),
        ],
        compiler_params=pltpu.CompilerParams(vmem_limit_bytes=58 * 1024 * 1024),
    )(summed)
    weight_grad = weight_grad.reshape(TAPS, TAPS, COUT, CIN)
    bias_grad = bias_grad.reshape(COUT)
    out_grad = jnp.transpose(grad, (2, 1, 0))[None]
    owned_score = owned.reshape(1, 1, CAP * LON_DEV)
    return (out_grad, owned_score, weight_grad, bias_grad)


def solution(mesh):
    in_specs = (P("member", None, None, "lon"), P(), P(), P(None, None, "lon"), P(), P("lon", None))
    out_specs = (P("member", None, None, "lon"), P("lon", "member", None), P(), P())
    return jax.shard_map(body, mesh=mesh, in_specs=in_specs, out_specs=out_specs, check_vma=False)
```

```python
import math

import jax
import jax.numpy as jnp
import numpy as np
from jax import lax
from jax.experimental import pallas as pl
from jax.experimental.pallas import tpu as pltpu
from jax.sharding import PartitionSpec as P

MESH = pl.DeviceIdType.MESH
MEMBERS = 8
GROUPS = 32
TAPS = 5
CIN = 641
COUT = 73
CHAN = 80
LAT = 16
LON_DEV = 45
PITCH = 48
POINTS = LAT * PITCH
CHUNK = 2 * PITCH
CAP = 6
TAP_ROWS = TAPS * CHAN
NT = (((1,), (1,)), ((), ()))
ROWS = 2048
LANES = 128
PARTS = 3
COLS = 768
WIDE = 640
PART_ROWS = (2048, 2048, 1024)
ORDERS = (("x", "y", "z"), ("y", "x", "z"), ("z", "x", "y"))


def position():
    member = lax.axis_index("member")
    lon = lax.axis_index("lon")
    return {
        "x": (lon // 16) * 2 + member % 2,
        "y": member // 2,
        "z": (lon // 2) % 8,
        "core": lon % 2,
    }


EXTENT = {"x": 4, "y": 4, "z": 8, "core": 2}


def device(at):
    return (at["y"] * 2 + at["x"] % 2, (at["x"] // 2) * 16 + at["z"] * 2 + at["core"])


def moved(at, axis, delta):
    there = dict(at)
    there[axis] = lax.rem(at[axis] + delta, EXTENT[axis])
    return there


def send(src, dst, send_sem, recv_sem, at):
    copy = pltpu.make_async_remote_copy(
        src_ref=src, dst_ref=dst, send_sem=send_sem, recv_sem=recv_sem,
        device_id=device(at), device_id_type=MESH,
    )
    copy.start()


def send_to(src, dst, send_sem, recv_sem, there):
    copy = pltpu.make_async_remote_copy(
        src_ref=src, dst_ref=dst, send_sem=send_sem, recv_sem=recv_sem,
        device_id=there, device_id_type=MESH,
    )
    copy.start()


def finish(ref, send_sem, recv_sem, at):
    copy = pltpu.make_async_remote_copy(
        src_ref=ref, dst_ref=ref, send_sem=send_sem, recv_sem=recv_sem,
        device_id=device(at), device_id_type=MESH,
    )
    return copy


def greet(at):
    barrier = pltpu.get_barrier_semaphore()
    count = 0
    for axis in ("core", "x", "y", "z"):
        for delta in range(1, EXTENT[axis]):
            pl.semaphore_signal(
                barrier, inc=1, device_id=device(moved(at, axis, delta)), device_id_type=MESH
            )
            count += 1
    member, lon = lax.axis_index("member"), lax.axis_index("lon")
    for delta in range(1, MEMBERS):
        there = (lax.rem(member + delta, MEMBERS), lon)
        pl.semaphore_signal(barrier, inc=1, device_id=there, device_id_type=MESH)
        count += 1
    for delta in (1, GROUPS - 1):
        there = (member, lax.rem(lon + delta, GROUPS))
        pl.semaphore_signal(barrier, inc=1, device_id=there, device_id_type=MESH)
        count += 1
    return barrier, count


def stage_rows(k):
    rows, sizes = PART_ROWS[k], []
    for axis in ORDERS[k][: 2 if k == 2 else 3]:
        rows //= EXTENT[axis]
        sizes.append(rows)
    return sizes


SIZES = [stage_rows(k) for k in range(PARTS)]


def place(at, out, k, row, rows):
    if k == 2:
        return out.at[4, pl.ds(pl.multiple_of(at["core"] * 1024 + row, 16), rows), :]
    return out.at[2 * at["core"] + k, pl.ds(pl.multiple_of(row, 16), rows), :]


def launch(at, k, s, cur, rxs, send_sems, recv_sems):
    axis, rows = ORDERS[k][s], SIZES[k][s]
    for delta in range(1, EXTENT[axis]):
        there = moved(at, axis, delta)
        source = cur[k][s].at[pl.ds(pl.multiple_of(there[axis] * rows, 16), rows)]
        send(source, rxs[k][s].at[delta - 1], send_sems.at[k, s + 1], recv_sems.at[k, s + 1], there)


def add_core(at, k, mine, core_rx, cur, send_sems, recv_sems):
    finish(core_rx[k], send_sems.at[k, 0], recv_sems.at[k, 0], at).wait_recv()
    step = 256

    def add(i, _):
        here = pl.ds(pl.multiple_of(i * step, step), step)
        if k == 2:
            own = mine[pl.ds(pl.multiple_of(at["core"] * 1024 + i * step, step), step), :]
        else:
            own = mine[k, here, :]
        cur[k][0][here, :] = (own + core_rx[k][here, :].astype(jnp.float32)).astype(jnp.bfloat16)
        return 0

    lax.fori_loop(0, PART_ROWS[k] // step, add, 0)


def gather(at, out, k, s, row, send_sems, recv_sems):
    axis = ORDERS[k][s]
    block = place(at, out, k, row, SIZES[k][s])
    for delta in range(1, EXTENT[axis]):
        send(block, block, send_sems.at[k, 4 + s], recv_sems.at[k, 4 + s], moved(at, axis, delta))


def spread(at, out, k, dy, dx, send_sem, recv_sem, there):
    first, second = ORDERS[k][0], ORDERS[k][1]
    row = lax.rem(at[first] + 4 - dx, 4) * SIZES[k][0] + lax.rem(at[second] + 4 - dy, 4) * SIZES[k][1]
    block = place(at, out, k, row, SIZES[k][1])
    if there is None:
        finish(block, send_sem, recv_sem, at).wait_recv()
    else:
        send(block, block, send_sem, recv_sem, there)


def all_reduce(at, out, core_rx, cur, rxs, shared, send_sems, recv_sems, mid_recv, far_recv):
    row = [0] * PARTS
    partner = moved(at, "core", 1)
    for s in range(3):
        for k in (2, 0, 1) if s == 2 else (0, 1, 2):
            if k == 2 and s == 2:
                finish(shared.at[0:3], send_sems.at[k, 3], recv_sems.at[k, 3], at).wait_recv()
                total = shared[0].astype(jnp.float32)
                for y in range(1, 4):
                    total = total + shared[y].astype(jnp.float32)
                place(at, out, k, row[k], 32)[...] = total.astype(jnp.bfloat16)
                gather(at, out, k, 1, row[k], send_sems, recv_sems)
                continue
            axis, rows = ORDERS[k][s], SIZES[k][s]
            finish(rxs[k][s], send_sems.at[k, s + 1], recv_sems.at[k, s + 1], at).wait_recv()
            row[k] = row[k] + at[axis] * rows
            base = pl.multiple_of(at[axis] * rows, 16)
            step = min(rows, 128)

            def add(i, _, k=k, s=s, axis=axis, base=base, step=step):
                total = cur[k][s][pl.ds(pl.multiple_of(base + i * step, 16), step), :].astype(jnp.float32)
                here = pl.ds(pl.multiple_of(i * step, 16), step)
                for slot in range(EXTENT[axis] - 1):
                    total = total + rxs[k][s][slot, here, :].astype(jnp.float32)
                total = total.astype(jnp.bfloat16)
                if k == 2 and s == 1:
                    shared[at["y"]] = total
                elif s == 2:
                    place(at, out, k, row[k], step)[...] = total
                else:
                    cur[k][s + 1][here, :] = total
                return 0

            if rows == step:
                add(0, 0)
            else:
                lax.fori_loop(0, rows // step, add, 0)
            if k == 2 and s == 1:
                for delta in range(1, 4):
                    own = shared.at[at["y"]]
                    send(own, own, send_sems.at[k, 3], recv_sems.at[k, 3], moved(at, "y", delta))
            elif s == 2:
                gather(at, out, k, 2, row[k], send_sems, recv_sems)
            else:
                launch(at, k, s + 1, cur, rxs, send_sems, recv_sems)
    def arrived(k, s):
        finish(rxs[k][s], send_sems.at[k, 4 + s], recv_sems.at[k, 4 + s], at).wait_recv()

    def onward(k, dy):
        first = ORDERS[k][0]
        for dx in (2, 1, 3):
            spread(at, out, k, dy, 0, send_sems.at[k, 4], far_recv.at[k, 4 * dx + dy], moved(at, first, dx))
        spread(at, out, k, dy, 0, send_sems.at[k, 7], recv_sems.at[k, 7], partner)

    arrived(2, 1)
    row[2] = row[2] - at["x"] * SIZES[2][1]
    gather(at, out, 2, 0, row[2], send_sems, recv_sems)
    for k in range(2):
        arrived(k, 2)
        for dy in (2, 1, 3):
            there = moved(at, ORDERS[k][1], dy)
            spread(at, out, k, 0, 0, send_sems.at[k, 5], mid_recv.at[k, dy], there)
        onward(k, 0)
    for dy in (1, 3, 2):
        for k in range(2):
            spread(at, out, k, dy, 0, send_sems.at[k, 5], mid_recv.at[k, dy], None)
            onward(k, dy)
    for dy in (0, 1, 3, 2):
        if dy == 2:
            arrived(2, 0)
            block = place(at, out, 2, 0, PART_ROWS[2])
            send(block, block, send_sems.at[2, 7], recv_sems.at[2, 7], partner)
        for dx in (1, 3, 2):
            for k in range(2):
                spread(at, out, k, dy, dx, send_sems.at[k, 4], far_recv.at[k, 4 * dx + dy], None)
                spread(at, out, k, dy, dx, send_sems.at[k, 7], recv_sems.at[k, 7], partner)
    for k in (2, 0, 1):
        finish(core_rx[k], send_sems.at[k, 7], recv_sems.at[k, 7], partner).wait_recv()
    for k in range(PARTS):
        finish(core_rx[k], send_sems.at[k, 0], recv_sems.at[k, 0], partner).wait_send()
        finish(core_rx[k], send_sems.at[k, 7], recv_sems.at[k, 7], partner).wait_send()
        for s in range(len(SIZES[k])):
            finish(rxs[k][s], send_sems.at[k, s + 1], recv_sems.at[k, s + 1], partner).wait_send()
            finish(rxs[k][s], send_sems.at[k, s + 4], recv_sems.at[k, s + 4], partner).wait_send()
    finish(shared.at[0:3], send_sems.at[2, 3], recv_sems.at[2, 3], partner).wait_send()


def reduce_scratch():
    shapes = [pltpu.VMEM((PART_ROWS[k], LANES), jnp.bfloat16) for k in range(PARTS)]
    for k in range(PARTS):
        rows = PART_ROWS[k]
        for size in SIZES[k]:
            shapes.append(pltpu.VMEM((rows, LANES), jnp.bfloat16))
            rows = size
    for k in range(PARTS):
        for axis, size in zip(ORDERS[k], SIZES[k]):
            shapes.append(pltpu.VMEM((EXTENT[axis] - 1, size, LANES), jnp.bfloat16))
    shapes.append(pltpu.VMEM((4, 32, LANES), jnp.bfloat16))
    shapes += [pltpu.SemaphoreType.DMA((PARTS, 8)), pltpu.SemaphoreType.DMA((PARTS, 8))]
    shapes += [pltpu.SemaphoreType.DMA((2, 4)), pltpu.SemaphoreType.DMA((2, 16))]
    return shapes


def edge_picks():
    picks = np.zeros((2, PITCH, (LAT + 4) * PITCH), np.float32)
    for side, first in ((0, LON_DEV - 2), (1, 0)):
        for i in range(LAT + 4):
            for h in range(2):
                picks[side, 2 * i + h, i * PITCH + first + h] = 1.0
    return picks.reshape(2 * PITCH, -1)


def margin_places():
    places = np.zeros((TAPS, 2, LAT, 2, LAT, PITCH), np.float32)
    for b in range(TAPS):
        for side, first in ((0, -2), (1, LON_DEV)):
            for h in range(2):
                j = first + h - b + 2
                if 0 <= j < LON_DEV:
                    for i in range(LAT):
                        places[b, side, i, h, i, j] = 1.0
    return places.reshape(TAPS, 4 * LAT, POINTS)


def stage_field(raw, x):
    lane = lax.broadcasted_iota(jnp.int32, (PITCH, LANES), 1)
    row = lax.broadcasted_iota(jnp.int32, (PITCH, LANES), 0)
    tail = jnp.where((lane == CIN - 640) & (row < LON_DEV), 1.0, 0.0).astype(jnp.bfloat16)
    zeros = jnp.zeros((16, COLS), jnp.bfloat16)

    def one(i, _):
        base = pl.multiple_of(i * PITCH, 16)
        x[pl.ds(base + 32, 16), :] = zeros
        x[pl.ds(base, PITCH), 640:COLS] = tail
        x[pl.ds(base, LON_DEV), 0:CIN] = raw[i]
        return 0

    lax.fori_loop(0, LAT + 4, one, 0)


def stage_columns(bias, widths, tile, vectors):
    tile[...] = jnp.ones((8, LANES), jnp.float32)
    tile[0:1, 0:COUT] = bias[...]
    tile[1:2, 0:COUT] = widths[...]
    vectors[:, 0:8] = jnp.transpose(tile[...])[0:CHAN, :]


def stage_target(observed, wide, target):
    spots = LON_DEV * LAT
    point = lax.broadcasted_iota(jnp.int32, (LANES, spots), 0)
    spot = lax.broadcasted_iota(jnp.int32, (LANES, spots), 1)
    second = (point >= PITCH).astype(jnp.int32)
    wanted = (point - PITCH * second) * LAT + 2 * lax.axis_index("member") + second
    chosen = ((spot == wanted) & (point < CHUNK)).astype(jnp.float32)
    wide[...] = jnp.zeros((LANES, LANES), jnp.float32)
    wide[:, 0:COUT] = jnp.dot(
        chosen, observed[...].reshape(spots, COUT),
        precision=lax.Precision.HIGHEST, preferred_element_type=jnp.float32,
    )
    target[...] = jnp.transpose(wide[...])[0:CHAN, :]


def write_gradient(packed, grad_out):
    spots = LON_DEV * LAT
    spot = lax.broadcasted_iota(jnp.int32, (spots, POINTS), 0)
    point = lax.broadcasted_iota(jnp.int32, (spots, POINTS), 1)
    wanted = (spot & (LAT - 1)) * PITCH + (spot >> 4)
    moves = jnp.where(point == wanted, 1.0, 0.0).astype(jnp.bfloat16)
    moved_grad = lax.dot_general(moves, packed[...], NT, preferred_element_type=jnp.float32)
    grad_out[...] = moved_grad.astype(jnp.bfloat16).reshape(LON_DEV, LAT, CHAN)[:, :, :COUT]


def stage_weight(w, staged):
    zeros = jnp.zeros((16, COLS), jnp.bfloat16)
    tail = jnp.zeros((64, COLS - 640), jnp.bfloat16)

    def one(a, _):
        for b in range(TAPS):
            base = pl.multiple_of(a * TAP_ROWS + b * CHAN, 16)
            staged[pl.ds(base + 64, 16), :] = zeros
            staged[pl.ds(base, 64), 640:COLS] = tail
            staged[pl.ds(base, COUT), 0:CIN] = w[a, b]
        return 0

    lax.fori_loop(0, TAPS, one, 0)


def forward_own(x, staged, taps):
    for n in range(3):
        lanes = slice(n * 256, n * 256 + 256)

        def one(a, total, n=n):
            rows = pl.ds(pl.multiple_of(a * PITCH + n * 256, 16), 256)
            left = staged[pl.ds(pl.multiple_of(a * TAP_ROWS, 16), TAP_ROWS), :]
            return total + lax.dot_general(left, x[rows, :], NT, preferred_element_type=jnp.float32)

        taps[:, lanes] = lax.fori_loop(0, TAPS, one, jnp.zeros((TAP_ROWS, 256), jnp.float32))


def stage_margin(halo, margin):
    left = halo[0].astype(jnp.float32)
    right = halo[1].astype(jnp.float32)
    for a in range(TAPS):
        margin[a, 0:32, :] = left[2 * a : 2 * a + 32, :].astype(jnp.bfloat16)
        margin[a, 32:64, :] = right[2 * a : 2 * a + 32, :].astype(jnp.bfloat16)


def forward_margin(margin, staged, edge_taps):
    def one(a, total):
        left = staged[pl.ds(pl.multiple_of(a * TAP_ROWS, 16), TAP_ROWS), :]
        return total + lax.dot_general(left, margin[a], NT, preferred_element_type=jnp.float32)

    edge_taps[...] = lax.fori_loop(0, TAPS, one, jnp.zeros((TAP_ROWS, 64), jnp.float32))


def convolved(taps, edge_taps, places, bias):
    total = jnp.broadcast_to(bias, (CHAN, POINTS))
    for b in range(TAPS):
        rows = slice(b * CHAN, b * CHAN + CHAN)
        part = taps[rows, :]
        total = total + (part if b == 2 else pltpu.roll(part, (2 - b) % POINTS, 1))
        if b != 2:
            total = total + jnp.dot(
                edge_taps[rows, :], places[b].astype(jnp.float32),
                precision=lax.Precision.HIGHEST, preferred_element_type=jnp.float32,
            )
    return total


def kernel_terms(values, target, vectors, gradients, score):
    lane = lax.broadcasted_iota(jnp.int32, (16, LANES), 1)
    real = (lane < LON_DEV) | ((lane >= PITCH) & (lane < PITCH + LON_DEV))

    def block(t, score_sum):
        rows = pl.ds(pl.multiple_of(t * 16, 16), 16)
        members = [values[m, rows, :].astype(jnp.float32) for m in range(MEMBERS)]
        width = vectors[rows, :][:, 1:2]
        inverse = jnp.broadcast_to(1.0 / (width * width), (16, LANES))
        half = -0.5 * inverse
        goal = target[rows, :]
        pulls = [jnp.zeros((16, LANES), jnp.float32) for _ in range(MEMBERS)]
        pair_sum = jnp.zeros((16, LANES), jnp.float32)
        for m in range(MEMBERS):
            for n in range(m + 1, MEMBERS):
                spread = members[m] - members[n]
                kernel_pair = jnp.exp(spread * spread * half)
                pair_sum = pair_sum + kernel_pair
                pull = kernel_pair * spread
                pulls[m] = pulls[m] + pull
                pulls[n] = pulls[n] - pull
        obs_sum = jnp.zeros((16, LANES), jnp.float32)
        for m in range(MEMBERS):
            misfit = members[m] - goal
            kernel_obs = jnp.exp(misfit * misfit * half)
            obs_sum = obs_sum + kernel_obs
            gradient = inverse * (misfit * kernel_obs - pulls[m] * (1.0 / MEMBERS))
            gradients[m, rows, :] = jnp.where(real, gradient, 0.0).astype(jnp.bfloat16)
        per_channel = (MEMBERS + 2.0 * pair_sum) * (1.0 / (2 * MEMBERS * MEMBERS)) - obs_sum * (1.0 / MEMBERS)
        channel = t * 16 + lax.broadcasted_iota(jnp.int32, (16, LANES), 0)
        return score_sum + jnp.where(channel < COUT, per_channel, 0.0)

    total = lax.fori_loop(0, CHAN // 16, block, jnp.zeros((16, LANES), jnp.float32))
    score[...] = jnp.broadcast_to(jnp.sum(total, axis=0, keepdims=True) * (1.0 / COUT), (8, LANES))


def stack_gradient(gathered, packed_grad, stacked, edge_stacked, places):
    grad = jnp.concatenate(
        [gathered[q].astype(jnp.float32)[:, :CHUNK] for q in range(MEMBERS)], axis=1
    )
    packed = grad.astype(jnp.bfloat16)
    packed_grad[...] = packed
    for b in range(TAPS):
        rows = slice(b * CHAN, b * CHAN + CHAN)
        if b == 2:
            stacked[rows, :] = packed
            edge_stacked[rows, :] = jnp.zeros((CHAN, 64), jnp.bfloat16)
        else:
            stacked[rows, :] = pltpu.roll(grad, (b - 2) % POINTS, 1).astype(jnp.bfloat16)
            edge = lax.dot_general(packed, places[b], NT, preferred_element_type=jnp.float32)
            edge_stacked[rows, :] = edge.astype(jnp.bfloat16)


def product(a, lanes, x, margin, stacked, edge_stacked):
    right = x[pl.ds(pl.multiple_of(a * PITCH, 16), POINTS), lanes]
    total = jnp.dot(stacked[...], right, preferred_element_type=jnp.float32)
    return total + jnp.dot(edge_stacked[...], margin[a, :, lanes], preferred_element_type=jnp.float32)


def shared_terms(x, margin, stacked, edge_stacked, fifth, fifth_sent, tails):
    def one(a, _):
        total = product(a, slice(512, 768), x, margin, stacked, edge_stacked)
        rows = pl.ds(pl.multiple_of(a * TAP_ROWS, 16), TAP_ROWS)
        fifth[rows, :] = total[:, :LANES]
        fifth_sent[rows, :] = total[:, :LANES].astype(jnp.bfloat16)
        tails[a, :, 0:TAP_ROWS] = jnp.transpose(total[:, LANES:])[0:8, :]
        return 0

    tails[...] = jnp.zeros((TAPS, 8, 512), jnp.float32)
    lax.fori_loop(0, TAPS, one, 0)
    spare = ROWS - TAPS * TAP_ROWS
    fifth[TAPS * TAP_ROWS : ROWS, :] = jnp.zeros((spare, LANES), jnp.float32)
    for n in range(TAPS + 1):
        a, channel = (n, 0) if n < TAPS else (2, 1)
        for q in range(4):
            row = TAPS * TAP_ROWS + 4 * n + q
            fifth[row : row + 1, :] = tails[a, channel : channel + 1, q * LANES : (q + 1) * LANES]
    fifth_sent[TAPS * TAP_ROWS : ROWS, :] = fifth[TAPS * TAP_ROWS : ROWS, :].astype(jnp.bfloat16)


def weight_terms(half, x, margin, stacked, edge_stacked, into):
    lanes = pl.ds(pl.multiple_of(half * 256, 256), 256)

    def one(a, _):
        total = product(a, lanes, x, margin, stacked, edge_stacked).astype(into.dtype)
        rows = pl.ds(pl.multiple_of(a * TAP_ROWS, 16), TAP_ROWS)
        for k in range(2):
            into[k, rows, :] = total[:, k * LANES : (k + 1) * LANES]
        return 0

    lax.fori_loop(0, TAPS, one, 0)
    first = TAPS * TAP_ROWS
    for k in range(2):
        into[k, first:ROWS, :] = jnp.zeros((ROWS - first, LANES), into.dtype)


def own_scores(starts, score_rx, owned):
    lane = lax.broadcasted_iota(jnp.int32, (8, LANES), 1)
    row = lax.broadcasted_iota(jnp.int32, (8, LANES), 0)
    me = lax.axis_index("member")
    first, count = starts[me], starts[me + 1] - starts[me]
    wanted = jnp.where(row < count, first + row, -1)
    total = jnp.zeros((8, LANES), jnp.float32)
    for q in range(MEMBERS):
        pair = score_rx[q]
        low = jnp.where(lane < LON_DEV, pair, 0.0)
        high = jnp.where(lane < LON_DEV, pltpu.roll(pair, LANES - PITCH, 1), 0.0)
        total = total + jnp.where(wanted == 2 * q, low, 0.0) + jnp.where(wanted == 2 * q + 1, high, 0.0)
    owned[...] = jnp.concatenate([total[s : s + 1, 0:LON_DEV] for s in range(CAP)], axis=1)


def whole_kernel(
    raw_hbm, w_hbm, observed_hbm, places_hbm, picks_hbm, bias, widths, starts, out, grad_out, owned, *scratch
):
    raw, w, observed, places, picks, x, tile, wide, vectors, target, packed, local = scratch[:12]
    scratch = scratch[12:]
    (
        staged, edges, halo, margin, taps, edge_taps, to_score, values, gradients, gathered, score, score_rx,
        stacked, edge_stacked, theirs, mine, fifth, fifth_sent, tails, near_send, near_recv,
    ) = scratch[:21]
    core_rx, rest = scratch[21:24], scratch[24:]
    cur = [rest[3 * k : 3 * k + 3] for k in range(PARTS)]
    rxs = [rest[8 + 3 * k : 11 + 3 * k] for k in range(PARTS)]
    shared, send_sems, recv_sems, mid_recv, far_recv = rest[16:21]
    at = position()
    member, lon = lax.axis_index("member"), lax.axis_index("lon")
    ahead = (member, lax.rem(lon + 1, GROUPS))
    behind = (member, lax.rem(lon + GROUPS - 1, GROUPS))
    others = [lax.rem(member + delta, MEMBERS) for delta in range(1, MEMBERS)]

    loads = [
        pltpu.make_async_copy(source, target_ref, local.at[n])
        for n, (source, target_ref) in enumerate(
            ((raw_hbm, raw), (picks_hbm, picks), (w_hbm, w), (places_hbm, places), (observed_hbm, observed))
        )
    ]
    for load in loads:
        load.start()
    barrier, count = greet(at)
    stage_columns(bias, widths, tile, vectors)
    loads[0].wait()
    stage_field(raw, x)
    loads[1].wait()
    edge = jnp.dot(picks[...], x[...], preferred_element_type=jnp.float32).astype(jnp.bfloat16)
    edges[0] = edge[:PITCH]
    edges[1] = edge[PITCH:]
    loads[2].wait()
    stage_weight(w, staged)
    pl.semaphore_wait(barrier, count)
    send_to(edges.at[0], halo.at[0], near_send.at[0], near_recv.at[0], ahead)
    send_to(edges.at[1], halo.at[1], near_send.at[1], near_recv.at[1], behind)
    forward_own(x, staged, taps)
    loads[3].wait()
    loads[4].wait()
    stage_target(observed, wide, target)
    finish(halo.at[0], near_send.at[0], near_recv.at[0], at).wait()
    finish(halo.at[1], near_send.at[1], near_recv.at[1], at).wait()
    stage_margin(halo, margin)
    forward_margin(margin, staged, edge_taps)
    outputs = convolved(taps, edge_taps, places, vectors[...][:, 0:1])
    for q in range(MEMBERS):
        to_score[q, :, 0:CHUNK] = outputs[:, q * CHUNK : (q + 1) * CHUNK].astype(jnp.bfloat16)
        to_score[q, :, CHUNK:LANES] = jnp.zeros((CHAN, LANES - CHUNK), jnp.bfloat16)
    for there in others:
        send_to(to_score.at[there], values.at[member], near_send.at[2], near_recv.at[2], (there, lon))
    values[member] = to_score[member]
    finish(values.at[0:7], near_send.at[2], near_recv.at[2], at).wait_recv()
    kernel_terms(values, target, vectors, gradients, score)
    for there in others:
        send_to(gradients.at[there], gathered.at[member], near_send.at[3], near_recv.at[3], (there, lon))
    for there in others:
        send_to(score, score_rx.at[member], near_send.at[4], near_recv.at[4], (there, lon))
    gathered[member] = gradients[member]
    score_rx[member] = score[...]
    finish(gathered.at[0:7], near_send.at[3], near_recv.at[3], at).wait_recv()
    stack_gradient(gathered, packed, stacked, edge_stacked, places)
    core, partner = at["core"], moved(at, "core", 1)
    weight_terms(1 - core, x, margin, stacked, edge_stacked, theirs)
    for k in range(2):
        send(theirs.at[k], core_rx[k], send_sems.at[k, 0], recv_sems.at[k, 0], partner)
    shared_terms(x, margin, stacked, edge_stacked, fifth, fifth_sent, tails)
    source = fifth_sent.at[pl.ds(pl.multiple_of((1 - core) * 1024, 16), 1024)]
    send(source, core_rx[2], send_sems.at[2, 0], recv_sems.at[2, 0], partner)
    weight_terms(core, x, margin, stacked, edge_stacked, mine)
    for k, own in ((0, mine), (1, mine), (2, fifth)):
        add_core(at, k, own, core_rx, cur, send_sems, recv_sems)
        launch(at, k, 0, cur, rxs, send_sems, recv_sems)
    write_gradient(packed, grad_out)
    finish(score_rx.at[0:7], near_send.at[4], near_recv.at[4], at).wait_recv()
    own_scores(starts, score_rx, owned)
    all_reduce(at, out, core_rx, cur, rxs, shared, send_sems, recv_sems, mid_recv, far_recv)
    finish(values.at[0:7], near_send.at[2], near_recv.at[2], at).wait_send()
    finish(gathered.at[0:7], near_send.at[3], near_recv.at[3], at).wait_send()
    finish(score_rx.at[0:7], near_send.at[4], near_recv.at[4], at).wait_send()


def kernel_scratch():
    chunk = (MEMBERS, CHAN, LANES)
    return [
        pltpu.VMEM((LAT + 4, LON_DEV, CIN), jnp.bfloat16),
        pltpu.VMEM((TAPS, TAPS, COUT, CIN), jnp.bfloat16),
        pltpu.VMEM((LON_DEV, LAT, COUT), jnp.float32),
        pltpu.VMEM((TAPS, 4 * LAT, POINTS), jnp.bfloat16),
        pltpu.VMEM((2 * PITCH, (LAT + 4) * PITCH), jnp.bfloat16),
        pltpu.VMEM(((LAT + 4) * PITCH, COLS), jnp.bfloat16),
        pltpu.VMEM((8, LANES), jnp.float32),
        pltpu.VMEM((LANES, LANES), jnp.float32),
        pltpu.VMEM((CHAN, LANES), jnp.float32),
        pltpu.VMEM((CHAN, LANES), jnp.float32),
        pltpu.VMEM((CHAN, POINTS), jnp.bfloat16),
        pltpu.SemaphoreType.DMA((5,)),
        pltpu.VMEM((TAPS * TAP_ROWS, COLS), jnp.bfloat16),
        pltpu.VMEM((2, PITCH, COLS), jnp.bfloat16),
        pltpu.VMEM((2, PITCH, COLS), jnp.bfloat16),
        pltpu.VMEM((TAPS, 64, COLS), jnp.bfloat16),
        pltpu.VMEM((TAP_ROWS, POINTS), jnp.float32),
        pltpu.VMEM((TAP_ROWS, 64), jnp.float32),
        pltpu.VMEM(chunk, jnp.bfloat16),
        pltpu.VMEM(chunk, jnp.bfloat16),
        pltpu.VMEM(chunk, jnp.bfloat16),
        pltpu.VMEM(chunk, jnp.bfloat16),
        pltpu.VMEM((8, LANES), jnp.float32),
        pltpu.VMEM((MEMBERS, 8, LANES), jnp.float32),
        pltpu.VMEM((TAP_ROWS, POINTS), jnp.bfloat16),
        pltpu.VMEM((TAP_ROWS, 64), jnp.bfloat16),
        pltpu.VMEM((2, ROWS, LANES), jnp.bfloat16),
        pltpu.VMEM((2, ROWS, LANES), jnp.float32),
        pltpu.VMEM((ROWS, LANES), jnp.float32),
        pltpu.VMEM((ROWS, LANES), jnp.bfloat16),
        pltpu.VMEM((TAPS, 8, 512), jnp.float32),
        pltpu.SemaphoreType.DMA((5,)),
        pltpu.SemaphoreType.DMA((5,)),
    ] + reduce_scratch()


def finish_kernel(
    summed, grad_in, owned_in, weight_grad, grad_out, owned_out, bias_grad,
    main, wide, grad_here, owned_here, in_sems, out_sems, pass_sems,
):
    factor = 1.0 / math.sqrt(MEMBERS * LAT * LON_DEV * GROUPS)
    first = TAPS * TAP_ROWS
    tail = (TAPS - 1, slice(first, ROWS))
    loads = [pltpu.make_async_copy(summed.at[tail], main.at[tail], in_sems.at[TAPS])]
    for a in range(TAPS):
        rows = (slice(None), slice(a * TAP_ROWS, (a + 1) * TAP_ROWS))
        loads.append(pltpu.make_async_copy(summed.at[rows], main.at[rows], in_sems.at[a]))
    taken = [
        pltpu.make_async_copy(grad_in, grad_here, pass_sems.at[0]),
        pltpu.make_async_copy(owned_in, owned_here, pass_sems.at[1]),
    ]
    for copy in loads + taken:
        copy.start()
    loads[0].wait()
    more = main[TAPS - 1, first:ROWS, :].astype(jnp.float32) * factor
    bias = jnp.concatenate([more[4 * TAPS + q : 4 * TAPS + q + 1, :] for q in range(4)], axis=1)
    bias_grad[...] = bias[:, 2 * CHAN : 2 * CHAN + COUT]
    stores = []
    for a in range(TAPS):
        last = jnp.concatenate([more[4 * a + q : 4 * a + q + 1, :] for q in range(4)], axis=1)
        last = jnp.transpose(jnp.broadcast_to(last, (8, 512)))
        loads[a + 1].wait()
        for b in range(TAPS):
            base, n = a * TAP_ROWS + b * CHAN, a * TAPS + b
            for block in range(TAPS):
                part = main[block, base : base + CHAN, :].astype(jnp.float32) * factor
                wide[n, :, block * LANES : (block + 1) * LANES] = part[:COUT]
            wide[n, :, WIDE:CIN] = last[b * CHAN : b * CHAN + COUT, 0:1]
            stores.append(pltpu.make_async_copy(wide.at[n], weight_grad.at[n], out_sems.at[n]))
            stores[-1].start()
    given = [
        pltpu.make_async_copy(grad_here, grad_out, pass_sems.at[2]),
        pltpu.make_async_copy(owned_here, owned_out, pass_sems.at[3]),
    ]
    for source, target in zip(taken, given):
        source.wait()
        target.start()
    for copy in stores + given:
        copy.wait()


def body(fields, weight, out_bias, observed, widths, owner_start):
    vmem = pl.BlockSpec(memory_space=pltpu.VMEM)
    hbm = pl.BlockSpec(memory_space=pl.ANY)
    summed, grad, owned = pl.pallas_call(
        whole_kernel,
        out_shape=[
            jax.ShapeDtypeStruct((TAPS, ROWS, LANES), jnp.bfloat16),
            jax.ShapeDtypeStruct((LON_DEV, LAT, COUT), jnp.bfloat16),
            jax.ShapeDtypeStruct((1, CAP * LON_DEV), jnp.float32),
        ],
        in_specs=[hbm] * 5 + [vmem] * 2 + [pl.BlockSpec(memory_space=pltpu.SMEM)],
        out_specs=[vmem] * 3,
        scratch_shapes=kernel_scratch(),
        compiler_params=pltpu.CompilerParams(
            collective_id=1, has_side_effects=True, vmem_limit_bytes=56 * 1024 * 1024
        ),
        cost_estimate=pl.CostEstimate(flops=6 << 30, bytes_accessed=16 << 20, transcendentals=1 << 20),
    )(
        jnp.transpose(fields[0], (1, 2, 0)), weight, jnp.transpose(observed, (2, 1, 0)),
        jnp.asarray(margin_places(), jnp.bfloat16), jnp.asarray(edge_picks(), jnp.bfloat16),
        out_bias.reshape(1, COUT), widths.reshape(1, COUT), owner_start[0],
    )
    weight_grad, grad, owned, bias_grad = pl.pallas_call(
        finish_kernel,
        out_shape=[
            jax.ShapeDtypeStruct((TAPS * TAPS, COUT, CIN), jnp.float32),
            jax.ShapeDtypeStruct((LON_DEV, LAT, COUT), jnp.bfloat16),
            jax.ShapeDtypeStruct((1, CAP * LON_DEV), jnp.float32),
            jax.ShapeDtypeStruct((1, COUT), jnp.float32),
        ],
        in_specs=[hbm] * 3,
        out_specs=[hbm] * 3 + [vmem],
        scratch_shapes=[
            pltpu.VMEM((TAPS, ROWS, LANES), jnp.bfloat16),
            pltpu.VMEM((TAPS * TAPS, COUT, CIN), jnp.float32),
            pltpu.VMEM((LON_DEV, LAT, COUT), jnp.bfloat16),
            pltpu.VMEM((1, CAP * LON_DEV), jnp.float32),
            pltpu.SemaphoreType.DMA((TAPS + 1,)),
            pltpu.SemaphoreType.DMA((TAPS * TAPS,)),
            pltpu.SemaphoreType.DMA((4,)),
        ],
        compiler_params=pltpu.CompilerParams(vmem_limit_bytes=58 * 1024 * 1024),
    )(summed, grad, owned)
    weight_grad = weight_grad.reshape(TAPS, TAPS, COUT, CIN)
    bias_grad = bias_grad.reshape(COUT)
    out_grad = jnp.transpose(grad, (2, 1, 0))[None]
    owned_score = owned.reshape(1, 1, CAP * LON_DEV)
    return (out_grad, owned_score, weight_grad, bias_grad)


def solution(mesh):
    in_specs = (P("member", None, None, "lon"), P(), P(), P(None, None, "lon"), P(), P("lon", None))
    out_specs = (P("member", None, None, "lon"), P("lon", "member", None), P(), P())
    return jax.shard_map(body, mesh=mesh, in_specs=in_specs, out_specs=out_specs, check_vma=False)
```

```python
import math

import jax
import jax.numpy as jnp
import numpy as np
from jax import lax
from jax.experimental import pallas as pl
from jax.experimental.pallas import tpu as pltpu
from jax.sharding import PartitionSpec as P

MESH = pl.DeviceIdType.MESH
MEMBERS = 8
GROUPS = 32
TAPS = 5
CIN = 641
COUT = 73
CHAN = 80
LAT = 16
LON_DEV = 45
PITCH = 48
POINTS = LAT * PITCH
CHUNK = 2 * PITCH
CAP = 6
TAP_ROWS = TAPS * CHAN
NT = (((1,), (1,)), ((), ()))
ROWS = 2048
LANES = 128
PARTS = 3
COLS = 768
WIDE = 640
PART_ROWS = (2048, 2048, 1024)
ORDERS = (("x", "y", "z"), ("y", "x", "z"), ("z", "x", "y"))


def position():
    member = lax.axis_index("member")
    lon = lax.axis_index("lon")
    return {
        "x": (lon // 16) * 2 + member % 2,
        "y": member // 2,
        "z": (lon // 2) % 8,
        "core": lon % 2,
    }


EXTENT = {"x": 4, "y": 4, "z": 8, "core": 2}


def device(at):
    return (at["y"] * 2 + at["x"] % 2, (at["x"] // 2) * 16 + at["z"] * 2 + at["core"])


def moved(at, axis, delta):
    there = dict(at)
    there[axis] = lax.rem(at[axis] + delta, EXTENT[axis])
    return there


def send(src, dst, send_sem, recv_sem, at):
    copy = pltpu.make_async_remote_copy(
        src_ref=src, dst_ref=dst, send_sem=send_sem, recv_sem=recv_sem,
        device_id=device(at), device_id_type=MESH,
    )
    copy.start()


def send_to(src, dst, send_sem, recv_sem, there):
    copy = pltpu.make_async_remote_copy(
        src_ref=src, dst_ref=dst, send_sem=send_sem, recv_sem=recv_sem,
        device_id=there, device_id_type=MESH,
    )
    copy.start()


def finish(ref, send_sem, recv_sem, at):
    copy = pltpu.make_async_remote_copy(
        src_ref=ref, dst_ref=ref, send_sem=send_sem, recv_sem=recv_sem,
        device_id=device(at), device_id_type=MESH,
    )
    return copy


def greet(at):
    barrier = pltpu.get_barrier_semaphore()
    count = 0
    for axis in ("core", "x", "y", "z"):
        for delta in range(1, EXTENT[axis]):
            pl.semaphore_signal(
                barrier, inc=1, device_id=device(moved(at, axis, delta)), device_id_type=MESH
            )
            count += 1
    member, lon = lax.axis_index("member"), lax.axis_index("lon")
    for delta in range(1, MEMBERS):
        there = (lax.rem(member + delta, MEMBERS), lon)
        pl.semaphore_signal(barrier, inc=1, device_id=there, device_id_type=MESH)
        count += 1
    for delta in (1, GROUPS - 1):
        there = (member, lax.rem(lon + delta, GROUPS))
        pl.semaphore_signal(barrier, inc=1, device_id=there, device_id_type=MESH)
        count += 1
    return barrier, count


def stage_rows(k):
    rows, sizes = PART_ROWS[k], []
    for axis in ORDERS[k][: 2 if k == 2 else 3]:
        rows //= EXTENT[axis]
        sizes.append(rows)
    return sizes


SIZES = [stage_rows(k) for k in range(PARTS)]


def place(at, out, k, row, rows):
    if k == 2:
        return out.at[4, pl.ds(pl.multiple_of(at["core"] * 1024 + row, 16), rows), :]
    return out.at[2 * at["core"] + k, pl.ds(pl.multiple_of(row, 16), rows), :]


def launch(at, k, s, cur, rxs, send_sems, recv_sems):
    axis, rows = ORDERS[k][s], SIZES[k][s]
    for delta in range(1, EXTENT[axis]):
        there = moved(at, axis, delta)
        source = cur[k][s].at[pl.ds(pl.multiple_of(there[axis] * rows, 16), rows)]
        send(source, rxs[k][s].at[delta - 1], send_sems.at[k, s + 1], recv_sems.at[k, s + 1], there)


def launch_pieces(at, k, cur, rxs, send_sems, piece_recv):
    first, second = ORDERS[k][0], ORDERS[k][1]
    rows, piece = SIZES[k][0], SIZES[k][1]
    for dy in (2, 1, 3, 0):
        for dx in (2, 1, 3):
            there = moved(at, first, dx)
            row = there[first] * rows + moved(at, second, dy)[second] * piece
            source = cur[k][0].at[pl.ds(pl.multiple_of(row, 16), piece)]
            into = rxs[k][0].at[dx - 1, dy * piece : (dy + 1) * piece]
            send(source, into, send_sems.at[k, 1], piece_recv.at[k, 4 * dx + dy], there)


def pass_piece(at, k, dy, cur, rxs, send_sems, recv_sems, piece_recv):
    first, second = ORDERS[k][0], ORDERS[k][1]
    rows, piece = SIZES[k][0], SIZES[k][1]
    there = moved(at, second, dy)
    total = cur[k][0][
        pl.ds(pl.multiple_of(at[first] * rows + there[second] * piece, 16), piece), :
    ].astype(jnp.float32)
    for dx in (1, 3, 2):
        landed = rxs[k][0].at[dx - 1, dy * piece : (dy + 1) * piece]
        finish(landed, send_sems.at[k, 1], piece_recv.at[k, 4 * dx + dy], at).wait_recv()
        total = total + landed[...].astype(jnp.float32)
    here = pl.ds(pl.multiple_of(there[second] * piece, 16), piece)
    cur[k][1][here, :] = total.astype(jnp.bfloat16)
    if dy:
        send(cur[k][1].at[here], rxs[k][1].at[dy - 1], send_sems.at[k, 2], recv_sems.at[k, 2], there)


def add_core(at, k, mine, core_rx, cur, send_sems, recv_sems):
    finish(core_rx[k], send_sems.at[k, 0], recv_sems.at[k, 0], at).wait_recv()
    step = 256

    def add(i, _):
        here = pl.ds(pl.multiple_of(i * step, step), step)
        if k == 2:
            own = mine[pl.ds(pl.multiple_of(at["core"] * 1024 + i * step, step), step), :]
        else:
            own = mine[k, here, :]
        cur[k][0][here, :] = (own + core_rx[k][here, :].astype(jnp.float32)).astype(jnp.bfloat16)
        return 0

    lax.fori_loop(0, PART_ROWS[k] // step, add, 0)


def gather(at, out, k, s, row, send_sems, recv_sems):
    axis = ORDERS[k][s]
    block = place(at, out, k, row, SIZES[k][s])
    for delta in range(1, EXTENT[axis]):
        send(block, block, send_sems.at[k, 4 + s], recv_sems.at[k, 4 + s], moved(at, axis, delta))


def spread(at, out, k, dy, dx, send_sem, recv_sem, there):
    first, second = ORDERS[k][0], ORDERS[k][1]
    row = lax.rem(at[first] + 4 - dx, 4) * SIZES[k][0] + lax.rem(at[second] + 4 - dy, 4) * SIZES[k][1]
    block = place(at, out, k, row, SIZES[k][1])
    if there is None:
        finish(block, send_sem, recv_sem, at).wait_recv()
    else:
        send(block, block, send_sem, recv_sem, there)


def all_reduce(at, out, core_rx, cur, rxs, shared, send_sems, recv_sems, mid_recv, far_recv, piece_recv):
    row = [0] * PARTS
    partner = moved(at, "core", 1)
    for s in range(3):
        for k in (2, 0, 1) if s == 2 else (0, 1, 2):
            if k == 2 and s == 2:
                finish(shared.at[0:3], send_sems.at[k, 3], recv_sems.at[k, 3], at).wait_recv()
                total = shared[0].astype(jnp.float32)
                for y in range(1, 4):
                    total = total + shared[y].astype(jnp.float32)
                place(at, out, k, row[k], 32)[...] = total.astype(jnp.bfloat16)
                gather(at, out, k, 1, row[k], send_sems, recv_sems)
                continue
            if s == 0 and k < 2:
                row[k] = row[k] + at[ORDERS[k][0]] * SIZES[k][0]
                if k == 1:
                    for dy in (2, 1, 3, 0):
                        for part in range(2):
                            pass_piece(at, part, dy, cur, rxs, send_sems, recv_sems, piece_recv)
                continue
            axis, rows = ORDERS[k][s], SIZES[k][s]
            finish(rxs[k][s], send_sems.at[k, s + 1], recv_sems.at[k, s + 1], at).wait_recv()
            row[k] = row[k] + at[axis] * rows
            base = pl.multiple_of(at[axis] * rows, 16)
            step = min(rows, 128)

            def add(i, _, k=k, s=s, axis=axis, base=base, step=step):
                total = cur[k][s][pl.ds(pl.multiple_of(base + i * step, 16), step), :].astype(jnp.float32)
                here = pl.ds(pl.multiple_of(i * step, 16), step)
                for slot in range(EXTENT[axis] - 1):
                    total = total + rxs[k][s][slot, here, :].astype(jnp.float32)
                total = total.astype(jnp.bfloat16)
                if k == 2 and s == 1:
                    shared[at["y"]] = total
                elif s == 2:
                    place(at, out, k, row[k], step)[...] = total
                else:
                    cur[k][s + 1][here, :] = total
                return 0

            if rows == step:
                add(0, 0)
            else:
                lax.fori_loop(0, rows // step, add, 0)
            if k == 2 and s == 1:
                for delta in range(1, 4):
                    own = shared.at[at["y"]]
                    send(own, own, send_sems.at[k, 3], recv_sems.at[k, 3], moved(at, "y", delta))
            elif s == 2:
                gather(at, out, k, 2, row[k], send_sems, recv_sems)
            else:
                launch(at, k, s + 1, cur, rxs, send_sems, recv_sems)
    def arrived(k, s):
        finish(rxs[k][s], send_sems.at[k, 4 + s], recv_sems.at[k, 4 + s], at).wait_recv()

    def onward(k, dy):
        first = ORDERS[k][0]
        for dx in (2, 1, 3):
            spread(at, out, k, dy, 0, send_sems.at[k, 4], far_recv.at[k, 4 * dx + dy], moved(at, first, dx))
        spread(at, out, k, dy, 0, send_sems.at[k, 7], recv_sems.at[k, 7], partner)

    arrived(2, 1)
    row[2] = row[2] - at["x"] * SIZES[2][1]
    gather(at, out, 2, 0, row[2], send_sems, recv_sems)
    for k in range(2):
        arrived(k, 2)
        for dy in (2, 1, 3):
            there = moved(at, ORDERS[k][1], dy)
            spread(at, out, k, 0, 0, send_sems.at[k, 5], mid_recv.at[k, dy], there)
        onward(k, 0)
    for dy in (1, 3, 2):
        for k in range(2):
            spread(at, out, k, dy, 0, send_sems.at[k, 5], mid_recv.at[k, dy], None)
            onward(k, dy)
    for dy in (0, 1, 3, 2):
        if dy == 2:
            arrived(2, 0)
            block = place(at, out, 2, 0, PART_ROWS[2])
            send(block, block, send_sems.at[2, 7], recv_sems.at[2, 7], partner)
        for dx in (1, 3, 2):
            for k in range(2):
                spread(at, out, k, dy, dx, send_sems.at[k, 4], far_recv.at[k, 4 * dx + dy], None)
                spread(at, out, k, dy, dx, send_sems.at[k, 7], recv_sems.at[k, 7], partner)
    for k in (2, 0, 1):
        finish(core_rx[k], send_sems.at[k, 7], recv_sems.at[k, 7], partner).wait_recv()
    for k in range(PARTS):
        finish(core_rx[k], send_sems.at[k, 0], recv_sems.at[k, 0], partner).wait_send()
        finish(core_rx[k], send_sems.at[k, 7], recv_sems.at[k, 7], partner).wait_send()
        for s in range(len(SIZES[k])):
            finish(rxs[k][s], send_sems.at[k, s + 1], recv_sems.at[k, s + 1], partner).wait_send()
            finish(rxs[k][s], send_sems.at[k, s + 4], recv_sems.at[k, s + 4], partner).wait_send()
    finish(shared.at[0:3], send_sems.at[2, 3], recv_sems.at[2, 3], partner).wait_send()


def reduce_scratch():
    shapes = [pltpu.VMEM((PART_ROWS[k], LANES), jnp.bfloat16) for k in range(PARTS)]
    for k in range(PARTS):
        rows = PART_ROWS[k]
        for size in SIZES[k]:
            shapes.append(pltpu.VMEM((rows, LANES), jnp.bfloat16))
            rows = size
    for k in range(PARTS):
        for axis, size in zip(ORDERS[k], SIZES[k]):
            shapes.append(pltpu.VMEM((EXTENT[axis] - 1, size, LANES), jnp.bfloat16))
    shapes.append(pltpu.VMEM((4, 32, LANES), jnp.bfloat16))
    shapes += [pltpu.SemaphoreType.DMA((PARTS, 8)), pltpu.SemaphoreType.DMA((PARTS, 8))]
    shapes += [pltpu.SemaphoreType.DMA((2, 4)), pltpu.SemaphoreType.DMA((2, 16))]
    shapes.append(pltpu.SemaphoreType.DMA((2, 16)))
    return shapes


def edge_picks():
    picks = np.zeros((2, PITCH, (LAT + 4) * PITCH), np.float32)
    for side, first in ((0, LON_DEV - 2), (1, 0)):
        for i in range(LAT + 4):
            for h in range(2):
                picks[side, 2 * i + h, i * PITCH + first + h] = 1.0
    return picks.reshape(2 * PITCH, -1)


def margin_places():
    places = np.zeros((TAPS, 2, LAT, 2, LAT, PITCH), np.float32)
    for b in range(TAPS):
        for side, first in ((0, -2), (1, LON_DEV)):
            for h in range(2):
                j = first + h - b + 2
                if 0 <= j < LON_DEV:
                    for i in range(LAT):
                        places[b, side, i, h, i, j] = 1.0
    return places.reshape(TAPS, 4 * LAT, POINTS)


def stage_field(raw, x):
    lane = lax.broadcasted_iota(jnp.int32, (PITCH, LANES), 1)
    row = lax.broadcasted_iota(jnp.int32, (PITCH, LANES), 0)
    tail = jnp.where((lane == CIN - 640) & (row < LON_DEV), 1.0, 0.0).astype(jnp.bfloat16)
    zeros = jnp.zeros((16, COLS), jnp.bfloat16)

    def one(i, _):
        base = pl.multiple_of(i * PITCH, 16)
        x[pl.ds(base + 32, 16), :] = zeros
        x[pl.ds(base, PITCH), 640:COLS] = tail
        x[pl.ds(base, LON_DEV), 0:CIN] = raw[i]
        return 0

    lax.fori_loop(0, LAT + 4, one, 0)


def stage_columns(bias, widths, tile, vectors):
    tile[...] = jnp.ones((8, LANES), jnp.float32)
    tile[0:1, 0:COUT] = bias[...]
    tile[1:2, 0:COUT] = widths[...]
    vectors[:, 0:8] = jnp.transpose(tile[...])[0:CHAN, :]


def stage_target(observed, wide, target):
    spots = LON_DEV * LAT
    point = lax.broadcasted_iota(jnp.int32, (LANES, spots), 0)
    spot = lax.broadcasted_iota(jnp.int32, (LANES, spots), 1)
    second = (point >= PITCH).astype(jnp.int32)
    wanted = (point - PITCH * second) * LAT + 2 * lax.axis_index("member") + second
    chosen = ((spot == wanted) & (point < CHUNK)).astype(jnp.float32)
    wide[...] = jnp.zeros((LANES, LANES), jnp.float32)
    wide[:, 0:COUT] = jnp.dot(
        chosen, observed[...].reshape(spots, COUT),
        precision=lax.Precision.HIGHEST, preferred_element_type=jnp.float32,
    )
    target[...] = jnp.transpose(wide[...])[0:CHAN, :]


def write_gradient(packed, grad_out):
    spots = LON_DEV * LAT
    spot = lax.broadcasted_iota(jnp.int32, (spots, POINTS), 0)
    point = lax.broadcasted_iota(jnp.int32, (spots, POINTS), 1)
    wanted = (spot & (LAT - 1)) * PITCH + (spot >> 4)
    moves = jnp.where(point == wanted, 1.0, 0.0).astype(jnp.bfloat16)
    moved_grad = lax.dot_general(moves, packed[...], NT, preferred_element_type=jnp.float32)
    grad_out[...] = moved_grad.astype(jnp.bfloat16).reshape(LON_DEV, LAT, CHAN)[:, :, :COUT]


def stage_weight(w, staged):
    zeros = jnp.zeros((16, COLS), jnp.bfloat16)
    tail = jnp.zeros((64, COLS - 640), jnp.bfloat16)

    def one(a, _):
        for b in range(TAPS):
            base = pl.multiple_of(a * TAP_ROWS + b * CHAN, 16)
            staged[pl.ds(base + 64, 16), :] = zeros
            staged[pl.ds(base, 64), 640:COLS] = tail
            staged[pl.ds(base, COUT), 0:CIN] = w[a, b]
        return 0

    lax.fori_loop(0, TAPS, one, 0)


def forward_own(x, staged, taps):
    for n in range(3):
        lanes = slice(n * 256, n * 256 + 256)

        def one(a, total, n=n):
            rows = pl.ds(pl.multiple_of(a * PITCH + n * 256, 16), 256)
            left = staged[pl.ds(pl.multiple_of(a * TAP_ROWS, 16), TAP_ROWS), :]
            return total + lax.dot_general(left, x[rows, :], NT, preferred_element_type=jnp.float32)

        taps[:, lanes] = lax.fori_loop(0, TAPS, one, jnp.zeros((TAP_ROWS, 256), jnp.float32))


def stage_margin(halo, margin):
    left = halo[0].astype(jnp.float32)
    right = halo[1].astype(jnp.float32)
    for a in range(TAPS):
        margin[a, 0:32, :] = left[2 * a : 2 * a + 32, :].astype(jnp.bfloat16)
        margin[a, 32:64, :] = right[2 * a : 2 * a + 32, :].astype(jnp.bfloat16)


def forward_margin(margin, staged, edge_taps):
    def one(a, total):
        left = staged[pl.ds(pl.multiple_of(a * TAP_ROWS, 16), TAP_ROWS), :]
        return total + lax.dot_general(left, margin[a], NT, preferred_element_type=jnp.float32)

    edge_taps[...] = lax.fori_loop(0, TAPS, one, jnp.zeros((TAP_ROWS, 64), jnp.float32))


def convolved(taps, edge_taps, places, bias):
    total = jnp.broadcast_to(bias, (CHAN, POINTS))
    for b in range(TAPS):
        rows = slice(b * CHAN, b * CHAN + CHAN)
        part = taps[rows, :]
        total = total + (part if b == 2 else pltpu.roll(part, (2 - b) % POINTS, 1))
        if b != 2:
            total = total + jnp.dot(
                edge_taps[rows, :], places[b].astype(jnp.float32),
                precision=lax.Precision.HIGHEST, preferred_element_type=jnp.float32,
            )
    return total


def kernel_terms(values, target, vectors, gradients, score):
    lane = lax.broadcasted_iota(jnp.int32, (16, LANES), 1)
    real = (lane < LON_DEV) | ((lane >= PITCH) & (lane < PITCH + LON_DEV))

    def block(t, score_sum):
        rows = pl.ds(pl.multiple_of(t * 16, 16), 16)
        members = [values[m, rows, :].astype(jnp.float32) for m in range(MEMBERS)]
        width = vectors[rows, :][:, 1:2]
        inverse = jnp.broadcast_to(1.0 / (width * width), (16, LANES))
        half = -0.5 * inverse
        goal = target[rows, :]
        pulls = [jnp.zeros((16, LANES), jnp.float32) for _ in range(MEMBERS)]
        pair_sum = jnp.zeros((16, LANES), jnp.float32)
        for m in range(MEMBERS):
            for n in range(m + 1, MEMBERS):
                spread = members[m] - members[n]
                kernel_pair = jnp.exp(spread * spread * half)
                pair_sum = pair_sum + kernel_pair
                pull = kernel_pair * spread
                pulls[m] = pulls[m] + pull
                pulls[n] = pulls[n] - pull
        obs_sum = jnp.zeros((16, LANES), jnp.float32)
        for m in range(MEMBERS):
            misfit = members[m] - goal
            kernel_obs = jnp.exp(misfit * misfit * half)
            obs_sum = obs_sum + kernel_obs
            gradient = inverse * (misfit * kernel_obs - pulls[m] * (1.0 / MEMBERS))
            gradients[m, rows, :] = jnp.where(real, gradient, 0.0).astype(jnp.bfloat16)
        per_channel = (MEMBERS + 2.0 * pair_sum) * (1.0 / (2 * MEMBERS * MEMBERS)) - obs_sum * (1.0 / MEMBERS)
        channel = t * 16 + lax.broadcasted_iota(jnp.int32, (16, LANES), 0)
        return score_sum + jnp.where(channel < COUT, per_channel, 0.0)

    total = lax.fori_loop(0, CHAN // 16, block, jnp.zeros((16, LANES), jnp.float32))
    score[...] = jnp.broadcast_to(jnp.sum(total, axis=0, keepdims=True) * (1.0 / COUT), (8, LANES))


def stack_gradient(gathered, packed_grad, stacked, edge_stacked, places):
    grad = jnp.concatenate(
        [gathered[q].astype(jnp.float32)[:, :CHUNK] for q in range(MEMBERS)], axis=1
    )
    packed = grad.astype(jnp.bfloat16)
    packed_grad[...] = packed
    for b in range(TAPS):
        rows = slice(b * CHAN, b * CHAN + CHAN)
        if b == 2:
            stacked[rows, :] = packed
            edge_stacked[rows, :] = jnp.zeros((CHAN, 64), jnp.bfloat16)
        else:
            stacked[rows, :] = pltpu.roll(grad, (b - 2) % POINTS, 1).astype(jnp.bfloat16)
            edge = lax.dot_general(packed, places[b], NT, preferred_element_type=jnp.float32)
            edge_stacked[rows, :] = edge.astype(jnp.bfloat16)


def product(a, lanes, x, margin, stacked, edge_stacked):
    right = x[pl.ds(pl.multiple_of(a * PITCH, 16), POINTS), lanes]
    total = jnp.dot(stacked[...], right, preferred_element_type=jnp.float32)
    return total + jnp.dot(edge_stacked[...], margin[a, :, lanes], preferred_element_type=jnp.float32)


def shared_terms(x, margin, stacked, edge_stacked, fifth, fifth_sent, tails):
    def one(a, _):
        total = product(a, slice(512, 768), x, margin, stacked, edge_stacked)
        rows = pl.ds(pl.multiple_of(a * TAP_ROWS, 16), TAP_ROWS)
        fifth[rows, :] = total[:, :LANES]
        fifth_sent[rows, :] = total[:, :LANES].astype(jnp.bfloat16)
        tails[a, :, 0:TAP_ROWS] = jnp.transpose(total[:, LANES:])[0:8, :]
        return 0

    tails[...] = jnp.zeros((TAPS, 8, 512), jnp.float32)
    lax.fori_loop(0, TAPS, one, 0)
    spare = ROWS - TAPS * TAP_ROWS
    fifth[TAPS * TAP_ROWS : ROWS, :] = jnp.zeros((spare, LANES), jnp.float32)
    for n in range(TAPS + 1):
        a, channel = (n, 0) if n < TAPS else (2, 1)
        for q in range(4):
            row = TAPS * TAP_ROWS + 4 * n + q
            fifth[row : row + 1, :] = tails[a, channel : channel + 1, q * LANES : (q + 1) * LANES]
    fifth_sent[TAPS * TAP_ROWS : ROWS, :] = fifth[TAPS * TAP_ROWS : ROWS, :].astype(jnp.bfloat16)


def weight_terms(half, x, margin, stacked, edge_stacked, into):
    lanes = pl.ds(pl.multiple_of(half * 256, 256), 256)

    def one(a, _):
        total = product(a, lanes, x, margin, stacked, edge_stacked).astype(into.dtype)
        rows = pl.ds(pl.multiple_of(a * TAP_ROWS, 16), TAP_ROWS)
        for k in range(2):
            into[k, rows, :] = total[:, k * LANES : (k + 1) * LANES]
        return 0

    lax.fori_loop(0, TAPS, one, 0)
    first = TAPS * TAP_ROWS
    for k in range(2):
        into[k, first:ROWS, :] = jnp.zeros((ROWS - first, LANES), into.dtype)


def own_scores(starts, score_rx, owned):
    lane = lax.broadcasted_iota(jnp.int32, (8, LANES), 1)
    row = lax.broadcasted_iota(jnp.int32, (8, LANES), 0)
    me = lax.axis_index("member")
    first, count = starts[me], starts[me + 1] - starts[me]
    wanted = jnp.where(row < count, first + row, -1)
    total = jnp.zeros((8, LANES), jnp.float32)
    for q in range(MEMBERS):
        pair = score_rx[q]
        low = jnp.where(lane < LON_DEV, pair, 0.0)
        high = jnp.where(lane < LON_DEV, pltpu.roll(pair, LANES - PITCH, 1), 0.0)
        total = total + jnp.where(wanted == 2 * q, low, 0.0) + jnp.where(wanted == 2 * q + 1, high, 0.0)
    owned[...] = jnp.concatenate([total[s : s + 1, 0:LON_DEV] for s in range(CAP)], axis=1)


def whole_kernel(
    raw_hbm, w_hbm, observed_hbm, places_hbm, picks_hbm, bias, widths, starts, out, grad_out, owned, *scratch
):
    raw, w, observed, places, picks, x, tile, wide, vectors, target, packed, local = scratch[:12]
    scratch = scratch[12:]
    (
        staged, edges, halo, margin, taps, edge_taps, to_score, values, gradients, gathered, score, score_rx,
        stacked, edge_stacked, theirs, mine, fifth, fifth_sent, tails, near_send, near_recv,
    ) = scratch[:21]
    core_rx, rest = scratch[21:24], scratch[24:]
    cur = [rest[3 * k : 3 * k + 3] for k in range(PARTS)]
    rxs = [rest[8 + 3 * k : 11 + 3 * k] for k in range(PARTS)]
    shared, send_sems, recv_sems, mid_recv, far_recv, piece_recv = rest[16:22]
    at = position()
    member, lon = lax.axis_index("member"), lax.axis_index("lon")
    ahead = (member, lax.rem(lon + 1, GROUPS))
    behind = (member, lax.rem(lon + GROUPS - 1, GROUPS))
    others = [lax.rem(member + delta, MEMBERS) for delta in range(1, MEMBERS)]

    loads = [
        pltpu.make_async_copy(source, target_ref, local.at[n])
        for n, (source, target_ref) in enumerate(
            ((raw_hbm, raw), (picks_hbm, picks), (w_hbm, w), (places_hbm, places), (observed_hbm, observed))
        )
    ]
    for load in loads:
        load.start()
    barrier, count = greet(at)
    stage_columns(bias, widths, tile, vectors)
    loads[0].wait()
    stage_field(raw, x)
    loads[1].wait()
    edge = jnp.dot(picks[...], x[...], preferred_element_type=jnp.float32).astype(jnp.bfloat16)
    edges[0] = edge[:PITCH]
    edges[1] = edge[PITCH:]
    loads[2].wait()
    stage_weight(w, staged)
    pl.semaphore_wait(barrier, count)
    send_to(edges.at[0], halo.at[0], near_send.at[0], near_recv.at[0], ahead)
    send_to(edges.at[1], halo.at[1], near_send.at[1], near_recv.at[1], behind)
    forward_own(x, staged, taps)
    loads[3].wait()
    loads[4].wait()
    stage_target(observed, wide, target)
    finish(halo.at[0], near_send.at[0], near_recv.at[0], at).wait()
    finish(halo.at[1], near_send.at[1], near_recv.at[1], at).wait()
    stage_margin(halo, margin)
    forward_margin(margin, staged, edge_taps)
    outputs = convolved(taps, edge_taps, places, vectors[...][:, 0:1])
    for q in range(MEMBERS):
        to_score[q, :, 0:CHUNK] = outputs[:, q * CHUNK : (q + 1) * CHUNK].astype(jnp.bfloat16)
        to_score[q, :, CHUNK:LANES] = jnp.zeros((CHAN, LANES - CHUNK), jnp.bfloat16)
    for there in others:
        send_to(to_score.at[there], values.at[member], near_send.at[2], near_recv.at[2], (there, lon))
    values[member] = to_score[member]
    finish(values.at[0:7], near_send.at[2], near_recv.at[2], at).wait_recv()
    kernel_terms(values, target, vectors, gradients, score)
    for there in others:
        send_to(gradients.at[there], gathered.at[member], near_send.at[3], near_recv.at[3], (there, lon))
    for there in others:
        send_to(score, score_rx.at[member], near_send.at[4], near_recv.at[4], (there, lon))
    gathered[member] = gradients[member]
    score_rx[member] = score[...]
    finish(gathered.at[0:7], near_send.at[3], near_recv.at[3], at).wait_recv()
    stack_gradient(gathered, packed, stacked, edge_stacked, places)
    core, partner = at["core"], moved(at, "core", 1)
    weight_terms(1 - core, x, margin, stacked, edge_stacked, theirs)
    for k in range(2):
        send(theirs.at[k], core_rx[k], send_sems.at[k, 0], recv_sems.at[k, 0], partner)
    shared_terms(x, margin, stacked, edge_stacked, fifth, fifth_sent, tails)
    source = fifth_sent.at[pl.ds(pl.multiple_of((1 - core) * 1024, 16), 1024)]
    send(source, core_rx[2], send_sems.at[2, 0], recv_sems.at[2, 0], partner)
    weight_terms(core, x, margin, stacked, edge_stacked, mine)
    for k, own in ((0, mine), (1, mine), (2, fifth)):
        add_core(at, k, own, core_rx, cur, send_sems, recv_sems)
        if k == 2:
            launch(at, k, 0, cur, rxs, send_sems, recv_sems)
        else:
            launch_pieces(at, k, cur, rxs, send_sems, piece_recv)
    write_gradient(packed, grad_out)
    finish(score_rx.at[0:7], near_send.at[4], near_recv.at[4], at).wait_recv()
    own_scores(starts, score_rx, owned)
    all_reduce(at, out, core_rx, cur, rxs, shared, send_sems, recv_sems, mid_recv, far_recv, piece_recv)
    finish(values.at[0:7], near_send.at[2], near_recv.at[2], at).wait_send()
    finish(gathered.at[0:7], near_send.at[3], near_recv.at[3], at).wait_send()
    finish(score_rx.at[0:7], near_send.at[4], near_recv.at[4], at).wait_send()


def kernel_scratch():
    chunk = (MEMBERS, CHAN, LANES)
    return [
        pltpu.VMEM((LAT + 4, LON_DEV, CIN), jnp.bfloat16),
        pltpu.VMEM((TAPS, TAPS, COUT, CIN), jnp.bfloat16),
        pltpu.VMEM((LON_DEV, LAT, COUT), jnp.float32),
        pltpu.VMEM((TAPS, 4 * LAT, POINTS), jnp.bfloat16),
        pltpu.VMEM((2 * PITCH, (LAT + 4) * PITCH), jnp.bfloat16),
        pltpu.VMEM(((LAT + 4) * PITCH, COLS), jnp.bfloat16),
        pltpu.VMEM((8, LANES), jnp.float32),
        pltpu.VMEM((LANES, LANES), jnp.float32),
        pltpu.VMEM((CHAN, LANES), jnp.float32),
        pltpu.VMEM((CHAN, LANES), jnp.float32),
        pltpu.VMEM((CHAN, POINTS), jnp.bfloat16),
        pltpu.SemaphoreType.DMA((5,)),
        pltpu.VMEM((TAPS * TAP_ROWS, COLS), jnp.bfloat16),
        pltpu.VMEM((2, PITCH, COLS), jnp.bfloat16),
        pltpu.VMEM((2, PITCH, COLS), jnp.bfloat16),
        pltpu.VMEM((TAPS, 64, COLS), jnp.bfloat16),
        pltpu.VMEM((TAP_ROWS, POINTS), jnp.float32),
        pltpu.VMEM((TAP_ROWS, 64), jnp.float32),
        pltpu.VMEM(chunk, jnp.bfloat16),
        pltpu.VMEM(chunk, jnp.bfloat16),
        pltpu.VMEM(chunk, jnp.bfloat16),
        pltpu.VMEM(chunk, jnp.bfloat16),
        pltpu.VMEM((8, LANES), jnp.float32),
        pltpu.VMEM((MEMBERS, 8, LANES), jnp.float32),
        pltpu.VMEM((TAP_ROWS, POINTS), jnp.bfloat16),
        pltpu.VMEM((TAP_ROWS, 64), jnp.bfloat16),
        pltpu.VMEM((2, ROWS, LANES), jnp.bfloat16),
        pltpu.VMEM((2, ROWS, LANES), jnp.float32),
        pltpu.VMEM((ROWS, LANES), jnp.float32),
        pltpu.VMEM((ROWS, LANES), jnp.bfloat16),
        pltpu.VMEM((TAPS, 8, 512), jnp.float32),
        pltpu.SemaphoreType.DMA((5,)),
        pltpu.SemaphoreType.DMA((5,)),
    ] + reduce_scratch()


def finish_kernel(
    summed, grad_in, owned_in, weight_grad, grad_out, owned_out, bias_grad,
    main, wide, grad_here, owned_here, in_sems, out_sems, pass_sems,
):
    factor = 1.0 / math.sqrt(MEMBERS * LAT * LON_DEV * GROUPS)
    first = TAPS * TAP_ROWS
    tail = (TAPS - 1, slice(first, ROWS))
    loads = [pltpu.make_async_copy(summed.at[tail], main.at[tail], in_sems.at[TAPS])]
    for a in range(TAPS):
        rows = (slice(None), slice(a * TAP_ROWS, (a + 1) * TAP_ROWS))
        loads.append(pltpu.make_async_copy(summed.at[rows], main.at[rows], in_sems.at[a]))
    taken = [
        pltpu.make_async_copy(grad_in, grad_here, pass_sems.at[0]),
        pltpu.make_async_copy(owned_in, owned_here, pass_sems.at[1]),
    ]
    for copy in loads + taken:
        copy.start()
    loads[0].wait()
    more = main[TAPS - 1, first:ROWS, :].astype(jnp.float32) * factor
    bias = jnp.concatenate([more[4 * TAPS + q : 4 * TAPS + q + 1, :] for q in range(4)], axis=1)
    bias_grad[...] = bias[:, 2 * CHAN : 2 * CHAN + COUT]
    stores = []
    for a in range(TAPS):
        last = jnp.concatenate([more[4 * a + q : 4 * a + q + 1, :] for q in range(4)], axis=1)
        last = jnp.transpose(jnp.broadcast_to(last, (8, 512)))
        loads[a + 1].wait()
        for b in range(TAPS):
            base, n = a * TAP_ROWS + b * CHAN, a * TAPS + b
            for block in range(TAPS):
                part = main[block, base : base + CHAN, :].astype(jnp.float32) * factor
                wide[n, :, block * LANES : (block + 1) * LANES] = part[:COUT]
            wide[n, :, WIDE:CIN] = last[b * CHAN : b * CHAN + COUT, 0:1]
            stores.append(pltpu.make_async_copy(wide.at[n], weight_grad.at[n], out_sems.at[n]))
            stores[-1].start()
    given = [
        pltpu.make_async_copy(grad_here, grad_out, pass_sems.at[2]),
        pltpu.make_async_copy(owned_here, owned_out, pass_sems.at[3]),
    ]
    for source, target in zip(taken, given):
        source.wait()
        target.start()
    for copy in stores + given:
        copy.wait()


def body(fields, weight, out_bias, observed, widths, owner_start):
    vmem = pl.BlockSpec(memory_space=pltpu.VMEM)
    hbm = pl.BlockSpec(memory_space=pl.ANY)
    summed, grad, owned = pl.pallas_call(
        whole_kernel,
        out_shape=[
            jax.ShapeDtypeStruct((TAPS, ROWS, LANES), jnp.bfloat16),
            jax.ShapeDtypeStruct((LON_DEV, LAT, COUT), jnp.bfloat16),
            jax.ShapeDtypeStruct((1, CAP * LON_DEV), jnp.float32),
        ],
        in_specs=[hbm] * 5 + [vmem] * 2 + [pl.BlockSpec(memory_space=pltpu.SMEM)],
        out_specs=[vmem] * 3,
        scratch_shapes=kernel_scratch(),
        compiler_params=pltpu.CompilerParams(
            collective_id=1, has_side_effects=True, vmem_limit_bytes=56 * 1024 * 1024
        ),
        cost_estimate=pl.CostEstimate(flops=6 << 30, bytes_accessed=16 << 20, transcendentals=1 << 20),
    )(
        jnp.transpose(fields[0], (1, 2, 0)), weight, jnp.transpose(observed, (2, 1, 0)),
        jnp.asarray(margin_places(), jnp.bfloat16), jnp.asarray(edge_picks(), jnp.bfloat16),
        out_bias.reshape(1, COUT), widths.reshape(1, COUT), owner_start[0],
    )
    weight_grad, grad, owned, bias_grad = pl.pallas_call(
        finish_kernel,
        out_shape=[
            jax.ShapeDtypeStruct((TAPS * TAPS, COUT, CIN), jnp.float32),
            jax.ShapeDtypeStruct((LON_DEV, LAT, COUT), jnp.bfloat16),
            jax.ShapeDtypeStruct((1, CAP * LON_DEV), jnp.float32),
            jax.ShapeDtypeStruct((1, COUT), jnp.float32),
        ],
        in_specs=[hbm] * 3,
        out_specs=[hbm] * 3 + [vmem],
        scratch_shapes=[
            pltpu.VMEM((TAPS, ROWS, LANES), jnp.bfloat16),
            pltpu.VMEM((TAPS * TAPS, COUT, CIN), jnp.float32),
            pltpu.VMEM((LON_DEV, LAT, COUT), jnp.bfloat16),
            pltpu.VMEM((1, CAP * LON_DEV), jnp.float32),
            pltpu.SemaphoreType.DMA((TAPS + 1,)),
            pltpu.SemaphoreType.DMA((TAPS * TAPS,)),
            pltpu.SemaphoreType.DMA((4,)),
        ],
        compiler_params=pltpu.CompilerParams(vmem_limit_bytes=58 * 1024 * 1024),
    )(summed, grad, owned)
    weight_grad = weight_grad.reshape(TAPS, TAPS, COUT, CIN)
    bias_grad = bias_grad.reshape(COUT)
    out_grad = jnp.transpose(grad, (2, 1, 0))[None]
    owned_score = owned.reshape(1, 1, CAP * LON_DEV)
    return (out_grad, owned_score, weight_grad, bias_grad)


def solution(mesh):
    in_specs = (P("member", None, None, "lon"), P(), P(), P(None, None, "lon"), P(), P("lon", None))
    out_specs = (P("member", None, None, "lon"), P("lon", "member", None), P(), P())
    return jax.shard_map(body, mesh=mesh, in_specs=in_specs, out_specs=out_specs, check_vma=False)
```

```python
import math

import jax
import jax.numpy as jnp
import numpy as np
from jax import lax
from jax.experimental import pallas as pl
from jax.experimental.pallas import tpu as pltpu
from jax.sharding import PartitionSpec as P

MESH = pl.DeviceIdType.MESH
MEMBERS = 8
GROUPS = 32
TAPS = 5
CIN = 641
COUT = 73
CHAN = 80
LAT = 16
LON_DEV = 45
PITCH = 48
POINTS = LAT * PITCH
CHUNK = 2 * PITCH
CAP = 6
TAP_ROWS = TAPS * CHAN
NT = (((1,), (1,)), ((), ()))
ROWS = 2048
LANES = 128
PARTS = 3
COLS = 768
WIDE = 640
PART_ROWS = (2048, 2048, 1024)
ORDERS = (("x", "y", "z"), ("y", "x", "z"), ("z", "x", "y"))


def position():
    member = lax.axis_index("member")
    lon = lax.axis_index("lon")
    return {
        "x": (lon // 16) * 2 + member % 2,
        "y": member // 2,
        "z": (lon // 2) % 8,
        "core": lon % 2,
    }


EXTENT = {"x": 4, "y": 4, "z": 8, "core": 2}


def device(at):
    return (at["y"] * 2 + at["x"] % 2, (at["x"] // 2) * 16 + at["z"] * 2 + at["core"])


def moved(at, axis, delta):
    there = dict(at)
    there[axis] = lax.rem(at[axis] + delta, EXTENT[axis])
    return there


def send(src, dst, send_sem, recv_sem, at):
    copy = pltpu.make_async_remote_copy(
        src_ref=src, dst_ref=dst, send_sem=send_sem, recv_sem=recv_sem,
        device_id=device(at), device_id_type=MESH,
    )
    copy.start()


def send_to(src, dst, send_sem, recv_sem, there):
    copy = pltpu.make_async_remote_copy(
        src_ref=src, dst_ref=dst, send_sem=send_sem, recv_sem=recv_sem,
        device_id=there, device_id_type=MESH,
    )
    copy.start()


def finish(ref, send_sem, recv_sem, at):
    copy = pltpu.make_async_remote_copy(
        src_ref=ref, dst_ref=ref, send_sem=send_sem, recv_sem=recv_sem,
        device_id=device(at), device_id_type=MESH,
    )
    return copy


def greet(at):
    barrier = pltpu.get_barrier_semaphore()
    count = 0
    for axis in ("core", "x", "y", "z"):
        for delta in range(1, EXTENT[axis]):
            pl.semaphore_signal(
                barrier, inc=1, device_id=device(moved(at, axis, delta)), device_id_type=MESH
            )
            count += 1
    member, lon = lax.axis_index("member"), lax.axis_index("lon")
    for delta in range(1, MEMBERS):
        there = (lax.rem(member + delta, MEMBERS), lon)
        pl.semaphore_signal(barrier, inc=1, device_id=there, device_id_type=MESH)
        count += 1
    for delta in (1, GROUPS - 1):
        there = (member, lax.rem(lon + delta, GROUPS))
        pl.semaphore_signal(barrier, inc=1, device_id=there, device_id_type=MESH)
        count += 1
    return barrier, count


def stage_rows(k):
    rows, sizes = PART_ROWS[k], []
    for axis in ORDERS[k][: 2 if k == 2 else 3]:
        rows //= EXTENT[axis]
        sizes.append(rows)
    return sizes


SIZES = [stage_rows(k) for k in range(PARTS)]


def place(at, out, k, row, rows):
    if k == 2:
        return out.at[4, pl.ds(pl.multiple_of(at["core"] * 1024 + row, 16), rows), :]
    return out.at[2 * at["core"] + k, pl.ds(pl.multiple_of(row, 16), rows), :]


def launch(at, k, s, cur, rxs, send_sems, recv_sems):
    axis, rows = ORDERS[k][s], SIZES[k][s]
    for delta in range(1, EXTENT[axis]):
        there = moved(at, axis, delta)
        source = cur[k][s].at[pl.ds(pl.multiple_of(there[axis] * rows, 16), rows)]
        send(source, rxs[k][s].at[delta - 1], send_sems.at[k, s + 1], recv_sems.at[k, s + 1], there)


def add_core(at, k, mine, core_rx, cur, send_sems, recv_sems):
    finish(core_rx[k], send_sems.at[k, 0], recv_sems.at[k, 0], at).wait_recv()
    step = 256

    def add(i, _):
        here = pl.ds(pl.multiple_of(i * step, step), step)
        if k == 2:
            own = mine[pl.ds(pl.multiple_of(at["core"] * 1024 + i * step, step), step), :]
        else:
            own = mine[k, here, :]
        cur[k][0][here, :] = (own + core_rx[k][here, :].astype(jnp.float32)).astype(jnp.bfloat16)
        return 0

    lax.fori_loop(0, PART_ROWS[k] // step, add, 0)


def gather(at, out, k, s, row, send_sems, recv_sems):
    axis = ORDERS[k][s]
    block = place(at, out, k, row, SIZES[k][s])
    for delta in range(1, EXTENT[axis]):
        send(block, block, send_sems.at[k, 4 + s], recv_sems.at[k, 4 + s], moved(at, axis, delta))


def spread(at, out, k, dy, dx, send_sem, recv_sem, there):
    first, second = ORDERS[k][0], ORDERS[k][1]
    row = lax.rem(at[first] + 4 - dx, 4) * SIZES[k][0] + lax.rem(at[second] + 4 - dy, 4) * SIZES[k][1]
    block = place(at, out, k, row, SIZES[k][1])
    if there is None:
        finish(block, send_sem, recv_sem, at).wait_recv()
    else:
        send(block, block, send_sem, recv_sem, there)


def all_reduce(at, out, core_rx, cur, rxs, shared, send_sems, recv_sems, mid_recv, far_recv):
    row = [0] * PARTS
    partner = moved(at, "core", 1)
    for s in range(3):
        for k in (2, 0, 1) if s == 2 else (0, 1, 2):
            if k == 2 and s == 2:
                finish(shared.at[0:3], send_sems.at[k, 3], recv_sems.at[k, 3], at).wait_recv()
                total = shared[0].astype(jnp.float32)
                for y in range(1, 4):
                    total = total + shared[y].astype(jnp.float32)
                place(at, out, k, row[k], 32)[...] = total.astype(jnp.bfloat16)
                gather(at, out, k, 1, row[k], send_sems, recv_sems)
                continue
            axis, rows = ORDERS[k][s], SIZES[k][s]
            finish(rxs[k][s], send_sems.at[k, s + 1], recv_sems.at[k, s + 1], at).wait_recv()
            row[k] = row[k] + at[axis] * rows
            base = pl.multiple_of(at[axis] * rows, 16)
            step = min(rows, 128)

            def add(i, _, k=k, s=s, axis=axis, base=base, step=step):
                total = cur[k][s][pl.ds(pl.multiple_of(base + i * step, 16), step), :].astype(jnp.float32)
                here = pl.ds(pl.multiple_of(i * step, 16), step)
                for slot in range(EXTENT[axis] - 1):
                    total = total + rxs[k][s][slot, here, :].astype(jnp.float32)
                total = total.astype(jnp.bfloat16)
                if k == 2 and s == 1:
                    shared[at["y"]] = total
                elif s == 2:
                    place(at, out, k, row[k], step)[...] = total
                else:
                    cur[k][s + 1][here, :] = total
                return 0

            if rows == step:
                add(0, 0)
            else:
                lax.fori_loop(0, rows // step, add, 0)
            if k == 2 and s == 1:
                for delta in range(1, 4):
                    own = shared.at[at["y"]]
                    send(own, own, send_sems.at[k, 3], recv_sems.at[k, 3], moved(at, "y", delta))
            elif s == 2:
                gather(at, out, k, 2, row[k], send_sems, recv_sems)
            else:
                launch(at, k, s + 1, cur, rxs, send_sems, recv_sems)
    def arrived(k, s):
        finish(rxs[k][s], send_sems.at[k, 4 + s], recv_sems.at[k, 4 + s], at).wait_recv()

    def onward(k, dy):
        first = ORDERS[k][0]
        for dx in (2, 1, 3):
            spread(at, out, k, dy, 0, send_sems.at[k, 4], far_recv.at[k, 4 * dx + dy], moved(at, first, dx))
        spread(at, out, k, dy, 0, send_sems.at[k, 7], recv_sems.at[k, 7], partner)

    arrived(2, 1)
    row[2] = row[2] - at["x"] * SIZES[2][1]
    gather(at, out, 2, 0, row[2], send_sems, recv_sems)
    for k in range(2):
        arrived(k, 2)
        for dy in (2, 1, 3):
            there = moved(at, ORDERS[k][1], dy)
            spread(at, out, k, 0, 0, send_sems.at[k, 5], mid_recv.at[k, dy], there)
        onward(k, 0)
    for dy in (1, 3, 2):
        for k in range(2):
            spread(at, out, k, dy, 0, send_sems.at[k, 5], mid_recv.at[k, dy], None)
            onward(k, dy)
    for dy in (0, 1, 3, 2):
        if dy == 2:
            arrived(2, 0)
            block = place(at, out, 2, 0, PART_ROWS[2])
            send(block, block, send_sems.at[2, 7], recv_sems.at[2, 7], partner)
        for dx in (1, 3, 2):
            for k in range(2):
                spread(at, out, k, dy, dx, send_sems.at[k, 4], far_recv.at[k, 4 * dx + dy], None)
                spread(at, out, k, dy, dx, send_sems.at[k, 7], recv_sems.at[k, 7], partner)
    for k in (2, 0, 1):
        finish(core_rx[k], send_sems.at[k, 7], recv_sems.at[k, 7], partner).wait_recv()
    for k in range(PARTS):
        finish(core_rx[k], send_sems.at[k, 0], recv_sems.at[k, 0], partner).wait_send()
        finish(core_rx[k], send_sems.at[k, 7], recv_sems.at[k, 7], partner).wait_send()
        for s in range(len(SIZES[k])):
            finish(rxs[k][s], send_sems.at[k, s + 1], recv_sems.at[k, s + 1], partner).wait_send()
            finish(rxs[k][s], send_sems.at[k, s + 4], recv_sems.at[k, s + 4], partner).wait_send()
    finish(shared.at[0:3], send_sems.at[2, 3], recv_sems.at[2, 3], partner).wait_send()


def reduce_scratch():
    shapes = [pltpu.VMEM((PART_ROWS[k], LANES), jnp.bfloat16) for k in range(PARTS)]
    for k in range(PARTS):
        rows = PART_ROWS[k]
        for size in SIZES[k]:
            shapes.append(pltpu.VMEM((rows, LANES), jnp.bfloat16))
            rows = size
    for k in range(PARTS):
        for axis, size in zip(ORDERS[k], SIZES[k]):
            shapes.append(pltpu.VMEM((EXTENT[axis] - 1, size, LANES), jnp.bfloat16))
    shapes.append(pltpu.VMEM((4, 32, LANES), jnp.bfloat16))
    shapes += [pltpu.SemaphoreType.DMA((PARTS, 8)), pltpu.SemaphoreType.DMA((PARTS, 8))]
    shapes += [pltpu.SemaphoreType.DMA((2, 4)), pltpu.SemaphoreType.DMA((2, 16))]
    return shapes


def edge_picks():
    picks = np.zeros((2, PITCH, (LAT + 4) * PITCH), np.float32)
    for side, first in ((0, LON_DEV - 2), (1, 0)):
        for i in range(LAT + 4):
            for h in range(2):
                picks[side, 2 * i + h, i * PITCH + first + h] = 1.0
    return picks.reshape(2 * PITCH, -1)


def margin_places():
    places = np.zeros((TAPS, 2, LAT, 2, LAT, PITCH), np.float32)
    for b in range(TAPS):
        for side, first in ((0, -2), (1, LON_DEV)):
            for h in range(2):
                j = first + h - b + 2
                if 0 <= j < LON_DEV:
                    for i in range(LAT):
                        places[b, side, i, h, i, j] = 1.0
    return places.reshape(TAPS, 4 * LAT, POINTS)


def stage_field(raw, x):
    lane = lax.broadcasted_iota(jnp.int32, (PITCH, LANES), 1)
    row = lax.broadcasted_iota(jnp.int32, (PITCH, LANES), 0)
    tail = jnp.where((lane == CIN - 640) & (row < LON_DEV), 1.0, 0.0).astype(jnp.bfloat16)
    zeros = jnp.zeros((16, COLS), jnp.bfloat16)

    def one(i, _):
        base = pl.multiple_of(i * PITCH, 16)
        x[pl.ds(base + 32, 16), :] = zeros
        x[pl.ds(base, PITCH), 640:COLS] = tail
        x[pl.ds(base, LON_DEV), 0:CIN] = raw[i]
        return 0

    lax.fori_loop(0, LAT + 4, one, 0)


def stage_columns(bias, widths, tile, vectors):
    tile[...] = jnp.ones((8, LANES), jnp.float32)
    tile[0:1, 0:COUT] = bias[...]
    tile[1:2, 0:COUT] = widths[...]
    vectors[:, 0:8] = jnp.transpose(tile[...])[0:CHAN, :]


def stage_target(observed, wide, target):
    spots = LON_DEV * LAT
    point = lax.broadcasted_iota(jnp.int32, (LANES, spots), 0)
    spot = lax.broadcasted_iota(jnp.int32, (LANES, spots), 1)
    second = (point >= PITCH).astype(jnp.int32)
    wanted = (point - PITCH * second) * LAT + 2 * lax.axis_index("member") + second
    chosen = ((spot == wanted) & (point < CHUNK)).astype(jnp.float32)
    wide[...] = jnp.zeros((LANES, LANES), jnp.float32)
    wide[:, 0:COUT] = jnp.dot(
        chosen, observed[...].reshape(spots, COUT),
        precision=lax.Precision.HIGHEST, preferred_element_type=jnp.float32,
    )
    target[...] = jnp.transpose(wide[...])[0:CHAN, :]


def write_gradient(packed, grad_out):
    spots = LON_DEV * LAT
    spot = lax.broadcasted_iota(jnp.int32, (spots, POINTS), 0)
    point = lax.broadcasted_iota(jnp.int32, (spots, POINTS), 1)
    wanted = (spot & (LAT - 1)) * PITCH + (spot >> 4)
    moves = jnp.where(point == wanted, 1.0, 0.0).astype(jnp.bfloat16)
    moved_grad = lax.dot_general(moves, packed[...], NT, preferred_element_type=jnp.float32)
    grad_out[...] = moved_grad.astype(jnp.bfloat16).reshape(LON_DEV, LAT, CHAN)[:, :, :COUT]


def stage_weight(w, staged):
    zeros = jnp.zeros((16, COLS), jnp.bfloat16)
    tail = jnp.zeros((64, COLS - 640), jnp.bfloat16)

    def one(a, _):
        for b in range(TAPS):
            base = pl.multiple_of(a * TAP_ROWS + b * CHAN, 16)
            staged[pl.ds(base + 64, 16), :] = zeros
            staged[pl.ds(base, 64), 640:COLS] = tail
            staged[pl.ds(base, COUT), 0:CIN] = w[a, b]
        return 0

    lax.fori_loop(0, TAPS, one, 0)


def forward_own(x, staged, taps):
    for n in range(3):
        lanes = slice(n * 256, n * 256 + 256)

        def one(a, total, n=n):
            rows = pl.ds(pl.multiple_of(a * PITCH + n * 256, 16), 256)
            left = staged[pl.ds(pl.multiple_of(a * TAP_ROWS, 16), TAP_ROWS), :]
            return total + lax.dot_general(left, x[rows, :], NT, preferred_element_type=jnp.float32)

        taps[:, lanes] = lax.fori_loop(0, TAPS, one, jnp.zeros((TAP_ROWS, 256), jnp.float32))


def stage_margin(halo, margin):
    left = halo[0].astype(jnp.float32)
    right = halo[1].astype(jnp.float32)
    for a in range(TAPS):
        margin[a, 0:32, :] = left[2 * a : 2 * a + 32, :].astype(jnp.bfloat16)
        margin[a, 32:64, :] = right[2 * a : 2 * a + 32, :].astype(jnp.bfloat16)


def forward_margin(margin, staged, edge_taps):
    def one(a, total):
        left = staged[pl.ds(pl.multiple_of(a * TAP_ROWS, 16), TAP_ROWS), :]
        return total + lax.dot_general(left, margin[a], NT, preferred_element_type=jnp.float32)

    edge_taps[...] = lax.fori_loop(0, TAPS, one, jnp.zeros((TAP_ROWS, 64), jnp.float32))


def sum_own(taps, bias):
    total = jnp.broadcast_to(bias, (CHAN, POINTS))
    for b in range(TAPS):
        part = taps[b * CHAN : (b + 1) * CHAN, :]
        total = total + (part if b == 2 else pltpu.roll(part, (2 - b) % POINTS, 1))
    taps[0:CHAN, :] = total


def convolved(taps, edge_taps, places):
    total = taps[0:CHAN, :]
    for b in (0, 1, 3, 4):
        total = total + jnp.dot(
            edge_taps[b * CHAN : (b + 1) * CHAN, :], places[b].astype(jnp.float32),
            precision=lax.Precision.HIGHEST, preferred_element_type=jnp.float32,
        )
    return total


def kernel_terms(values, target, vectors, gradients, score):
    lane = lax.broadcasted_iota(jnp.int32, (16, LANES), 1)
    real = (lane < LON_DEV) | ((lane >= PITCH) & (lane < PITCH + LON_DEV))

    def block(t, score_sum):
        rows = pl.ds(pl.multiple_of(t * 16, 16), 16)
        members = [values[m, rows, :].astype(jnp.float32) for m in range(MEMBERS)]
        width = vectors[rows, :][:, 1:2]
        inverse = jnp.broadcast_to(1.0 / (width * width), (16, LANES))
        half = -0.5 * inverse
        goal = target[rows, :]
        pulls = [jnp.zeros((16, LANES), jnp.float32) for _ in range(MEMBERS)]
        pair_sum = jnp.zeros((16, LANES), jnp.float32)
        for m in range(MEMBERS):
            for n in range(m + 1, MEMBERS):
                spread = members[m] - members[n]
                kernel_pair = jnp.exp(spread * spread * half)
                pair_sum = pair_sum + kernel_pair
                pull = kernel_pair * spread
                pulls[m] = pulls[m] + pull
                pulls[n] = pulls[n] - pull
        obs_sum = jnp.zeros((16, LANES), jnp.float32)
        for m in range(MEMBERS):
            misfit = members[m] - goal
            kernel_obs = jnp.exp(misfit * misfit * half)
            obs_sum = obs_sum + kernel_obs
            gradient = inverse * (misfit * kernel_obs - pulls[m] * (1.0 / MEMBERS))
            gradients[m, rows, :] = jnp.where(real, gradient, 0.0).astype(jnp.bfloat16)
        per_channel = (MEMBERS + 2.0 * pair_sum) * (1.0 / (2 * MEMBERS * MEMBERS)) - obs_sum * (1.0 / MEMBERS)
        channel = t * 16 + lax.broadcasted_iota(jnp.int32, (16, LANES), 0)
        return score_sum + jnp.where(channel < COUT, per_channel, 0.0)

    total = lax.fori_loop(0, CHAN // 16, block, jnp.zeros((16, LANES), jnp.float32))
    score[...] = jnp.broadcast_to(jnp.sum(total, axis=0, keepdims=True) * (1.0 / COUT), (8, LANES))


def stack_gradient(gathered, packed_grad, stacked, edge_stacked, places):
    grad = jnp.concatenate(
        [gathered[q].astype(jnp.float32)[:, :CHUNK] for q in range(MEMBERS)], axis=1
    )
    packed = grad.astype(jnp.bfloat16)
    packed_grad[...] = packed
    for b in range(TAPS):
        rows = slice(b * CHAN, b * CHAN + CHAN)
        if b == 2:
            stacked[rows, :] = packed
            edge_stacked[rows, :] = jnp.zeros((CHAN, 64), jnp.bfloat16)
        else:
            stacked[rows, :] = pltpu.roll(grad, (b - 2) % POINTS, 1).astype(jnp.bfloat16)
            edge = lax.dot_general(packed, places[b], NT, preferred_element_type=jnp.float32)
            edge_stacked[rows, :] = edge.astype(jnp.bfloat16)


def product(a, lanes, x, margin, stacked, edge_stacked):
    right = x[pl.ds(pl.multiple_of(a * PITCH, 16), POINTS), lanes]
    total = jnp.dot(stacked[...], right, preferred_element_type=jnp.float32)
    return total + jnp.dot(edge_stacked[...], margin[a, :, lanes], preferred_element_type=jnp.float32)


def shared_terms(x, margin, stacked, edge_stacked, fifth, fifth_sent, tails):
    def one(a, _):
        total = product(a, slice(512, 768), x, margin, stacked, edge_stacked)
        rows = pl.ds(pl.multiple_of(a * TAP_ROWS, 16), TAP_ROWS)
        fifth[rows, :] = total[:, :LANES]
        fifth_sent[rows, :] = total[:, :LANES].astype(jnp.bfloat16)
        tails[a, :, 0:TAP_ROWS] = jnp.transpose(total[:, LANES:])[0:8, :]
        return 0

    tails[...] = jnp.zeros((TAPS, 8, 512), jnp.float32)
    lax.fori_loop(0, TAPS, one, 0)
    spare = ROWS - TAPS * TAP_ROWS
    fifth[TAPS * TAP_ROWS : ROWS, :] = jnp.zeros((spare, LANES), jnp.float32)
    for n in range(TAPS + 1):
        a, channel = (n, 0) if n < TAPS else (2, 1)
        for q in range(4):
            row = TAPS * TAP_ROWS + 4 * n + q
            fifth[row : row + 1, :] = tails[a, channel : channel + 1, q * LANES : (q + 1) * LANES]
    fifth_sent[TAPS * TAP_ROWS : ROWS, :] = fifth[TAPS * TAP_ROWS : ROWS, :].astype(jnp.bfloat16)


def weight_terms(half, x, margin, stacked, edge_stacked, into):
    lanes = pl.ds(pl.multiple_of(half * 256, 256), 256)

    def one(a, _):
        total = product(a, lanes, x, margin, stacked, edge_stacked).astype(into.dtype)
        rows = pl.ds(pl.multiple_of(a * TAP_ROWS, 16), TAP_ROWS)
        for k in range(2):
            into[k, rows, :] = total[:, k * LANES : (k + 1) * LANES]
        return 0

    lax.fori_loop(0, TAPS, one, 0)
    first = TAPS * TAP_ROWS
    for k in range(2):
        into[k, first:ROWS, :] = jnp.zeros((ROWS - first, LANES), into.dtype)


def own_scores(starts, score_rx, owned):
    lane = lax.broadcasted_iota(jnp.int32, (8, LANES), 1)
    row = lax.broadcasted_iota(jnp.int32, (8, LANES), 0)
    me = lax.axis_index("member")
    first, count = starts[me], starts[me + 1] - starts[me]
    wanted = jnp.where(row < count, first + row, -1)
    total = jnp.zeros((8, LANES), jnp.float32)
    for q in range(MEMBERS):
        pair = score_rx[q]
        low = jnp.where(lane < LON_DEV, pair, 0.0)
        high = jnp.where(lane < LON_DEV, pltpu.roll(pair, LANES - PITCH, 1), 0.0)
        total = total + jnp.where(wanted == 2 * q, low, 0.0) + jnp.where(wanted == 2 * q + 1, high, 0.0)
    owned[...] = jnp.concatenate([total[s : s + 1, 0:LON_DEV] for s in range(CAP)], axis=1)


def whole_kernel(
    raw_hbm, w_hbm, observed_hbm, places_hbm, picks_hbm, bias, widths, starts, out, grad_out, owned, *scratch
):
    raw, w, observed, places, picks, x, tile, wide, vectors, target, packed, local = scratch[:12]
    scratch = scratch[12:]
    (
        staged, edges, halo, margin, taps, edge_taps, to_score, values, gradients, gathered, score, score_rx,
        stacked, edge_stacked, theirs, mine, fifth, fifth_sent, tails, near_send, near_recv,
    ) = scratch[:21]
    core_rx, rest = scratch[21:24], scratch[24:]
    cur = [rest[3 * k : 3 * k + 3] for k in range(PARTS)]
    rxs = [rest[8 + 3 * k : 11 + 3 * k] for k in range(PARTS)]
    shared, send_sems, recv_sems, mid_recv, far_recv = rest[16:21]
    at = position()
    member, lon = lax.axis_index("member"), lax.axis_index("lon")
    ahead = (member, lax.rem(lon + 1, GROUPS))
    behind = (member, lax.rem(lon + GROUPS - 1, GROUPS))
    others = [lax.rem(member + delta, MEMBERS) for delta in range(1, MEMBERS)]

    loads = [
        pltpu.make_async_copy(source, target_ref, local.at[n])
        for n, (source, target_ref) in enumerate(
            ((raw_hbm, raw), (picks_hbm, picks), (w_hbm, w), (places_hbm, places), (observed_hbm, observed))
        )
    ]
    for load in loads:
        load.start()
    barrier, count = greet(at)
    stage_columns(bias, widths, tile, vectors)
    loads[0].wait()
    stage_field(raw, x)
    loads[1].wait()
    edge = jnp.dot(picks[...], x[...], preferred_element_type=jnp.float32).astype(jnp.bfloat16)
    edges[0] = edge[:PITCH]
    edges[1] = edge[PITCH:]
    loads[2].wait()
    stage_weight(w, staged)
    pl.semaphore_wait(barrier, count)
    send_to(edges.at[0], halo.at[0], near_send.at[0], near_recv.at[0], ahead)
    send_to(edges.at[1], halo.at[1], near_send.at[1], near_recv.at[1], behind)
    forward_own(x, staged, taps)
    sum_own(taps, vectors[...][:, 0:1])
    loads[3].wait()
    loads[4].wait()
    stage_target(observed, wide, target)
    finish(halo.at[0], near_send.at[0], near_recv.at[0], at).wait()
    finish(halo.at[1], near_send.at[1], near_recv.at[1], at).wait()
    stage_margin(halo, margin)
    forward_margin(margin, staged, edge_taps)
    outputs = convolved(taps, edge_taps, places)
    for q in range(MEMBERS):
        to_score[q, :, 0:CHUNK] = outputs[:, q * CHUNK : (q + 1) * CHUNK].astype(jnp.bfloat16)
        to_score[q, :, CHUNK:LANES] = jnp.zeros((CHAN, LANES - CHUNK), jnp.bfloat16)
    for there in others:
        send_to(to_score.at[there], values.at[member], near_send.at[2], near_recv.at[2], (there, lon))
    values[member] = to_score[member]
    finish(values.at[0:7], near_send.at[2], near_recv.at[2], at).wait_recv()
    kernel_terms(values, target, vectors, gradients, score)
    for there in others:
        send_to(gradients.at[there], gathered.at[member], near_send.at[3], near_recv.at[3], (there, lon))
    for there in others:
        send_to(score, score_rx.at[member], near_send.at[4], near_recv.at[4], (there, lon))
    gathered[member] = gradients[member]
    score_rx[member] = score[...]
    finish(gathered.at[0:7], near_send.at[3], near_recv.at[3], at).wait_recv()
    stack_gradient(gathered, packed, stacked, edge_stacked, places)
    core, partner = at["core"], moved(at, "core", 1)
    weight_terms(1 - core, x, margin, stacked, edge_stacked, theirs)
    for k in range(2):
        send(theirs.at[k], core_rx[k], send_sems.at[k, 0], recv_sems.at[k, 0], partner)
    shared_terms(x, margin, stacked, edge_stacked, fifth, fifth_sent, tails)
    source = fifth_sent.at[pl.ds(pl.multiple_of((1 - core) * 1024, 16), 1024)]
    send(source, core_rx[2], send_sems.at[2, 0], recv_sems.at[2, 0], partner)
    weight_terms(core, x, margin, stacked, edge_stacked, mine)
    for k, own in ((0, mine), (1, mine), (2, fifth)):
        add_core(at, k, own, core_rx, cur, send_sems, recv_sems)
        launch(at, k, 0, cur, rxs, send_sems, recv_sems)
    write_gradient(packed, grad_out)
    finish(score_rx.at[0:7], near_send.at[4], near_recv.at[4], at).wait_recv()
    own_scores(starts, score_rx, owned)
    all_reduce(at, out, core_rx, cur, rxs, shared, send_sems, recv_sems, mid_recv, far_recv)
    finish(values.at[0:7], near_send.at[2], near_recv.at[2], at).wait_send()
    finish(gathered.at[0:7], near_send.at[3], near_recv.at[3], at).wait_send()
    finish(score_rx.at[0:7], near_send.at[4], near_recv.at[4], at).wait_send()


def kernel_scratch():
    chunk = (MEMBERS, CHAN, LANES)
    return [
        pltpu.VMEM((LAT + 4, LON_DEV, CIN), jnp.bfloat16),
        pltpu.VMEM((TAPS, TAPS, COUT, CIN), jnp.bfloat16),
        pltpu.VMEM((LON_DEV, LAT, COUT), jnp.float32),
        pltpu.VMEM((TAPS, 4 * LAT, POINTS), jnp.bfloat16),
        pltpu.VMEM((2 * PITCH, (LAT + 4) * PITCH), jnp.bfloat16),
        pltpu.VMEM(((LAT + 4) * PITCH, COLS), jnp.bfloat16),
        pltpu.VMEM((8, LANES), jnp.float32),
        pltpu.VMEM((LANES, LANES), jnp.float32),
        pltpu.VMEM((CHAN, LANES), jnp.float32),
        pltpu.VMEM((CHAN, LANES), jnp.float32),
        pltpu.VMEM((CHAN, POINTS), jnp.bfloat16),
        pltpu.SemaphoreType.DMA((5,)),
        pltpu.VMEM((TAPS * TAP_ROWS, COLS), jnp.bfloat16),
        pltpu.VMEM((2, PITCH, COLS), jnp.bfloat16),
        pltpu.VMEM((2, PITCH, COLS), jnp.bfloat16),
        pltpu.VMEM((TAPS, 64, COLS), jnp.bfloat16),
        pltpu.VMEM((TAP_ROWS, POINTS), jnp.float32),
        pltpu.VMEM((TAP_ROWS, 64), jnp.float32),
        pltpu.VMEM(chunk, jnp.bfloat16),
        pltpu.VMEM(chunk, jnp.bfloat16),
        pltpu.VMEM(chunk, jnp.bfloat16),
        pltpu.VMEM(chunk, jnp.bfloat16),
        pltpu.VMEM((8, LANES), jnp.float32),
        pltpu.VMEM((MEMBERS, 8, LANES), jnp.float32),
        pltpu.VMEM((TAP_ROWS, POINTS), jnp.bfloat16),
        pltpu.VMEM((TAP_ROWS, 64), jnp.bfloat16),
        pltpu.VMEM((2, ROWS, LANES), jnp.bfloat16),
        pltpu.VMEM((2, ROWS, LANES), jnp.float32),
        pltpu.VMEM((ROWS, LANES), jnp.float32),
        pltpu.VMEM((ROWS, LANES), jnp.bfloat16),
        pltpu.VMEM((TAPS, 8, 512), jnp.float32),
        pltpu.SemaphoreType.DMA((5,)),
        pltpu.SemaphoreType.DMA((5,)),
    ] + reduce_scratch()


def finish_kernel(
    summed, grad_in, owned_in, weight_grad, grad_out, owned_out, bias_grad,
    main, wide, grad_here, owned_here, in_sems, out_sems, pass_sems,
):
    factor = 1.0 / math.sqrt(MEMBERS * LAT * LON_DEV * GROUPS)
    first = TAPS * TAP_ROWS
    tail = (TAPS - 1, slice(first, ROWS))
    loads = [pltpu.make_async_copy(summed.at[tail], main.at[tail], in_sems.at[TAPS])]
    for a in range(TAPS):
        rows = (slice(None), slice(a * TAP_ROWS, (a + 1) * TAP_ROWS))
        loads.append(pltpu.make_async_copy(summed.at[rows], main.at[rows], in_sems.at[a]))
    taken = [
        pltpu.make_async_copy(grad_in, grad_here, pass_sems.at[0]),
        pltpu.make_async_copy(owned_in, owned_here, pass_sems.at[1]),
    ]
    for copy in loads + taken:
        copy.start()
    loads[0].wait()
    more = main[TAPS - 1, first:ROWS, :].astype(jnp.float32) * factor
    bias = jnp.concatenate([more[4 * TAPS + q : 4 * TAPS + q + 1, :] for q in range(4)], axis=1)
    bias_grad[...] = bias[:, 2 * CHAN : 2 * CHAN + COUT]
    stores = []
    for a in range(TAPS):
        last = jnp.concatenate([more[4 * a + q : 4 * a + q + 1, :] for q in range(4)], axis=1)
        last = jnp.transpose(jnp.broadcast_to(last, (8, 512)))
        loads[a + 1].wait()
        for b in range(TAPS):
            base, n = a * TAP_ROWS + b * CHAN, a * TAPS + b
            for block in range(TAPS):
                part = main[block, base : base + CHAN, :].astype(jnp.float32) * factor
                wide[n, :, block * LANES : (block + 1) * LANES] = part[:COUT]
            wide[n, :, WIDE:CIN] = last[b * CHAN : b * CHAN + COUT, 0:1]
            stores.append(pltpu.make_async_copy(wide.at[n], weight_grad.at[n], out_sems.at[n]))
            stores[-1].start()
    given = [
        pltpu.make_async_copy(grad_here, grad_out, pass_sems.at[2]),
        pltpu.make_async_copy(owned_here, owned_out, pass_sems.at[3]),
    ]
    for source, target in zip(taken, given):
        source.wait()
        target.start()
    for copy in stores + given:
        copy.wait()


def body(fields, weight, out_bias, observed, widths, owner_start):
    vmem = pl.BlockSpec(memory_space=pltpu.VMEM)
    hbm = pl.BlockSpec(memory_space=pl.ANY)
    summed, grad, owned = pl.pallas_call(
        whole_kernel,
        out_shape=[
            jax.ShapeDtypeStruct((TAPS, ROWS, LANES), jnp.bfloat16),
            jax.ShapeDtypeStruct((LON_DEV, LAT, COUT), jnp.bfloat16),
            jax.ShapeDtypeStruct((1, CAP * LON_DEV), jnp.float32),
        ],
        in_specs=[hbm] * 5 + [vmem] * 2 + [pl.BlockSpec(memory_space=pltpu.SMEM)],
        out_specs=[vmem] * 3,
        scratch_shapes=kernel_scratch(),
        compiler_params=pltpu.CompilerParams(
            collective_id=1, has_side_effects=True, vmem_limit_bytes=56 * 1024 * 1024
        ),
        cost_estimate=pl.CostEstimate(flops=6 << 30, bytes_accessed=16 << 20, transcendentals=1 << 20),
    )(
        jnp.transpose(fields[0], (1, 2, 0)), weight, jnp.transpose(observed, (2, 1, 0)),
        jnp.asarray(margin_places(), jnp.bfloat16), jnp.asarray(edge_picks(), jnp.bfloat16),
        out_bias.reshape(1, COUT), widths.reshape(1, COUT), owner_start[0],
    )
    weight_grad, grad, owned, bias_grad = pl.pallas_call(
        finish_kernel,
        out_shape=[
            jax.ShapeDtypeStruct((TAPS * TAPS, COUT, CIN), jnp.float32),
            jax.ShapeDtypeStruct((LON_DEV, LAT, COUT), jnp.bfloat16),
            jax.ShapeDtypeStruct((1, CAP * LON_DEV), jnp.float32),
            jax.ShapeDtypeStruct((1, COUT), jnp.float32),
        ],
        in_specs=[hbm] * 3,
        out_specs=[hbm] * 3 + [vmem],
        scratch_shapes=[
            pltpu.VMEM((TAPS, ROWS, LANES), jnp.bfloat16),
            pltpu.VMEM((TAPS * TAPS, COUT, CIN), jnp.float32),
            pltpu.VMEM((LON_DEV, LAT, COUT), jnp.bfloat16),
            pltpu.VMEM((1, CAP * LON_DEV), jnp.float32),
            pltpu.SemaphoreType.DMA((TAPS + 1,)),
            pltpu.SemaphoreType.DMA((TAPS * TAPS,)),
            pltpu.SemaphoreType.DMA((4,)),
        ],
        compiler_params=pltpu.CompilerParams(vmem_limit_bytes=58 * 1024 * 1024),
    )(summed, grad, owned)
    weight_grad = weight_grad.reshape(TAPS, TAPS, COUT, CIN)
    bias_grad = bias_grad.reshape(COUT)
    out_grad = jnp.transpose(grad, (2, 1, 0))[None]
    owned_score = owned.reshape(1, 1, CAP * LON_DEV)
    return (out_grad, owned_score, weight_grad, bias_grad)


def solution(mesh):
    in_specs = (P("member", None, None, "lon"), P(), P(), P(None, None, "lon"), P(), P("lon", None))
    out_specs = (P("member", None, None, "lon"), P("lon", "member", None), P(), P())
    return jax.shard_map(body, mesh=mesh, in_specs=in_specs, out_specs=out_specs, check_vma=False)
```
